32 devices in a mesh: dp: 8 (over z, y), head: 4 (over x, core).
Axes of the slice: x: 2, y: 2, z: 4, core: 2. Of those that a mesh axis runs over, the one named last changes fastest.
Arguments:
- segment: bfloat16 [8, 512, 1024], P('dp'), may hold values from -6 to 6
- memory: bfloat16 [8, 512, 1024], P('dp'), may hold values from -6 to 6
- compressed: bfloat16 [8, 512, 1024], P('dp'), may hold values from -6 to 6
- mem_fill: int32 [8], P('dp'), may hold values from 0 to 512, as said below
- comp_fill: int32 [8], P('dp'), may hold values from 0 to 512, as said below
- gain_attn: float32 [1024], replicated, may hold values from 0.1 to 1.9
- w_qkv: bfloat16 [1024, 3072], P(None, 'head'), may hold values from -0.1875 to 0.1875
- content_bias: float32 [128, 8], P(None, 'head'), may hold values from -3 to 3
- position_bias: float32 [128, 8], P(None, 'head'), may hold values from -3 to 3
- w_rel: bfloat16 [1024, 1024], P(None, 'head'), may hold values from -0.1875 to 0.1875
- w_out: bfloat16 [1024, 1024], P(None, 'head'), may hold values from -1 to 1
- gain_ffn: float32 [1024], replicated, may hold values from 0.1 to 1.9
- w_up: bfloat16 [1024, 4096], P(None, 'head'), may hold values from -0.1875 to 0.1875
- w_down: bfloat16 [1024, 4096], P(None, 'head'), may hold values from -0.09375 to 0.09375
- w_comp: bfloat16 [3072, 1024], P(None, 'head'), may hold values from -0.109375 to 0.109375
- out_cotangent: bfloat16 [8, 512, 1024], P('dp'), may hold values from -6 to 6
- comp_cotangent: bfloat16 [8, 170, 1024], P('dp', None, 'head'), may hold values from -6 to 6
Outputs:
- layer_output: bfloat16 [8, 512, 1024], P('dp')
- new_compressed: bfloat16 [8, 170, 1024], P('dp', None, 'head')
- input_grad: float32 [8, 512, 1024], P('dp')
- gain_attn_grad: float32 [1024], P('dp')
- qkv_grad: float32 [1024, 3072], P('dp', 'head')
- content_bias_grad: float32 [128, 8], P('dp', 'head')
- position_bias_grad: float32 [128, 8], P('dp', 'head')
- rel_grad: float32 [1024, 1024], P('dp', 'head')
- out_proj_grad: float32 [1024, 1024], P('dp', 'head')
- gain_ffn_grad: float32 [1024], P('dp')
- up_grad: float32 [1024, 4096], P('dp', 'head')
- down_grad: float32 [1024, 4096], P('dp', 'head')
- comp_grad: float32 [3072, 1024], P('dp', 'head')
The draws below stay inside these ranges and needn't reach their ends.
Inputs may be any that keep to these rules, and one draw needn't show every extreme that they name: `mem_fill`: the empty memory slots of a stream are its oldest ones; streams whose memory is empty are common. `comp_fill`: the empty compressed slots are the oldest ones; a stream has compressed rows only where its memory is full.
All inputs are finite; a program needn't handle non-finite values.
Results may differ from the reference program's by a relative error of at most 0.017.
Values sent between devices are 32-bit elements; how exact they have to be, the bound alone decides.
A program may use at most 192 MiB of HBM per device.

```python
import jax
import jax.numpy as jnp
from jax import lax

D = 1024
H = 8
DH = 128
FF = 4096
SEG = 512
MEM = 512
CMEM = 512
CR = 170
KEYS = 1536
STREAMS = 8


def stream_history(key):
    seen = jax.random.randint(key, (STREAMS,), 0, MEM + 3 * CMEM + 1)
    fresh = jax.random.randint(jax.random.fold_in(key, 7), (STREAMS,), 0, 4) == 0
    seen = jnp.where(fresh, 0, seen)
    positions = jnp.arange(STREAMS)
    seen = jnp.where(positions == 0, 0, seen)
    return jnp.where(positions == 1, MEM + 3 * CMEM, seen)


def draw_mem_fill(key, part):
    seen = stream_history(key)
    return jnp.minimum(seen, MEM).astype(jnp.int32)


def draw_comp_fill(key, part):
    seen = stream_history(key)
    return jnp.minimum(jnp.maximum(seen - MEM, 0) // 3, CMEM).astype(jnp.int32)


def block_levels(stream_key, extent, pieces, low, high):
    loudness = 1.0
    for position, parts in pieces:
        steps = jax.random.uniform(jax.random.fold_in(jax.random.fold_in(stream_key, 6), position), (parts,), jnp.float32, low / len(pieces), high / len(pieces))
        loudness = loudness * jnp.repeat(jnp.exp(steps), extent[position] // parts).reshape((-1,) + (1,) * (len(extent) - 1 - position))
    return loudness


def bell_draw(stream_key, extent, scale, reach, pieces=(), kind=jnp.bfloat16):
    values = scale * jax.random.normal(stream_key, extent, jnp.float32)
    if pieces:
        values = values * block_levels(stream_key, extent, pieces, -0.22, 0.18)
    return jnp.clip(values, -reach, reach).astype(kind)


def setup_inputs(seed: int = 0) -> dict:
    arg_keys = jax.random.split(jax.random.key(seed), 18)
    segment = bell_draw(arg_keys[0], (STREAMS, SEG, D), 1.0, 6.0, ((0, 8),))
    memory = bell_draw(arg_keys[1], (STREAMS, MEM, D), 1.0, 6.0, ((0, 8),))
    compressed = bell_draw(arg_keys[2], (STREAMS, CMEM, D), 1.0, 6.0, ((0, 8),))
    mem_fill = draw_mem_fill(jax.random.fold_in(arg_keys[17], 71), 0)
    comp_fill = draw_comp_fill(jax.random.fold_in(arg_keys[17], 71), 0)
    gain_attn = jnp.clip(1.0 + 0.18 * jax.random.normal(arg_keys[5], (D,), jnp.float32), 0.1, 1.9)
    w_qkv = bell_draw(arg_keys[6], (D, 3 * H * DH), D ** -0.5, 0.1875, ((1, 4),))
    content_bias = bell_draw(arg_keys[7], (DH, H), 0.5, 3.0, ((1, 4),), jnp.float32)
    position_bias = bell_draw(arg_keys[8], (DH, H), 0.5, 3.0, ((1, 4),), jnp.float32)
    w_rel = bell_draw(arg_keys[9], (D, H * DH), D ** -0.5, 0.1875, ((1, 4),))
    w_out = bell_draw(arg_keys[10], (D, H * DH), (H * DH // 32) ** -0.5, 1.0, ((1, 4),))
    gain_ffn = jnp.clip(1.0 + 0.18 * jax.random.normal(arg_keys[11], (D,), jnp.float32), 0.1, 1.9)
    w_up = bell_draw(arg_keys[12], (D, FF), D ** -0.5, 0.1875, ((1, 4),))
    w_down = bell_draw(arg_keys[13], (D, FF), FF ** -0.5, 0.09375, ((1, 4),))
    w_comp = bell_draw(arg_keys[14], (3 * D, D), (3 * D) ** -0.5, 0.109375, ((1, 4),))
    out_cotangent = bell_draw(arg_keys[15], (STREAMS, SEG, D), 1.0, 6.0, ((0, 8),))
    comp_cotangent = bell_draw(arg_keys[16], (STREAMS, CR, D), 1.0, 6.0, ((0, 8), (2, 4)))
    return dict(segment=segment, memory=memory, compressed=compressed, mem_fill=mem_fill, comp_fill=comp_fill, gain_attn=gain_attn, w_qkv=w_qkv, content_bias=content_bias, position_bias=position_bias, w_rel=w_rel, w_out=w_out, gain_ffn=gain_ffn, w_up=w_up, w_down=w_down, w_comp=w_comp, out_cotangent=out_cotangent, comp_cotangent=comp_cotangent)


@jax.custom_vjp
def low(v):
    return lax.optimization_barrier(v.astype(jnp.bfloat16)).astype(jnp.float32)

@jax.custom_vjp
def low_back(v):
    return v

def low_keep(v):
    return (low(v), None)

def low_pass(kept, grad):
    return (grad,)

def back_keep(v):
    return (v, None)

def back_low(kept, grad):
    return (low(grad),)
low.defvjp(low_keep, low_pass)
low_back.defvjp(back_keep, back_low)
epsilon = 1e-05
masked_value = -1e+30
highest = lax.Precision.HIGHEST

def norm_rows(rows, gain):
    average = lax.optimization_barrier(jnp.mean(rows, axis=-1, keepdims=True))
    centered = rows - average
    spread = lax.optimization_barrier(jnp.mean(centered * centered, axis=-1, keepdims=True))
    return centered * lax.rsqrt(spread + epsilon) * gain

def angle_tables(model_width, row_count):
    half_width = model_width // 2
    frequency = jnp.exp(-jnp.log(10000.0) * jnp.arange(half_width, dtype=jnp.float32) / half_width)
    angles = jnp.arange(row_count, dtype=jnp.float32)[:, None] * frequency[None, :]
    return (jnp.sin(angles), jnp.cos(angles))

def rotate_rows(values, sine_rows, cosine_rows):
    half_width = values.shape[-1] // 2
    sine_rows = sine_rows[:, None, :]
    cosine_rows = cosine_rows[:, None, :]
    leading = values[..., :half_width]
    trailing = values[..., half_width:]
    return jnp.concatenate([leading * sine_rows + trailing * cosine_rows, trailing * sine_rows - leading * cosine_rows], axis=-1)

def key_masks(mem_count, comp_count):
    key_index = jnp.arange(KEYS)[None, :]
    query_index = jnp.arange(SEG)[:, None]
    in_comp = (key_index < CMEM) & (key_index >= CMEM - comp_count)
    in_memory = (key_index >= CMEM) & (key_index < CMEM + MEM) & (key_index >= CMEM + MEM - mem_count)
    in_segment = (key_index >= CMEM + MEM) & (key_index - CMEM - MEM <= query_index)
    memory_valid = (jnp.arange(MEM) >= MEM - mem_count).astype(jnp.float32)
    return (in_comp | in_memory | in_segment, memory_valid)

def layer_forward(params, segment_rows, memory_rows, compressed_rows, key_valid, memory_valid):
    gain_attn, w_qkv, content_bias, position_bias, w_rel, w_out, gain_ffn, w_up, w_down, w_comp = params
    all_rows = jnp.concatenate([compressed_rows, memory_rows, segment_rows], axis=0)
    normed = low(norm_rows(all_rows, gain_attn))
    projected = low_back(jnp.dot(normed, w_qkv, precision=highest)).reshape(KEYS, H, 3, DH)
    queries = projected[CMEM + MEM:, :, 0, :]
    key_rows = low(projected[:, :, 1, :])
    value_rows = low(projected[:, :, 2, :])
    content_q = low(queries + content_bias.T[None])
    pos_in = low(queries + position_bias.T[None])
    rel_proj = low_back(jnp.einsum('shc,dhc->shd', pos_in, w_rel.reshape(D, H, DH), precision=highest))
    sine_table, cosine_table = angle_tables(D, KEYS)
    rotated = low(rotate_rows(rel_proj, sine_table[KEYS - SEG:], cosine_table[KEYS - SEG:]))
    key_features = low(jnp.concatenate([cosine_table, sine_table], axis=-1))
    content = jnp.einsum('shc,khc->hsk', content_q, key_rows, precision=highest)
    place = jnp.einsum('shd,kd->hsk', rotated, key_features, precision=highest)
    scores = low_back((content + place) * DH ** (-0.5))
    masked = jnp.where(key_valid[None], scores, masked_value)
    row_top = lax.optimization_barrier(jnp.max(masked, axis=-1, keepdims=True))
    raised = jnp.exp(masked - row_top)
    attn_probs = low(raised / lax.optimization_barrier(jnp.sum(raised, axis=-1, keepdims=True)))
    mixed = low(low_back(jnp.einsum('hsk,khc->shc', attn_probs, value_rows, precision=highest))).reshape(SEG, H * DH)
    attention = low_back(jnp.dot(mixed, w_out.T, precision=highest))
    residual = segment_rows + attention
    normed_ffn = low(norm_rows(residual, gain_ffn))
    hidden = low_back(jnp.dot(normed_ffn, w_up, precision=highest))
    activated = low(jax.nn.gelu(hidden))
    ffn_out = low_back(jnp.dot(activated, w_down.T, precision=highest))
    windows = (memory_rows * memory_valid[:, None])[:3 * CR].reshape(CR, 3 * D)
    new_rows = jnp.dot(windows, w_comp, precision=highest)
    return (residual + ffn_out, new_rows)

def reference(segment, memory, compressed, mem_fill, comp_fill, gain_attn, w_qkv, content_bias, position_bias, w_rel, w_out, gain_ffn, w_up, w_down, w_comp, out_cotangent, comp_cotangent):
    params = tuple((tensor.astype(jnp.float32) for tensor in (gain_attn, w_qkv, content_bias, position_bias, w_rel, w_out, gain_ffn, w_up, w_down, w_comp)))
    initial = jax.tree.map(jnp.zeros_like, params)

    def stream_step(totals, stream):
        seg_rows, mem_rows, comp_rows, mem_count, comp_count, out_grad, new_grad = stream
        key_valid, memory_valid = key_masks(mem_count, comp_count)

        def forward(weights, inputs):
            return layer_forward(weights, inputs, mem_rows.astype(jnp.float32), comp_rows.astype(jnp.float32), key_valid, memory_valid)
        outputs, pullback = jax.vjp(forward, params, seg_rows.astype(jnp.float32))
        weight_grads, seg_grad = pullback((out_grad.astype(jnp.float32), new_grad.astype(jnp.float32)))
        totals = jax.tree.map(jnp.add, totals, weight_grads)
        return (totals, (outputs[0].astype(jnp.bfloat16), outputs[1].astype(jnp.bfloat16), seg_grad))
    totals, stacked = lax.scan(stream_step, initial, (segment, memory, compressed, mem_fill, comp_fill, out_cotangent, comp_cotangent))
    return (stacked[0], stacked[1], stacked[2], totals[0], totals[1], totals[2], totals[3], totals[4], totals[5], totals[6], totals[7], totals[8], totals[9])
```

```python
import functools

import jax
import jax.numpy as jnp
import numpy as np
from jax import lax
from jax.experimental import pallas as pl
from jax.experimental.pallas import tpu as pltpu
from jax.sharding import PartitionSpec as P

MESH = pl.DeviceIdType.MESH
BF = jnp.bfloat16
F32 = jnp.float32
EPS = 1e-05
MASKED = -1e30
NN = (((1,), (0,)), ((), ()))
NT = (((1,), (1,)), ((), ()))
TN = (((0,), (0,)), ((), ()))
FIRST_RING = 8
LATER_RING = 4


def dot(a, b, dims=NN):
    return lax.dot_general(a, b, dims, preferred_element_type=F32)


def row_loop(total, chunk, body):
    def step(index, carry):
        body(pl.multiple_of(index * chunk, chunk))
        return carry

    lax.fori_loop(0, total // chunk, step, 0)


def tables(width, prior, keys):
    half = width // 2
    frequency = np.exp(-np.log(10000.0) * np.arange(half) / half)
    angles = np.arange(keys)[:, None] * frequency[None, :]
    sine, cosine = np.sin(angles), np.cos(angles)
    features = np.concatenate([cosine, sine], axis=1).astype(np.float32)
    return features, sine[prior:].astype(np.float32), cosine[prior:].astype(np.float32)


def moments(rows):
    average = jnp.mean(rows, axis=-1, keepdims=True)
    centered = rows - average
    spread = jnp.mean(centered * centered, axis=-1, keepdims=True)
    return centered, lax.rsqrt(spread + EPS)


def norm_back(scaled, xhat, inverse):
    along = jnp.mean(scaled * xhat, axis=-1, keepdims=True)
    return (scaled - jnp.mean(scaled, axis=-1, keepdims=True) - xhat * along) * inverse


def gelu_pair(x):
    c = 0.7978845608028654
    square = x * x
    t = jnp.tanh(c * x * (1.0 + 0.044715 * square))
    half = 0.5 * (1.0 + t)
    slope = half + (0.5 * c) * x * (1.0 - t * t) * (1.0 + 0.134145 * square)
    return x * half, slope


def kernel(
    n,
    mem_fill,
    comp_fill,
    gain_attn,
    gain_ffn,
    content_bias,
    position_bias,
    comp_cot,
    segment,
    memory,
    compressed,
    w_qkv,
    w_rel,
    w_out,
    w_up,
    w_down,
    w_comp,
    cotangent,
    features,
    sine,
    cosine,
    layer_out,
    new_rows,
    input_grad,
    gain_attn_out,
    qkv_out,
    cbias_out,
    pbias_out,
    rel_out,
    outp_out,
    gain_ffn_out,
    up_out,
    down_out,
    comp_out,
    seg_v,
    mem_v,
    cmp_v,
    cot_v,
    wqkv,
    wrel,
    wout,
    wup,
    wdn,
    kf,
    qsin,
    qcos,
    vals,
    rot,
    pin,
    normed,
    probs,
    mix,
    mgrad,
    dseg,
    resid,
    rgrad,
    ccot,
    maskrow,
    grads,
    part,
    core_in,
    x_in,
    total,
    small,
    small_in,
    tiny,
    tiny_in,
    first_in,
    later_in,
    in_sem,
    out_sem,
    first_send,
    first_recv,
    first_free,
    later_send,
    later_recv,
    later_free,
    core_send,
    core_recv,
    core_free,
    x_send,
    x_recv,
    x_free,
    back_send,
    back_recv,
    back_free,
    small_send,
    small_recv,
    tiny_send,
    tiny_recv,
):
    steps = n.bit_length() - 1
    width = seg_v.shape[1]
    rows = seg_v.shape[0]
    prior = 2 * rows
    head_size = content_bias.shape[0]
    scale = head_size ** (-0.5)
    piece = width // n
    new_count = comp_cot.shape[0]
    pad_count = ccot.shape[0]

    dp = lax.axis_index("dp")
    head = lax.axis_index("head")
    core = lax.rem(head, 2)
    other = 1 - core
    core_peer = (dp, head + 1 - 2 * core)
    x_peer = (dp, lax.rem(head + 2, 4))
    bits = [lax.rem(dp // (1 << s), 2) for s in range(steps)]
    dp_peers = [(dp + (1 - 2 * bits[s]) * (1 << s), head) for s in range(steps)]

    loads = {}

    def load(name, index, source, target):
        copy = pltpu.make_async_copy(source, target, in_sem.at[index])
        copy.start()
        loads[name] = copy

    def loaded(name):
        loads.pop(name).wait()

    load("memory", 0, memory, mem_v)
    for tap in range(3):
        load(
            f"w_comp{tap}",
            1 + tap,
            w_comp.at[pl.ds(tap * width, width)],
            wup.at[:, pl.ds(256 * tap, 256)],
        )
    load("compressed", 4, compressed, cmp_v)
    load("segment", 5, segment, seg_v)
    load("w_qkv", 6, w_qkv, wqkv)
    load("w_rel", 7, w_rel, wrel)
    load("sine", 8, sine, qsin)
    load("cosine", 9, cosine, qcos)
    load("features", 10, features, kf.at[:, pl.ds(head_size, width)])
    load("w_out", 11, w_out, wout)
    load("cotangent", 12, cotangent, cot_v)
    load("w_down", 13, w_down, wdn)

    barrier = pltpu.get_barrier_semaphore()
    greeted = [core_peer, x_peer] + dp_peers
    for peer in greeted:
        pl.semaphore_signal(barrier, inc=1, device_id=peer, device_id_type=MESH)
    pl.semaphore_wait(barrier, len(greeted))

    def remote(source, target, send, recv, peer):
        copy = pltpu.make_async_remote_copy(
            src_ref=source,
            dst_ref=target,
            send_sem=send,
            recv_sem=recv,
            device_id=peer,
            device_id_type=MESH,
        )
        copy.start()
        return copy

    low_first = list(range(steps))
    low_last = low_first[1:] + [0]
    units = []
    for t in range(3):
        units.append((t, low_first, comp_out.at[pl.ds(t * piece, piece), :]))
    for t in range(4):
        units.append((3 + t, low_first, down_out.at[:, pl.ds(256 * t, 256)]))
    for t in range(4):
        units.append((7 + t, low_first, up_out.at[:, pl.ds(256 * t, 256)]))
    for t in range(3):
        units.append((t, low_first, qkv_out.at[:, pl.ds(256 * t, 256)]))
    units.append((11, low_last, outp_out.at[...]))
    units.append((12, low_last, rel_out.at[...]))
    COMP, DOWN, UP, QKV, OUT, REL = 0, 3, 7, 11, 14, 15
    outs = {}
    sends = {}
    done = set()

    def place(order, j):
        found = 0
        for bit in order:
            found = 2 * found + ((j >> bit) & 1)
        return found

    def store_rows(unit, j, value, lanes=slice(None)):
        at, order, _ = units[unit]
        row = place(order, j) * piece
        grads[2 * at + row // 512, pl.ds(row % 512, piece), lanes] = value

    def store_unit(unit, value, lanes=slice(None)):
        for j in range(n):
            store_rows(unit, j, value[piece * j : piece * (j + 1)], lanes)

    def region(unit, step, mine):
        at, order, _ = units[unit]
        first = bits[order[0]]
        if step == 0:
            return 2 * at + (first if mine else 1 - first), 0, 512
        start = 0
        for s in range(1, step):
            start = start + bits[order[s]] * (width >> (s + 1))
        length = width >> (step + 1)
        mybit = bits[order[step]]
        start = start + (mybit if mine else 1 - mybit) * length
        return 2 * at + first, pl.multiple_of(start, length), length

    def slot_refs(unit, step):
        if step == 0:
            slot = unit % FIRST_RING
            return first_in.at[slot], first_send.at[slot], first_recv.at[slot]
        slot = unit % LATER_RING
        index = (step - 1) * LATER_RING + slot
        length = width >> (step + 1)
        begin = 512 - (512 >> (step - 1))
        return (
            later_in.at[slot, pl.ds(begin, length), :],
            later_send.at[index],
            later_recv.at[index],
        )

    def slot_free(unit, step):
        kind = int(units[unit][1] is low_last)
        if step == 0:
            return first_free.at[kind, unit % FIRST_RING]
        return later_free.at[kind, (step - 1) * LATER_RING + unit % LATER_RING]

    def ring(step):
        return FIRST_RING if step == 0 else LATER_RING

    def unit_send(unit, step):
        target, send, recv = slot_refs(unit, step)
        if unit >= ring(step):
            assert (unit - ring(step), "done") in done
            pl.semaphore_wait(slot_free(unit, step), 1)
        at, start, length = region(unit, step, False)
        peer = dp_peers[units[unit][1][step]]
        sends[unit, step] = remote(grads.at[at, pl.ds(start, length), :], target, send, recv, peer)

    def unit_step(unit, step):
        if unit < 0 or unit >= len(units) or (unit, step) in done:
            return
        done.add((unit, step))
        target = slot_refs(unit, step)[0]
        sends[unit, step].wait_recv()
        at, start, length = region(unit, step, True)
        chunk = min(64, length)

        def add(offset):
            here = pl.ds(pl.multiple_of(start + offset, chunk), chunk)
            grads[at, here, :] = grads[at, here, :] + target[pl.ds(offset, chunk), :]

        row_loop(length, chunk, add)
        later = unit + ring(step)
        if later < len(units):
            peer = dp_peers[units[later][1][step]]
            pl.semaphore_signal(
                slot_free(later, step), inc=1, device_id=peer, device_id_type=MESH
            )
        if step + 1 < steps:
            unit_send(unit, step + 1)
        else:
            for s in range(steps):
                sends.pop((unit, s)).wait_send()
            copy = pltpu.make_async_copy(
                grads.at[at, pl.ds(start, length), :], units[unit][2], out_sem.at[unit]
            )
            copy.start()
            outs[unit] = copy
            done.add((unit, "done"))

    lag = 1 if steps <= LATER_RING - 1 else 0

    def tick(unit):
        for step in range(steps):
            unit_step(unit - step * lag, step)

    def drain(first, last):
        for unit in range(last, last + steps):
            for step in range(1, steps):
                if first <= unit + 1 - step <= last:
                    unit_step(unit + 1 - step, step)

    moves = {}
    subs = 4
    sub_rows = rows // subs

    def span(sub):
        return pl.ds(sub * sub_rows, sub_rows)

    def sum_source(k):
        return (grads, 22) if k == 2 else (part, 0)

    def sum_start(k, sub):
        if k >= 1 and sub == 0:
            pl.semaphore_wait(core_free, 1)
        ref, base = sum_source(k)
        moves[k, "core", sub] = remote(
            ref.at[pl.ds(base + 2 * other, 2), span(sub), :],
            core_in.at[:, span(sub), :],
            core_send.at[sub],
            core_recv.at[sub],
            core_peer,
        )

    def sum_across(k, sub):
        ref, base = sum_source(k)
        moves[k, "core", sub].wait()
        for i in range(2):
            at = base + 2 * core + i
            ref[at, span(sub), :] = ref[at, span(sub), :] + core_in[i, span(sub), :]
        if sub == subs - 1 and k < 3:
            pl.semaphore_signal(core_free, inc=1, device_id=core_peer, device_id_type=MESH)
        if k >= 2 and sub == 0:
            pl.semaphore_wait(x_free.at[k % 2], 1)
        moves[k, "x", sub] = remote(
            ref.at[pl.ds(base + 2 * core, 2), span(sub), :],
            x_in.at[k % 2, :, span(sub), :],
            x_send.at[k % 2, sub],
            x_recv.at[k % 2, sub],
            x_peer,
        )

    def sum_back(k, sub):
        ref, base = sum_source(k)
        moves[k, "x", sub].wait_recv()
        for i in range(2):
            total[2 * core + i, span(sub), :] = (
                ref[base + 2 * core + i, span(sub), :] + x_in[k % 2, i, span(sub), :]
            )
        if sub == subs - 1 and k < 2:
            pl.semaphore_signal(x_free.at[k % 2], inc=1, device_id=x_peer, device_id_type=MESH)
        if k >= 1 and sub == 0:
            pl.semaphore_wait(back_free, 1)
        here = total.at[pl.ds(2 * core, 2), span(sub), :]
        moves[k, "back", sub] = remote(here, here, back_send.at[sub], back_recv.at[sub], core_peer)

    def sum_done(k, sub):
        moves[k, "back", sub].wait_recv()

    def sum_used(k):
        for sub in range(subs):
            moves[k, "x", sub].wait_send()
            moves[k, "back", sub].wait_send()
        if k < 3:
            pl.semaphore_signal(back_free, inc=1, device_id=core_peer, device_id_type=MESH)

    def total_rows(here):
        return jnp.concatenate([total[t, here, :] for t in range(4)], axis=1)

    ccot[...] = jnp.zeros_like(ccot)
    ccot[0:new_count, :] = comp_cot[...]
    loaded("memory")
    fill = mem_fill[0]
    compressed_rows = jnp.zeros((pad_count, 256), F32)
    row_at = lax.broadcasted_iota(jnp.int32, (pad_count, rows), 0)
    slot_at = lax.broadcasted_iota(jnp.int32, (pad_count, rows), 1)
    for tap in range(3):
        pick = (slot_at == 3 * row_at + tap) & (slot_at >= rows - fill) & (row_at < new_count)
        window = dot(jnp.where(pick, 1.0, 0.0).astype(BF), mem_v[...]).astype(BF)
        loaded(f"w_comp{tap}")
        compressed_rows = compressed_rows + dot(window, wup[:, pl.ds(256 * tap, 256)])
        tap_grad = dot(window, ccot[...], TN)
        for i in range(n):
            j, t = divmod(n * tap + i, 3)
            store_rows(COMP + t, j, tap_grad[piece * i : piece * (i + 1)])
    new_rows[...] = compressed_rows[0:new_count].astype(BF)
    for t in range(3):
        unit_send(COMP + t, 0)
    load("w_up", 1, w_up, wup)

    lane = lax.broadcasted_iota(jnp.int32, (1, rows), 1)
    maskrow[0:1, 0:rows] = jnp.where(lane >= rows - comp_fill[0], 0.0, MASKED)
    maskrow[0:1, rows:prior] = jnp.where(lane >= rows - fill, 0.0, MASKED)

    def norm_into(source, base):
        def body(offset):
            centered, inverse = moments(source[pl.ds(offset, 32), :].astype(F32))
            normed[pl.ds(pl.multiple_of(base + offset, 32), 32), :] = (
                centered * inverse * gain_attn[...]
            ).astype(BF)

        row_loop(rows, 32, body)

    loaded("compressed")
    norm_into(cmp_v, 0)
    norm_into(mem_v, rows)
    loaded("segment")
    norm_into(seg_v, prior)

    def bias_row(ref, h):
        line = lax.broadcasted_iota(jnp.int32, (head_size, head_size), 0)
        column = lax.broadcasted_iota(jnp.int32, (head_size, head_size), 1)
        return jnp.sum(jnp.where(line == column, ref[:, h : h + 1], 0.0), axis=0, keepdims=True)

    loaded("w_qkv")
    loaded("features")
    dh = head_size
    key_lane = (0, dh + width)
    pair_lane = (0, dh)
    place_lane = (dh, 0)
    query_lane = (0, width)
    for block in range(2):
        here = pl.ds(block * rows, rows)
        for h in range(2):
            both = dot(normed[here, :], wqkv[:, 3 * dh * h + dh : 3 * dh * (h + 1)])
            kf[here, key_lane[h] : key_lane[h] + dh] = both[:, 0:dh].astype(BF)
            vals[here, dh * h : dh * (h + 1)] = both[:, dh:].astype(BF)
    here = pl.ds(prior, rows)
    queries = [None, None]
    three = [dot(normed[here, :], wqkv[:, 256 * t : 256 * (t + 1)]) for t in range(3)]
    queries[0] = three[0][:, 0:dh]
    kf[here, key_lane[0] : key_lane[0] + dh] = three[0][:, dh:].astype(BF)
    vals[here, 0:dh] = three[1][:, 0:dh].astype(BF)
    queries[1] = three[1][:, dh:]
    kf[here, key_lane[1] : key_lane[1] + dh] = three[2][:, 0:dh].astype(BF)
    vals[here, dh : 2 * dh] = three[2][:, dh:].astype(BF)
    for h in range(2):
        rot[h, :, query_lane[h] : query_lane[h] + dh] = (
            queries[h] + bias_row(content_bias, h)
        ).astype(BF)
        pin[:, dh * h : dh * (h + 1)] = (queries[h] + bias_row(position_bias, h)).astype(BF)

    loaded("w_rel")
    loaded("sine")
    loaded("cosine")
    half = width // 2
    for h in range(2):
        for j in range(2):
            cols = slice(256 * j, 256 * (j + 1))
            weights = wrel[256 * j : 256 * (j + 1), dh * h : dh * (h + 1)]
            upper = dot(pin[:, dh * h : dh * (h + 1)], weights, NT)
            weights = wrel[half + 256 * j : half + 256 * (j + 1), dh * h : dh * (h + 1)]
            lower = dot(pin[:, dh * h : dh * (h + 1)], weights, NT)
            begin = place_lane[h] + 256 * j
            rot[h, :, begin : begin + 256] = (
                upper * qsin[:, cols] + lower * qcos[:, cols]
            ).astype(BF)
            rot[h, :, begin + half : begin + half + 256] = (
                lower * qsin[:, cols] - upper * qcos[:, cols]
            ).astype(BF)

    block_rows = rows // 2
    probs[:, 0:block_rows, prior + 256 : prior + 512] = jnp.zeros((2, block_rows, 256), BF)
    for block in range(2):
        here = pl.ds(block * block_rows, block_rows)
        tiles = 5 + block
        for h in range(2):

            def score_tile(t, carry, h=h, here=here):
                keys = pl.ds(pl.multiple_of(t * 256, 256), 256)
                grads[6 + t, 0:block_rows, :] = dot(
                    rot[h, here, :], kf[keys, pair_lane[h] : pair_lane[h] + dh + width], NT
                )
                return carry

            lax.fori_loop(0, tiles, score_tile, 0)

            def soften(offset, h=h, block=block, tiles=tiles):
                inner = pl.ds(offset, 16)
                pieces = []
                for t in range(tiles):
                    s = grads[6 + t, inner, :] * scale
                    if t < 4:
                        s = s + maskrow[0:1, 256 * t : 256 * (t + 1)]
                    if t == tiles - 1:
                        line = lax.broadcasted_iota(jnp.int32, (16, 256), 0) + offset
                        column = lax.broadcasted_iota(jnp.int32, (16, 256), 1)
                        s = jnp.where(column <= line, s, MASKED)
                    pieces.append(s)
                top = functools.reduce(jnp.maximum, pieces)
                top = jnp.max(top, axis=-1, keepdims=True)
                raised = [jnp.exp(s - top) for s in pieces]
                whole = jnp.sum(functools.reduce(jnp.add, raised), axis=-1, keepdims=True)
                inverse = 1.0 / whole
                outer = pl.ds(pl.multiple_of(block * block_rows + offset, 16), 16)
                for t in range(tiles):
                    probs[h, outer, 256 * t : 256 * (t + 1)] = (raised[t] * inverse).astype(BF)

            row_loop(block_rows, 16, soften)
            mix[here, dh * h : dh * (h + 1)] = dot(
                probs[h, here, 0 : 256 * tiles], vals[0 : 256 * tiles, dh * h : dh * (h + 1)]
            ).astype(BF)
        if block == 0:
            loaded("w_out")
        for t in range(4):
            part[t, here, :] = dot(mix[here, :], wout[256 * t : 256 * (t + 1), :], NT)
        for sub in (2 * block, 2 * block + 1):
            sum_start(0, sub)
        if block == 0:
            tick(COMP)
        for sub in (2 * block, 2 * block + 1):
            sum_across(0, sub)

    loaded("cotangent")
    loaded("w_down")
    for t in range(4):
        cols = pl.ds(256 * t, 256)
        rgrad[:, cols] = dot(cot_v[...], wdn[:, cols])

    nf, act = mem_v, cmp_v
    for sub in range(subs):
        sum_back(0, sub)
        if sub in (1, 3):
            tick(COMP + 1 + sub // 2)
        sum_done(0, sub)

        def residual_rows(offset, sub=sub):
            here = pl.ds(pl.multiple_of(sub * sub_rows + offset, 32), 32)
            value = seg_v[here, :].astype(F32) + total_rows(here)
            resid[here, :] = value
            centered, inverse = moments(value)
            nf[here, :] = (centered * inverse * gain_ffn[...]).astype(BF)

        row_loop(sub_rows, 32, residual_rows)
    sum_used(0)

    loaded("w_up")
    hidden_lane = place_lane[0]
    for t in range(4):
        cols = slice(256 * t, 256 * (t + 1))
        value, slope = gelu_pair(dot(nf[...], wup[:, cols]))
        act[:, cols] = value.astype(BF)
        rot[0, :, hidden_lane + 256 * t : hidden_lane + 256 * (t + 1)] = (
            rgrad[:, cols] * slope
        ).astype(BF)
        store_unit(DOWN + t, dot(cot_v[...], act[:, cols], TN))
        unit_send(DOWN + t, 0)

    def hidden_grad():
        return rot[0, :, hidden_lane : hidden_lane + width]

    for which in (other, core):
        for i in range(2):
            lines = pl.ds(pl.multiple_of(512 * which + 256 * i, 256), 256)
            part[2 * which + i] = dot(hidden_grad(), wup[lines, :], NT)
        if which is other:
            for sub in range(subs):
                sum_start(1, sub)
    for sub in range(subs):
        sum_across(1, sub)
    drain(COMP, COMP + 2)
    for t in range(4):
        cols = slice(hidden_lane + 256 * t, hidden_lane + 256 * (t + 1))
        store_unit(UP + t, dot(nf[...], rot[0, :, cols], TN))
        unit_send(UP + t, 0)
    for t in range(4):
        grads[22 + t] = dot(act[...], wdn[256 * t : 256 * (t + 1), :], NT)
    for sub in range(subs):
        sum_start(2, sub)

    agrad = mem_v
    small[...] = jnp.zeros_like(small)
    for sub in range(subs):
        sum_back(1, sub)
        if sub == 2:
            tick(DOWN)
        sum_done(1, sub)

        def residual_back(offset, carry, sub=sub):
            here = pl.ds(pl.multiple_of(sub * sub_rows + offset * 32, 32), 32)
            grad = total_rows(here)
            centered, inverse = moments(resid[here, :])
            xhat = centered * inverse
            back = norm_back(grad * gain_ffn[...], xhat, inverse)
            value = cot_v[here, :].astype(F32) + back
            rgrad[here, :] = value
            agrad[here, :] = value.astype(BF)
            return carry + jnp.sum(grad * xhat, axis=0, keepdims=True)

        gain_part = lax.fori_loop(
            0, sub_rows // 32, residual_back, jnp.zeros((1, width), F32)
        )
        for j in range(width // 128):
            line = slice(8 + j, 9 + j)
            small[line, :] = small[line, :] + gain_part[:, 128 * j : 128 * (j + 1)]
    sum_used(1)
    for sub in range(subs):
        sum_across(2, sub)
    tick(DOWN + 1)

    mgrad[...] = dot(agrad[...], wout[...]).astype(BF)
    for h in range(2):
        wup[:, 3 * dh * h : 3 * dh * h + dh] = jnp.zeros((prior, dh), BF)
    for h in range(2):
        lanes = slice(dh * h, dh * (h + 1))
        col = 3 * dh * h
        mg = mgrad[:, lanes]
        delta = jnp.sum(mg.astype(F32) * mix[:, lanes].astype(F32), axis=-1, keepdims=True)

        def key_tile(t, target, lines, ds_rows, ds_cols, h=h, lanes=lanes, col=col, mg=mg, delta=delta):
            keys = pl.ds(pl.multiple_of(t * 256, 256), 256)
            p = probs[h, :, keys]
            dp_tile = dot(mg, vals[keys, lanes], NT)
            ds = (p.astype(F32) * (dp_tile - delta)).astype(BF)
            wdn[ds_rows, ds_cols] = ds
            cq = rot[h, :, query_lane[h] : query_lane[h] + dh]
            target[lines, col + dh : col + 2 * dh] = (dot(ds, cq, TN) * scale).astype(BF)
            target[lines, col + 2 * dh : col + 3 * dh] = dot(p, mg, TN).astype(BF)

        def prior_tile(t, carry):
            at = pl.ds(pl.multiple_of(t * 256, 256), 256)
            key_tile(t, wup, at, slice(0, rows), at)
            return carry

        lax.fori_loop(0, 4, prior_tile, 0)
        for t in range(2):
            at = slice(256 * t, 256 * (t + 1))
            key_tile(4 + t, dseg, at, slice(rows, 2 * rows), at)

        def times_keys(cols):
            return (
                dot(wdn[0:rows, :], kf[0:prior, cols])
                + dot(wdn[rows : 2 * rows, 0:rows], kf[prior : prior + rows, cols])
            ) * scale

        for j in range(2):
            cols = slice(256 * j, 256 * (j + 1))
            upper = times_keys(slice(dh + 256 * j, dh + 256 * (j + 1)))
            lower = times_keys(slice(dh + half + 256 * j, dh + half + 256 * (j + 1)))
            begin = place_lane[h] + 256 * j
            rot[h, :, begin : begin + 256] = (
                upper * qsin[:, cols] - lower * qcos[:, cols]
            ).astype(BF)
            rot[h, :, begin + half : begin + half + 256] = (
                upper * qcos[:, cols] + lower * qsin[:, cols]
            ).astype(BF)
        content = times_keys(slice(key_lane[h], key_lane[h] + dh))
        position = dot(rot[h, :, place_lane[h] : place_lane[h] + width], wrel[:, lanes])
        dseg[:, col : col + dh] = (content + position).astype(BF)
        small[h : h + 1, :] = jnp.sum(content, axis=0, keepdims=True)
        small[2 + h : 3 + h, :] = jnp.sum(position, axis=0, keepdims=True)
        if h == 0:
            tick(DOWN + 2)

    stage = cmp_v
    for sub in range(subs):
        sum_back(2, sub)
    tick(DOWN + 3)
    for which in (other, core):
        for i in range(2):
            lines = pl.ds(pl.multiple_of(512 * which + 256 * i, 256), 256)
            part[2 * which + i] = dot(dseg[...], wqkv[lines, :], NT)
        if which is other:
            for sub in range(subs):
                sum_start(3, sub)
    for sub in range(subs):
        sum_across(3, sub)
    for sub in range(subs):
        sum_done(2, sub)

        def output_rows(offset, sub=sub):
            here = pl.ds(pl.multiple_of(sub * sub_rows + offset, 32), 32)
            stage[here, :] = (resid[here, :] + total_rows(here)).astype(BF)

        row_loop(sub_rows, 32, output_rows)
    sum_used(2)
    out_copy = pltpu.make_async_copy(stage, layer_out, out_sem.at[16])
    out_copy.start()

    drain(DOWN, DOWN + 3)
    for t in range(3):
        outs.pop(COMP + t).wait()
        cols = slice(256 * t, 256 * (t + 1))
        store_unit(
            QKV + t,
            dot(normed[0:prior, :], wup[:, cols], TN) + dot(normed[prior:, :], dseg[:, cols], TN),
        )
        unit_send(QKV + t, 0)
    store_unit(OUT, dot(agrad[...], mix[...], TN))
    for h in range(2):
        lanes = slice(dh * h, dh * (h + 1))
        store_unit(
            REL,
            dot(rot[h, :, place_lane[h] : place_lane[h] + width], pin[:, lanes], TN),
            lanes,
        )
    unit_send(OUT, 0)

    for s in range(steps):
        copy = remote(small, small_in.at[s], small_send.at[s], small_recv.at[s], dp_peers[s])
        copy.wait()
        small[...] = small[...] + small_in[s]

    tick(UP)

    for sub in range(subs):
        sum_back(3, sub)
        sum_done(3, sub)

        def input_rows(offset, sub=sub):
            here = pl.ds(pl.multiple_of(sub * sub_rows + offset, 32), 32)
            centered, inverse = moments(seg_v[here, :].astype(F32))
            back = norm_back(total_rows(here) * gain_attn[...], centered * inverse, inverse)
            resid[here, :] = rgrad[here, :] + back

        row_loop(sub_rows, 32, input_rows)
    sum_used(3)
    grad_copy = pltpu.make_async_copy(resid, input_grad, out_sem.at[17])
    grad_copy.start()

    line = lax.broadcasted_iota(jnp.int32, (piece, width), 0)
    column = lax.broadcasted_iota(jnp.int32, (piece, width), 1)
    mine = column == dp * piece + line

    def own_column(row):
        return jnp.sum(jnp.where(mine, row, 0.0), axis=-1, keepdims=True)

    def as_row(values):
        line = lax.broadcasted_iota(jnp.int32, (piece, 128), 0)
        column = lax.broadcasted_iota(jnp.int32, (piece, 128), 1)
        return jnp.sum(jnp.where(line == column, values, 0.0), axis=0, keepdims=True)

    gain_row = jnp.concatenate([small[8 + j : 9 + j, :] for j in range(width // 128)], axis=1)
    gain_ffn_out[...] = as_row(own_column(gain_row))[:, 0:piece]
    bias_piece = head_size // n
    line = lax.broadcasted_iota(jnp.int32, (bias_piece, head_size), 0)
    column = lax.broadcasted_iota(jnp.int32, (bias_piece, head_size), 1)
    owned = column == dp * bias_piece + line
    for h in range(2):
        cbias_out[:, h : h + 1] = jnp.sum(
            jnp.where(owned, small[h : h + 1, :], 0.0), axis=-1, keepdims=True
        )
        pbias_out[:, h : h + 1] = jnp.sum(
            jnp.where(owned, small[2 + h : 3 + h, :], 0.0), axis=-1, keepdims=True
        )

    for unit in range(UP + 1, REL + 1):
        tick(unit)
        if unit == UP + 3:
            unit_send(REL, 0)
    drain(UP, REL)

    own = pl.ds(pl.multiple_of(dp * piece, piece), piece)
    gathered = jnp.zeros((piece, 1), F32)
    for t in range(3):
        at, start, length = region(QKV + t, steps - 1, True)
        product = grads[at, pl.ds(start, length), :] * wqkv[
            own, 256 * t : 256 * (t + 1)
        ].astype(F32)
        gathered = gathered + jnp.sum(product, axis=-1, keepdims=True)
    tiny[0:1, :] = as_row(gathered / own_column(gain_attn[...]))
    for s, peer in enumerate((core_peer, x_peer)):
        copy = remote(tiny, tiny_in.at[s], tiny_send.at[s], tiny_recv.at[s], peer)
        copy.wait()
        tiny[...] = tiny[...] + tiny_in[s]
    gain_attn_out[...] = tiny[0:1, 0:piece]

    for copy in outs.values():
        copy.wait()
    out_copy.wait()
    grad_copy.wait()


def shards(
    n,
    segment,
    memory,
    compressed,
    mem_fill,
    comp_fill,
    gain_attn,
    w_qkv,
    content_bias,
    position_bias,
    w_rel,
    w_out,
    gain_ffn,
    w_up,
    w_down,
    w_comp,
    out_cotangent,
    comp_cotangent,
):
    rows, width = segment.shape[1:]
    keys = 3 * rows
    steps = n.bit_length() - 1
    piece = width // n
    head_size = content_bias.shape[0]
    new_count = comp_cotangent.shape[1]
    pad_count = -(-new_count // 16) * 16
    features, sine, cosine = tables(width, 2 * rows, keys)
    vm, anyw = pl.BlockSpec(memory_space=pltpu.VMEM), pl.BlockSpec(memory_space=pl.ANY)
    smem = pl.BlockSpec(memory_space=pltpu.SMEM)
    dma = pltpu.SemaphoreType.DMA
    plain = pltpu.SemaphoreType.REGULAR
    later_count = LATER_RING * max(steps - 1, 1)
    scratch = [
        pltpu.VMEM((rows, width), BF),
        pltpu.VMEM((rows, width), BF),
        pltpu.VMEM((rows, width), BF),
        pltpu.VMEM((rows, width), BF),
        pltpu.VMEM(w_qkv.shape, BF),
        pltpu.VMEM(w_rel.shape, BF),
        pltpu.VMEM(w_out.shape, BF),
        pltpu.VMEM(w_up.shape, BF),
        pltpu.VMEM(w_down.shape, BF),
        pltpu.VMEM((keys, width + 2 * head_size), BF),
        pltpu.VMEM((rows, width // 2), F32),
        pltpu.VMEM((rows, width // 2), F32),
        pltpu.VMEM((keys, 2 * head_size), BF),
        pltpu.VMEM((2, rows, width + head_size), BF),
        pltpu.VMEM((rows, 2 * head_size), BF),
        pltpu.VMEM((keys, width), BF),
        pltpu.VMEM((2, rows, keys), BF),
        pltpu.VMEM((rows, 2 * head_size), BF),
        pltpu.VMEM((rows, 2 * head_size), BF),
        pltpu.VMEM((rows, 6 * head_size), BF),
        pltpu.VMEM((rows, width), F32),
        pltpu.VMEM((rows, width), F32),
        pltpu.VMEM((pad_count, 256), BF),
        pltpu.VMEM((8, 2 * rows), F32),
        pltpu.VMEM((26, 512, 256), F32),
        pltpu.VMEM((4, rows, 256), F32),
        pltpu.VMEM((2, rows, 256), F32),
        pltpu.VMEM((2, 2, rows, 256), F32),
        pltpu.VMEM((4, rows, 256), F32),
        pltpu.VMEM((16, 128), F32),
        pltpu.VMEM((steps, 16, 128), F32),
        pltpu.VMEM((8, 128), F32),
        pltpu.VMEM((2, 8, 128), F32),
        pltpu.VMEM((FIRST_RING, 512, 256), F32),
        pltpu.VMEM((LATER_RING, 512, 256), F32),
        dma((16,)),
        dma((18,)),
        dma((FIRST_RING,)),
        dma((FIRST_RING,)),
        plain((2, FIRST_RING)),
        dma((later_count,)),
        dma((later_count,)),
        plain((2, later_count)),
        dma((4,)),
        dma((4,)),
        plain,
        dma((2, 4)),
        dma((2, 4)),
        plain((2,)),
        dma((4,)),
        dma((4,)),
        plain,
        dma((steps,)),
        dma((steps,)),
        dma((2,)),
        dma((2,)),
    ]
    shape = jax.ShapeDtypeStruct
    results = pl.pallas_call(
        functools.partial(kernel, n),
        out_shape=(
            shape((rows, width), BF),
            shape((new_count, 256), BF),
            shape((rows, width), F32),
            shape((1, piece), F32),
            shape((piece, w_qkv.shape[1]), F32),
            shape((head_size // n, 2), F32),
            shape((head_size // n, 2), F32),
            shape((piece, w_rel.shape[1]), F32),
            shape((piece, w_out.shape[1]), F32),
            shape((1, piece), F32),
            shape((piece, w_up.shape[1]), F32),
            shape((piece, w_down.shape[1]), F32),
            shape((3 * piece, w_comp.shape[1]), F32),
        ),
        in_specs=[smem] * 2 + [vm] * 5 + [anyw] * 13,
        out_specs=(anyw, vm, anyw, vm, anyw, vm, vm, anyw, anyw, vm, anyw, anyw, anyw),
        scratch_shapes=scratch,
        compiler_params=pltpu.CompilerParams(
            collective_id=0, has_side_effects=True, vmem_limit_bytes=63 * 2**20
        ),
    )(
        mem_fill,
        comp_fill,
        gain_attn.reshape(1, width),
        gain_ffn.reshape(1, width),
        content_bias,
        position_bias,
        comp_cotangent[0],
        segment[0],
        memory[0],
        compressed[0],
        w_qkv,
        w_rel,
        w_out,
        w_up,
        w_down,
        w_comp,
        out_cotangent[0],
        jnp.asarray(features, BF),
        jnp.asarray(sine),
        jnp.asarray(cosine),
    )
    layer, new, grad, gattn, qkv, cbias, pbias, rel, outp, gffn, up, down, comp = results
    return (
        layer[None],
        new[None],
        grad[None],
        gattn.reshape(piece),
        qkv,
        cbias,
        pbias,
        rel,
        outp,
        gffn.reshape(piece),
        up,
        down,
        comp,
    )


def solution(mesh):
    stream = P("dp", None, None)
    split = P(None, "head")
    return jax.shard_map(
        functools.partial(shards, mesh.shape["dp"]),
        mesh=mesh,
        in_specs=(
            stream,
            stream,
            stream,
            P("dp"),
            P("dp"),
            P(),
            split,
            split,
            split,
            split,
            split,
            P(),
            split,
            split,
            split,
            stream,
            P("dp", None, "head"),
        ),
        out_specs=(
            stream,
            P("dp", None, "head"),
            stream,
            P("dp"),
            P("dp", "head"),
            P("dp", "head"),
            P("dp", "head"),
            P("dp", "head"),
            P("dp", "head"),
            P("dp"),
            P("dp", "head"),
            P("dp", "head"),
            P("dp", "head"),
        ),
        check_vma=False,
    )
```

```python
import functools

import jax
import jax.numpy as jnp
import numpy as np
from jax import lax
from jax.experimental import pallas as pl
from jax.experimental.pallas import tpu as pltpu
from jax.sharding import PartitionSpec as P

MESH = pl.DeviceIdType.MESH
BF = jnp.bfloat16
F32 = jnp.float32
EPS = 1e-05
MASKED = -1e30
NN = (((1,), (0,)), ((), ()))
NT = (((1,), (1,)), ((), ()))
TN = (((0,), (0,)), ((), ()))
FIRST_SLOTS = 8
BLOCKS = 4
LATER_SLOTS = 4


def dot(a, b, dims=NN):
    return lax.dot_general(a, b, dims, preferred_element_type=F32)


def row_loop(total, chunk, body, unroll=1):
    def step(index, carry):
        body(pl.multiple_of(index * chunk, chunk))
        return carry

    lax.fori_loop(0, total // chunk, step, 0, unroll=unroll)


def tables(width, prior, keys):
    half = width // 2
    frequency = np.exp(-np.log(10000.0) * np.arange(half) / half)
    angles = np.arange(keys)[:, None] * frequency[None, :]
    sine, cosine = np.sin(angles), np.cos(angles)
    features = np.concatenate([cosine, sine], axis=1).astype(np.float32)
    return features, sine[prior:].astype(np.float32), cosine[prior:].astype(np.float32)


def moments(rows):
    average = jnp.mean(rows, axis=-1, keepdims=True)
    centered = rows - average
    spread = jnp.mean(centered * centered, axis=-1, keepdims=True)
    return centered, lax.rsqrt(spread + EPS)


def norm_back(scaled, xhat, inverse):
    along = jnp.mean(scaled * xhat, axis=-1, keepdims=True)
    return (scaled - jnp.mean(scaled, axis=-1, keepdims=True) - xhat * along) * inverse


def gelu_pair(x):
    c = 0.7978845608028654
    square = x * x
    t = jnp.tanh(c * x * (1.0 + 0.044715 * square))
    half = 0.5 * (1.0 + t)
    slope = half + (0.5 * c) * x * (1.0 - t * t) * (1.0 + 0.134145 * square)
    return x * half, slope


def kernel(
    n,
    mem_fill,
    comp_fill,
    gain_attn,
    gain_ffn,
    content_bias,
    position_bias,
    comp_cot,
    segment,
    memory,
    compressed,
    w_qkv,
    w_rel,
    w_out,
    w_up,
    w_down,
    w_comp,
    cotangent,
    features,
    sine,
    cosine,
    layer_out,
    new_rows,
    input_grad,
    gain_attn_out,
    qkv_out,
    cbias_out,
    pbias_out,
    rel_out,
    outp_out,
    gain_ffn_out,
    up_out,
    down_out,
    comp_out,
    seg_v,
    mem_v,
    cmp_v,
    cot_v,
    wqkv,
    wrel,
    wout,
    wup,
    wdn,
    kf,
    qsin,
    qcos,
    vals,
    rot,
    pin,
    normed,
    probs,
    mix,
    shrink,
    mgrad,
    dseg,
    resid,
    rgrad,
    ccot,
    maskrow,
    grads,
    part,
    core_in,
    x_in,
    total,
    small,
    small_in,
    tiny,
    tiny_in,
    first_in,
    later_in,
    in_sem,
    out_sem,
    first_send,
    first_recv,
    first_free,
    later_send,
    later_recv,
    later_free,
    core_send,
    core_recv,
    core_free,
    x_send,
    x_recv,
    x_free,
    back_send,
    back_recv,
    back_free,
    small_send,
    small_recv,
    tiny_send,
    tiny_recv,
):
    steps = n.bit_length() - 1
    width = seg_v.shape[1]
    rows = seg_v.shape[0]
    prior = 2 * rows
    head_size = content_bias.shape[1]
    scale = head_size ** (-0.5)
    piece = width // n
    new_count = comp_cot.shape[0]
    pad_count = ccot.shape[0]

    dp = lax.axis_index("dp")
    head = lax.axis_index("head")
    core = lax.rem(head, 2)
    other = 1 - core
    core_peer = (dp, head + 1 - 2 * core)
    x_peer = (dp, lax.rem(head + 2, 4))
    bits = [lax.rem(dp // (1 << s), 2) for s in range(steps)]
    dp_peers = [(dp + (1 - 2 * bits[s]) * (1 << s), head) for s in range(steps)]

    loads = {}

    def load(name, index, source, target):
        copy = pltpu.make_async_copy(source, target, in_sem.at[index])
        copy.start()
        loads[name] = copy

    def loaded(name):
        loads.pop(name).wait()

    load("memory", 0, memory, mem_v)
    for tap in range(3):
        load(
            f"w_comp{tap}",
            1 + tap,
            w_comp.at[pl.ds(tap * width, width)],
            wup.at[:, pl.ds(256 * tap, 256)],
        )
    load("compressed", 4, compressed, cmp_v)
    load("segment", 5, segment, seg_v)
    load("w_qkv", 6, w_qkv, wqkv)
    load("w_rel", 7, w_rel, wrel)
    load("sine", 8, sine, qsin)
    load("cosine", 9, cosine, qcos)
    load("features", 10, features, kf.at[:, pl.ds(head_size, width)])
    load("w_out", 11, w_out, wout)
    load("cotangent", 12, cotangent, cot_v)
    load("w_down", 13, w_down, wdn)

    barrier = pltpu.get_barrier_semaphore()
    greeted = [core_peer, x_peer] + dp_peers
    for peer in greeted:
        pl.semaphore_signal(barrier, inc=1, device_id=peer, device_id_type=MESH)

    def remote(source, target, send, recv, peer):
        copy = pltpu.make_async_remote_copy(
            src_ref=source,
            dst_ref=target,
            send_sem=send,
            recv_sem=recv,
            device_id=peer,
            device_id_type=MESH,
        )
        copy.start()
        return copy

    low_first = list(range(steps))
    units = []
    for t in range(3):
        units.append((t, low_first, comp_out.at[pl.ds(t * piece, piece), :]))
    for t in range(4):
        units.append((3 + t, low_first, down_out.at[:, pl.ds(256 * t, 256)]))
    for t in range(4):
        units.append((7 + t, low_first, up_out.at[:, pl.ds(256 * t, 256)]))
    for t in range(3):
        units.append((t, low_first, qkv_out.at[:, pl.ds(256 * t, 256)]))
    units.append((11, low_first, outp_out.at[...]))
    units.append((12, low_first, rel_out.at[...]))
    COMP, DOWN, UP, QKV, OUT, REL = 0, 3, 7, 11, 14, 15
    outs = {}
    sends = {}
    done = set()

    def place(order, j):
        found = 0
        for bit in order:
            found = 2 * found + ((j >> bit) & 1)
        return found

    def store_rows(unit, j, value, lanes=slice(None)):
        at, order, _ = units[unit]
        row = place(order, j) * piece
        grads[2 * at + row // 512, pl.ds(row % 512, piece), lanes] = value

    def store_unit(unit, value, lanes=slice(None)):
        for j in range(n):
            store_rows(unit, j, value[piece * j : piece * (j + 1)], lanes)

    def region(unit, step, mine):
        at, order, _ = units[unit]
        first = bits[order[0]]
        if step == 0:
            return 2 * at + (first if mine else 1 - first), 0, 512
        start = 0
        for s in range(1, step):
            start = start + bits[order[s]] * (width >> (s + 1))
        length = width >> (step + 1)
        mybit = bits[order[step]]
        start = start + (mybit if mine else 1 - mybit) * length
        return 2 * at + first, pl.multiple_of(start, length), length

    def slot_refs(unit, step):
        if step == 0:
            slot = unit % FIRST_SLOTS
            return first_in.at[slot], first_send.at[slot], first_recv.at[slot], first_free.at[slot]
        slot = unit % LATER_SLOTS
        index = (step - 1) * LATER_SLOTS + slot
        length = width >> (step + 1)
        begin = 512 - (512 >> (step - 1))
        return (
            later_in.at[slot, pl.ds(begin, length), :],
            later_send.at[index],
            later_recv.at[index],
            later_free.at[index],
        )

    def slots(step):
        return LATER_SLOTS if step else FIRST_SLOTS

    def unit_send(unit, step):
        target, send, recv, free = slot_refs(unit, step)
        if unit >= slots(step):
            assert (unit - slots(step), "done") in done
            pl.semaphore_wait(free, 1)
        at, start, length = region(unit, step, False)
        peer = dp_peers[units[unit][1][step]]
        sends[unit, step] = remote(grads.at[at, pl.ds(start, length), :], target, send, recv, peer)

    def unit_step(unit, step):
        if (unit, step) in done:
            return
        done.add((unit, step))
        target, _, _, free = slot_refs(unit, step)
        sends[unit, step].wait_recv()
        at, start, length = region(unit, step, True)
        chunk = min(64, length)

        def add(offset):
            here = pl.ds(pl.multiple_of(start + offset, chunk), chunk)
            grads[at, here, :] = grads[at, here, :] + target[pl.ds(offset, chunk), :]

        row_loop(length, chunk, add)
        later = unit + slots(step)
        if later < len(units):
            peer = dp_peers[units[later][1][step]]
            pl.semaphore_signal(free, inc=1, device_id=peer, device_id_type=MESH)
        if step + 1 < steps:
            unit_send(unit, step + 1)
        else:
            for s in range(steps):
                sends.pop((unit, s)).wait_send()
            copy = pltpu.make_async_copy(
                grads.at[at, pl.ds(start, length), :], units[unit][2], out_sem.at[unit]
            )
            copy.start()
            outs[unit] = copy
            done.add((unit, "done"))

    lags = [0, 1, 3] if steps == 3 else [0] * steps

    def tick(unit):
        for step in range(steps):
            if unit >= lags[step]:
                unit_step(unit - lags[step], step)

    def unit_upto(unit, last):
        for step in range(last + 1):
            unit_step(unit, step)

    def drain(unit):
        for passed in range(1, max(lags) + 1):
            for step in range(1, steps):
                if 0 <= unit + passed - lags[step] <= unit:
                    unit_step(unit + passed - lags[step], step)

    moves = {}
    subs = 4
    sub_rows = rows // subs

    def span(sub):
        return pl.ds(sub * sub_rows, sub_rows)

    def sum_source(k):
        return (grads, 22) if k == 2 else (part, 0)

    def sum_start(k, sub):
        if k >= 1 and sub == 0:
            pl.semaphore_wait(core_free, 1)
        ref, base = sum_source(k)
        moves[k, "core", sub] = remote(
            ref.at[pl.ds(base + 2 * other, 2), span(sub), :],
            core_in.at[:, span(sub), :],
            core_send.at[sub],
            core_recv.at[sub],
            core_peer,
        )

    def sum_across(k, sub):
        ref, base = sum_source(k)
        moves[k, "core", sub].wait()
        for i in range(2):
            at = base + 2 * core + i
            ref[at, span(sub), :] = ref[at, span(sub), :] + core_in[i, span(sub), :]
        if sub == subs - 1 and k < 3:
            pl.semaphore_signal(core_free, inc=1, device_id=core_peer, device_id_type=MESH)
        if k >= 2 and sub == 0:
            pl.semaphore_wait(x_free.at[k % 2], 1)
        moves[k, "x", sub] = remote(
            ref.at[pl.ds(base + 2 * core, 2), span(sub), :],
            x_in.at[k % 2, :, span(sub), :],
            x_send.at[k % 2, sub],
            x_recv.at[k % 2, sub],
            x_peer,
        )

    def sum_back(k, sub):
        ref, base = sum_source(k)
        moves[k, "x", sub].wait_recv()
        for i in range(2):
            total[2 * core + i, span(sub), :] = (
                ref[base + 2 * core + i, span(sub), :] + x_in[k % 2, i, span(sub), :]
            )
        if sub == subs - 1 and k < 2:
            pl.semaphore_signal(x_free.at[k % 2], inc=1, device_id=x_peer, device_id_type=MESH)
        if k >= 1 and sub == 0:
            pl.semaphore_wait(back_free, 1)
        here = total.at[pl.ds(2 * core, 2), span(sub), :]
        moves[k, "back", sub] = remote(here, here, back_send.at[sub], back_recv.at[sub], core_peer)

    def sum_done(k, sub):
        moves[k, "back", sub].wait_recv()

    def sum_used(k):
        for sub in range(subs):
            moves[k, "x", sub].wait_send()
            moves[k, "back", sub].wait_send()
        if k < 3:
            pl.semaphore_signal(back_free, inc=1, device_id=core_peer, device_id_type=MESH)

    def total_rows(here):
        return jnp.concatenate([total[t, here, :] for t in range(4)], axis=1)

    ccot[...] = jnp.zeros_like(ccot)
    ccot[0:new_count, :] = comp_cot[...]
    loaded("memory")
    fill = mem_fill[0]
    compressed_rows = jnp.zeros((pad_count, 256), F32)
    row_at = lax.broadcasted_iota(jnp.int32, (pad_count, rows), 0)
    slot_at = lax.broadcasted_iota(jnp.int32, (pad_count, rows), 1)
    for tap in range(3):
        pick = (slot_at == 3 * row_at + tap) & (slot_at >= rows - fill) & (row_at < new_count)
        window = dot(jnp.where(pick, 1.0, 0.0).astype(BF), mem_v[...]).astype(BF)
        loaded(f"w_comp{tap}")
        compressed_rows = compressed_rows + dot(window, wup[:, pl.ds(256 * tap, 256)])
        tap_grad = dot(window, ccot[...], TN)
        for i in range(n):
            j, t = divmod(n * tap + i, 3)
            store_rows(COMP + t, j, tap_grad[piece * i : piece * (i + 1)])
    new_rows[...] = compressed_rows[0:new_count].astype(BF)
    pl.semaphore_wait(barrier, len(greeted))
    for t in range(3):
        unit_send(COMP + t, 0)
    load("w_up", 1, w_up, wup)

    lane = lax.broadcasted_iota(jnp.int32, (1, rows), 1)
    maskrow[0:1, 0:rows] = jnp.where(lane >= rows - comp_fill[0], 0.0, MASKED)
    maskrow[0:1, rows:prior] = jnp.where(lane >= rows - fill, 0.0, MASKED)

    def norm_into(source, base):
        def body(offset):
            centered, inverse = moments(source[pl.ds(offset, 64), :].astype(F32))
            normed[pl.ds(pl.multiple_of(base + offset, 64), 64), :] = (
                centered * inverse * gain_attn[...]
            ).astype(BF)

        row_loop(rows, 64, body)

    loaded("compressed")
    norm_into(cmp_v, 0)
    norm_into(mem_v, rows)
    loaded("segment")
    norm_into(seg_v, prior)

    loaded("w_qkv")
    loaded("features")
    dh = head_size
    key_lane = (0, dh + width)
    pair_lane = (0, dh)
    place_lane = (dh, 0)
    query_lane = (0, width)
    for block in range(2):
        here = pl.ds(block * rows, rows)
        for h in range(2):
            both = dot(normed[here, :], wqkv[:, 3 * dh * h + dh : 3 * dh * (h + 1)])
            kf[here, key_lane[h] : key_lane[h] + dh] = both[:, 0:dh].astype(BF)
            vals[here, dh * h : dh * (h + 1)] = both[:, dh:].astype(BF)
    here = pl.ds(prior, rows)
    queries = [None, None]
    three = [dot(normed[here, :], wqkv[:, 256 * t : 256 * (t + 1)]) for t in range(3)]
    queries[0] = three[0][:, 0:dh]
    kf[here, key_lane[0] : key_lane[0] + dh] = three[0][:, dh:].astype(BF)
    vals[here, 0:dh] = three[1][:, 0:dh].astype(BF)
    queries[1] = three[1][:, dh:]
    kf[here, key_lane[1] : key_lane[1] + dh] = three[2][:, 0:dh].astype(BF)
    vals[here, dh : 2 * dh] = three[2][:, dh:].astype(BF)
    for h in range(2):
        rot[h, :, query_lane[h] : query_lane[h] + dh] = (
            queries[h] + content_bias[h : h + 1, :]
        ).astype(BF)
        pin[:, dh * h : dh * (h + 1)] = (queries[h] + position_bias[h : h + 1, :]).astype(BF)

    loaded("w_rel")
    loaded("sine")
    loaded("cosine")
    half = width // 2
    for h in range(2):
        for j in range(2):
            cols = slice(256 * j, 256 * (j + 1))
            weights = wrel[256 * j : 256 * (j + 1), dh * h : dh * (h + 1)]
            upper = dot(pin[:, dh * h : dh * (h + 1)], weights, NT)
            weights = wrel[half + 256 * j : half + 256 * (j + 1), dh * h : dh * (h + 1)]
            lower = dot(pin[:, dh * h : dh * (h + 1)], weights, NT)
            begin = place_lane[h] + 256 * j
            rot[h, :, begin : begin + 256] = (
                upper * qsin[:, cols] + lower * qcos[:, cols]
            ).astype(BF)
            rot[h, :, begin + half : begin + half + 256] = (
                lower * qsin[:, cols] - upper * qcos[:, cols]
            ).astype(BF)

    block_rows = rows // BLOCKS
    exponent_scale = scale * 1.4426950408889634
    probs[:, 0 : rows // 2, prior + 256 : prior + 512] = jnp.zeros((2, rows // 2, 256), BF)
    line = lax.broadcasted_iota(jnp.int32, (block_rows, 256), 0)
    column = lax.broadcasted_iota(jnp.int32, (block_rows, 256), 1)
    for block in range(BLOCKS):
        base = block * block_rows
        here = pl.ds(base, block_rows)
        tiles = 5 + base // 256
        for h in range(2):
            top = None
            for t in range(tiles):
                keys = slice(256 * t, 256 * (t + 1))
                s = dot(rot[h, here, :], kf[keys, pair_lane[h] : pair_lane[h] + dh + width], NT)
                s = s * exponent_scale
                if t < 4:
                    s = s + maskrow[0:1, keys]
                if t == tiles - 1:
                    s = jnp.where(column <= line + base % 256, s, MASKED)
                grads[6 + t, 256 * h : 256 * h + block_rows, :] = s
                wide = jnp.maximum(s[:, 0:128], s[:, 128:256])
                top = wide if top is None else jnp.maximum(top, wide)
            top = jnp.max(top, axis=-1, keepdims=True)
            whole = None
            for t in range(tiles):
                raised = jnp.exp2(grads[6 + t, 256 * h : 256 * h + block_rows, :] - top)
                probs[h, here, 256 * t : 256 * (t + 1)] = raised.astype(BF)
                wide = raised[:, 0:128] + raised[:, 128:256]
                whole = wide if whole is None else whole + wide
            inverse = 1.0 / jnp.sum(whole, axis=-1, keepdims=True)
            shrink[here, h : h + 1] = inverse
            if block and h == 0:
                for sub in waiting:
                    sum_across(0, sub)
            lanes = slice(dh * h, dh * (h + 1))
            mix[here, lanes] = (
                dot(probs[h, here, 0 : 256 * tiles], vals[0 : 256 * tiles, lanes]) * inverse
            ).astype(BF)
        if block == 0:
            loaded("w_out")
        for t in range(4):
            part[t, here, :] = dot(mix[here, :], wout[256 * t : 256 * (t + 1), :], NT)
        new_subs = range(block * subs // BLOCKS, (block + 1) * subs // BLOCKS)
        for sub in new_subs:
            sum_start(0, sub)
        waiting = list(new_subs)

    loaded("cotangent")
    loaded("w_down")
    for t in range(4):
        cols = pl.ds(256 * t, 256)
        rgrad[:, cols] = dot(cot_v[...], wdn[:, cols])
        if t == 1:
            for sub in waiting:
                sum_across(0, sub)
    tick(COMP)

    nf, act = mem_v, cmp_v
    for sub in range(subs):
        sum_back(0, sub)
        if sub == 2:
            tick(COMP + 1)
        sum_done(0, sub)

        def residual_rows(offset, sub=sub):
            here = pl.ds(pl.multiple_of(sub * sub_rows + offset, 64), 64)
            value = seg_v[here, :].astype(F32) + total_rows(here)
            resid[here, :] = value
            centered, inverse = moments(value)
            nf[here, :] = (centered * inverse * gain_ffn[...]).astype(BF)

        row_loop(sub_rows, 64, residual_rows)
    sum_used(0)

    loaded("w_up")
    hidden_lane = place_lane[0]
    for t in range(4):
        cols = slice(256 * t, 256 * (t + 1))
        value, slope = gelu_pair(dot(nf[...], wup[:, cols]))
        act[:, cols] = value.astype(BF)
        rot[0, :, hidden_lane + 256 * t : hidden_lane + 256 * (t + 1)] = (
            rgrad[:, cols] * slope
        ).astype(BF)
        store_unit(DOWN + t, dot(cot_v[...], act[:, cols], TN))
        unit_send(DOWN + t, 0)

    def hidden_grad():
        return rot[0, :, hidden_lane : hidden_lane + width]

    for which in (other, core):
        for i in range(2):
            lines = pl.ds(pl.multiple_of(512 * which + 256 * i, 256), 256)
            part[2 * which + i] = dot(hidden_grad(), wup[lines, :], NT)
        if which is other:
            for sub in range(subs):
                sum_start(1, sub)
    for sub in range(subs):
        sum_across(1, sub)
    for t in range(4):
        cols = slice(hidden_lane + 256 * t, hidden_lane + 256 * (t + 1))
        store_unit(UP + t, dot(nf[...], rot[0, :, cols], TN))
        if t == 0:
            tick(COMP + 2)
            if steps != 3:
                drain(COMP + 2)
        if t >= 1:
            unit_upto(COMP + t - 1, steps - 1)
        unit_send(UP + t, 0)
    for t in range(4):
        grads[22 + t] = dot(act[...], wdn[256 * t : 256 * (t + 1), :], NT)
    for sub in range(subs):
        sum_start(2, sub)

    agrad = mem_v
    small[...] = jnp.zeros_like(small)
    for sub in range(subs):
        sum_back(1, sub)
        if sub in (1, 3):
            tick(DOWN + sub // 2)
        sum_done(1, sub)

        def residual_back(offset, carry, sub=sub):
            here = pl.ds(pl.multiple_of(sub * sub_rows + offset * 64, 64), 64)
            grad = total_rows(here)
            centered, inverse = moments(resid[here, :])
            xhat = centered * inverse
            back = norm_back(grad * gain_ffn[...], xhat, inverse)
            value = cot_v[here, :].astype(F32) + back
            rgrad[here, :] = value
            agrad[here, :] = value.astype(BF)
            return carry + jnp.sum(grad * xhat, axis=0, keepdims=True)

        gain_part = lax.fori_loop(
            0, sub_rows // 64, residual_back, jnp.zeros((1, width), F32)
        )
        for j in range(width // 128):
            line = slice(8 + j, 9 + j)
            small[line, :] = small[line, :] + gain_part[:, 128 * j : 128 * (j + 1)]
    sum_used(1)
    for sub in range(subs):
        sum_across(2, sub)

    for h in range(2):
        lanes = slice(dh * h, dh * (h + 1))
        mgrad[:, lanes] = (dot(agrad[...], wout[:, lanes]) * shrink[:, h : h + 1]).astype(BF)
    for h in range(2):
        wup[:, 3 * dh * h : 3 * dh * h + dh] = jnp.zeros((prior, dh), BF)
    for h in range(2):
        lanes = slice(dh * h, dh * (h + 1))
        col = 3 * dh * h
        mg = mgrad[:, lanes]
        delta = jnp.sum(mg.astype(F32) * mix[:, lanes].astype(F32), axis=-1, keepdims=True)

        def key_tile(t, target, lines, ds_rows, ds_cols, h=h, lanes=lanes, col=col, mg=mg, delta=delta):
            keys = pl.ds(pl.multiple_of(t * 256, 256), 256)
            p = probs[h, :, keys]
            dp_tile = dot(mg, vals[keys, lanes], NT)
            ds = (p.astype(F32) * (dp_tile - delta)).astype(BF)
            wdn[ds_rows, ds_cols] = ds
            cq = rot[h, :, query_lane[h] : query_lane[h] + dh]
            target[lines, col + dh : col + 2 * dh] = (dot(ds, cq, TN) * scale).astype(BF)
            target[lines, col + 2 * dh : col + 3 * dh] = dot(p, mg, TN).astype(BF)

        def prior_tile(t, carry):
            at = pl.ds(pl.multiple_of(t * 256, 256), 256)
            key_tile(t, wup, at, slice(0, rows), at)
            return carry

        lax.fori_loop(0, 4, prior_tile, 0)
        for t in range(2):
            at = slice(256 * t, 256 * (t + 1))
            key_tile(4 + t, dseg, at, slice(rows, 2 * rows), at)

        def times_keys(cols):
            return (
                dot(wdn[0:rows, :], kf[0:prior, cols])
                + dot(wdn[rows : 2 * rows, 0:rows], kf[prior : prior + rows, cols])
            ) * scale

        for j in range(2):
            cols = slice(256 * j, 256 * (j + 1))
            upper = times_keys(slice(dh + 256 * j, dh + 256 * (j + 1)))
            lower = times_keys(slice(dh + half + 256 * j, dh + half + 256 * (j + 1)))
            begin = place_lane[h] + 256 * j
            rot[h, :, begin : begin + 256] = (
                upper * qsin[:, cols] - lower * qcos[:, cols]
            ).astype(BF)
            rot[h, :, begin + half : begin + half + 256] = (
                upper * qcos[:, cols] + lower * qsin[:, cols]
            ).astype(BF)
        content = times_keys(slice(key_lane[h], key_lane[h] + dh))
        position = dot(rot[h, :, place_lane[h] : place_lane[h] + width], wrel[:, lanes])
        dseg[:, col : col + dh] = (content + position).astype(BF)
        small[h : h + 1, :] = jnp.sum(content, axis=0, keepdims=True)
        small[2 + h : 3 + h, :] = jnp.sum(position, axis=0, keepdims=True)
        if h == 0:
            tick(DOWN + 2)

    stage = cmp_v
    for which in (other, core):
        for i in range(2):
            lines = pl.ds(pl.multiple_of(512 * which + 256 * i, 256), 256)
            part[2 * which + i] = dot(dseg[...], wqkv[lines, :], NT)
        if which is other:
            for sub in range(subs):
                sum_start(3, sub)
    for sub in range(subs):
        sum_across(3, sub)

    def small_start(s):
        moves["small", s] = remote(
            small, small_in.at[s], small_send.at[s], small_recv.at[s], dp_peers[s]
        )

    def small_step(s):
        moves["small", s].wait()
        small[...] = small[...] + small_in[s]
        if s + 1 < steps:
            small_start(s + 1)

    small_start(0)

    tick(DOWN + 3)

    def qkv_unit(t):
        outs.pop(COMP + t).wait()
        cols = slice(256 * t, 256 * (t + 1))
        store_unit(
            QKV + t,
            dot(normed[0:prior, :], wup[:, cols], TN) + dot(normed[prior:, :], dseg[:, cols], TN),
        )
        unit_send(QKV + t, 0)

    qkv_unit(0)
    tick(UP)

    for sub in range(subs):
        sum_back(2, sub)
    for sub in range(subs):
        sum_done(2, sub)

        def output_rows(offset, sub=sub):
            here = pl.ds(pl.multiple_of(sub * sub_rows + offset, 64), 64)
            stage[here, :] = (resid[here, :] + total_rows(here)).astype(BF)

        row_loop(sub_rows, 64, output_rows)
    sum_used(2)
    out_copy = pltpu.make_async_copy(stage, layer_out, out_sem.at[16])
    out_copy.start()

    for sub in range(subs):
        sum_back(3, sub)
        if sub in (1, 3):
            tick(UP + 1 + sub // 2)
            qkv_unit(1 + sub // 2)
        sum_done(3, sub)

        def input_rows(offset, sub=sub):
            here = pl.ds(pl.multiple_of(sub * sub_rows + offset, 64), 64)
            centered, inverse = moments(seg_v[here, :].astype(F32))
            back = norm_back(total_rows(here) * gain_attn[...], centered * inverse, inverse)
            resid[here, :] = rgrad[here, :] + back

        row_loop(sub_rows, 64, input_rows)
    sum_used(3)
    grad_copy = pltpu.make_async_copy(resid, input_grad, out_sem.at[17])
    grad_copy.start()
    store_unit(OUT, dot(agrad[...], mix[...], TN))
    for h in range(2):
        lanes = slice(dh * h, dh * (h + 1))
        store_unit(
            REL,
            dot(rot[h, :, place_lane[h] : place_lane[h] + width], pin[:, lanes], TN),
            lanes,
        )
    tick(UP + 3)
    unit_send(OUT, 0)
    small_step(0)
    tick(QKV)
    unit_send(REL, 0)
    small_step(1)
    tick(QKV + 1)
    for s in range(2, steps):
        small_step(s)
    tick(QKV + 2)

    line = lax.broadcasted_iota(jnp.int32, (piece, width), 0)
    column = lax.broadcasted_iota(jnp.int32, (piece, width), 1)
    mine = column == dp * piece + line

    def own_column(row):
        return jnp.sum(jnp.where(mine, row, 0.0), axis=-1, keepdims=True)

    def as_row(values):
        line = lax.broadcasted_iota(jnp.int32, (piece, 128), 0)
        column = lax.broadcasted_iota(jnp.int32, (piece, 128), 1)
        return jnp.sum(jnp.where(line == column, values, 0.0), axis=0, keepdims=True)

    gain_row = jnp.concatenate([small[8 + j : 9 + j, :] for j in range(width // 128)], axis=1)
    gain_ffn_out[...] = as_row(own_column(gain_row))[:, 0:piece]
    bias_piece = head_size // n
    line = lax.broadcasted_iota(jnp.int32, (bias_piece, head_size), 0)
    column = lax.broadcasted_iota(jnp.int32, (bias_piece, head_size), 1)
    for target, begin in ((cbias_out, 0), (pbias_out, 2)):
        for h in range(2):
            row = small[begin + h : begin + h + 1, :]
            values = jnp.sum(
                jnp.where(column == dp * bias_piece + line, row, 0.0), axis=-1, keepdims=True
            )
            across = jnp.sum(jnp.where(column == line, values, 0.0), axis=0, keepdims=True)
            target[h : h + 1, :] = across[:, 0:bias_piece]
    tick(OUT)
    tick(REL)
    unit_upto(QKV + 2, steps - 1)

    own = pl.ds(pl.multiple_of(dp * piece, piece), piece)
    gathered = jnp.zeros((piece, 1), F32)
    for t in range(3):
        at, start, length = region(QKV + t, steps - 1, True)
        product = grads[at, pl.ds(start, length), :] * wqkv[
            own, 256 * t : 256 * (t + 1)
        ].astype(F32)
        gathered = gathered + jnp.sum(product, axis=-1, keepdims=True)
    tiny[0:1, :] = as_row(gathered / own_column(gain_attn[...]))
    for s, peer in enumerate((core_peer, x_peer)):
        copy = remote(tiny, tiny_in.at[s], tiny_send.at[s], tiny_recv.at[s], peer)
        copy.wait()
        tiny[...] = tiny[...] + tiny_in[s]
    gain_attn_out[...] = tiny[0:1, 0:piece]
    drain(REL)

    for copy in outs.values():
        copy.wait()
    out_copy.wait()
    grad_copy.wait()


def hand_on(count, *refs):
    sources, targets, rooms = refs[:count], refs[count : 2 * count], refs[2 * count : 3 * count]
    sem_in, sem_out = refs[3 * count :]
    arrivals, departures = [], []
    for i in range(count):
        parts = 4 if sources[i].shape[0] % 64 == 0 else 1
        size = sources[i].shape[0] // parts
        for k in range(parts):
            here = pl.ds(k * size, size)
            copy = pltpu.make_async_copy(sources[i].at[here], rooms[i].at[here], sem_in.at[i, k])
            copy.start()
            arrivals.append((copy, i, k, here))
    for copy, i, k, here in arrivals:
        copy.wait()
        copy = pltpu.make_async_copy(rooms[i].at[here], targets[i].at[here], sem_out.at[i, k])
        copy.start()
        departures.append(copy)
    for copy in departures:
        copy.wait()


def shards(
    n,
    segment,
    memory,
    compressed,
    mem_fill,
    comp_fill,
    gain_attn,
    w_qkv,
    content_bias,
    position_bias,
    w_rel,
    w_out,
    gain_ffn,
    w_up,
    w_down,
    w_comp,
    out_cotangent,
    comp_cotangent,
):
    rows, width = segment.shape[1:]
    keys = 3 * rows
    steps = n.bit_length() - 1
    piece = width // n
    head_size = content_bias.shape[0]
    new_count = comp_cotangent.shape[1]
    pad_count = -(-new_count // 16) * 16
    features, sine, cosine = tables(width, 2 * rows, keys)
    vm, anyw = pl.BlockSpec(memory_space=pltpu.VMEM), pl.BlockSpec(memory_space=pl.ANY)
    smem = pl.BlockSpec(memory_space=pltpu.SMEM)
    dma = pltpu.SemaphoreType.DMA
    plain = pltpu.SemaphoreType.REGULAR
    later_count = LATER_SLOTS * max(steps - 1, 1)
    scratch = [
        pltpu.VMEM((rows, width), BF),
        pltpu.VMEM((rows, width), BF),
        pltpu.VMEM((rows, width), BF),
        pltpu.VMEM((rows, width), BF),
        pltpu.VMEM(w_qkv.shape, BF),
        pltpu.VMEM(w_rel.shape, BF),
        pltpu.VMEM(w_out.shape, BF),
        pltpu.VMEM(w_up.shape, BF),
        pltpu.VMEM(w_down.shape, BF),
        pltpu.VMEM((keys, width + 2 * head_size), BF),
        pltpu.VMEM((rows, width // 2), F32),
        pltpu.VMEM((rows, width // 2), F32),
        pltpu.VMEM((keys, 2 * head_size), BF),
        pltpu.VMEM((2, rows, width + head_size), BF),
        pltpu.VMEM((rows, 2 * head_size), BF),
        pltpu.VMEM((keys, width), BF),
        pltpu.VMEM((2, rows, keys), BF),
        pltpu.VMEM((rows, 2 * head_size), BF),
        pltpu.VMEM((rows, 2), F32),
        pltpu.VMEM((rows, 2 * head_size), BF),
        pltpu.VMEM((rows, 6 * head_size), BF),
        pltpu.VMEM((rows, width), F32),
        pltpu.VMEM((rows, width), F32),
        pltpu.VMEM((pad_count, 256), BF),
        pltpu.VMEM((8, 2 * rows), F32),
        pltpu.VMEM((26, 512, 256), F32),
        pltpu.VMEM((4, rows, 256), F32),
        pltpu.VMEM((2, rows, 256), F32),
        pltpu.VMEM((2, 2, rows, 256), F32),
        pltpu.VMEM((4, rows, 256), F32),
        pltpu.VMEM((16, 128), F32),
        pltpu.VMEM((steps, 16, 128), F32),
        pltpu.VMEM((8, 128), F32),
        pltpu.VMEM((2, 8, 128), F32),
        pltpu.VMEM((FIRST_SLOTS, 512, 256), F32),
        pltpu.VMEM((LATER_SLOTS, 512, 256), F32),
        dma((16,)),
        dma((18,)),
        dma((FIRST_SLOTS,)),
        dma((FIRST_SLOTS,)),
        plain((FIRST_SLOTS,)),
        dma((later_count,)),
        dma((later_count,)),
        plain((later_count,)),
        dma((4,)),
        dma((4,)),
        plain,
        dma((2, 4)),
        dma((2, 4)),
        plain((2,)),
        dma((4,)),
        dma((4,)),
        plain,
        dma((steps,)),
        dma((steps,)),
        dma((2,)),
        dma((2,)),
    ]
    shape = jax.ShapeDtypeStruct
    results = pl.pallas_call(
        functools.partial(kernel, n),
        out_shape=(
            shape((rows, width), BF),
            shape((new_count, 256), BF),
            shape((rows, width), F32),
            shape((1, piece), F32),
            shape((piece, w_qkv.shape[1]), F32),
            shape((2, head_size // n), F32),
            shape((2, head_size // n), F32),
            shape((piece, w_rel.shape[1]), F32),
            shape((piece, w_out.shape[1]), F32),
            shape((1, piece), F32),
            shape((piece, w_up.shape[1]), F32),
            shape((piece, w_down.shape[1]), F32),
            shape((3 * piece, w_comp.shape[1]), F32),
        ),
        in_specs=[smem] * 2 + [vm] * 5 + [anyw] * 13,
        out_specs=(anyw, vm, anyw, vm, anyw, vm, vm, anyw, anyw, vm, anyw, anyw, anyw),
        scratch_shapes=scratch,
        compiler_params=pltpu.CompilerParams(
            collective_id=0, has_side_effects=True, vmem_limit_bytes=63 * 2**20
        ),
    )(
        mem_fill,
        comp_fill,
        gain_attn.reshape(1, width),
        gain_ffn.reshape(1, width),
        content_bias.T,
        position_bias.T,
        comp_cotangent[0],
        segment[0],
        memory[0],
        compressed[0],
        w_qkv,
        w_rel,
        w_out,
        w_up,
        w_down,
        w_comp,
        out_cotangent[0],
        jnp.asarray(features, BF),
        jnp.asarray(sine),
        jnp.asarray(cosine),
    )
    count = len(results)
    results = pl.pallas_call(
        functools.partial(hand_on, count),
        out_shape=tuple(shape(r.shape, r.dtype) for r in results),
        in_specs=[anyw] * count,
        out_specs=(anyw,) * count,
        scratch_shapes=[pltpu.VMEM(r.shape, r.dtype) for r in results] + [dma((count, 4))] * 2,
        compiler_params=pltpu.CompilerParams(vmem_limit_bytes=63 * 2**20),
    )(*results)
    layer, new, grad, gattn, qkv, cbias, pbias, rel, outp, gffn, up, down, comp = results
    return (
        layer[None],
        new[None],
        grad[None],
        gattn.reshape(piece),
        qkv,
        cbias.T,
        pbias.T,
        rel,
        outp,
        gffn.reshape(piece),
        up,
        down,
        comp,
    )


def solution(mesh):
    stream = P("dp", None, None)
    split = P(None, "head")
    return jax.shard_map(
        functools.partial(shards, mesh.shape["dp"]),
        mesh=mesh,
        in_specs=(
            stream,
            stream,
            stream,
            P("dp"),
            P("dp"),
            P(),
            split,
            split,
            split,
            split,
            split,
            P(),
            split,
            split,
            split,
            stream,
            P("dp", None, "head"),
        ),
        out_specs=(
            stream,
            P("dp", None, "head"),
            stream,
            P("dp"),
            P("dp", "head"),
            P("dp", "head"),
            P("dp", "head"),
            P("dp", "head"),
            P("dp", "head"),
            P("dp"),
            P("dp", "head"),
            P("dp", "head"),
            P("dp", "head"),
        ),
        check_vma=False,
    )
```

```python
import functools

import jax
import jax.numpy as jnp
import numpy as np
from jax import lax
from jax.experimental import pallas as pl
from jax.experimental.pallas import tpu as pltpu
from jax.sharding import PartitionSpec as P

MESH = pl.DeviceIdType.MESH
BF = jnp.bfloat16
F32 = jnp.float32
EPS = 1e-05
MASKED = -1e30
NN = (((1,), (0,)), ((), ()))
NT = (((1,), (1,)), ((), ()))
TN = (((0,), (0,)), ((), ()))
FIRST_SLOTS = 8
BLOCKS = 4
LATER_SLOTS = 4


def dot(a, b, dims=NN):
    return lax.dot_general(a, b, dims, preferred_element_type=F32)


def row_loop(total, chunk, body, unroll=1):
    def step(index, carry):
        body(pl.multiple_of(index * chunk, chunk))
        return carry

    lax.fori_loop(0, total // chunk, step, 0, unroll=unroll)


def tables(width, prior, keys):
    half = width // 2
    frequency = np.exp(-np.log(10000.0) * np.arange(half) / half)
    angles = np.arange(keys)[:, None] * frequency[None, :]
    sine, cosine = np.sin(angles), np.cos(angles)
    features = np.concatenate([cosine, sine], axis=1).astype(np.float32)
    return features, sine[prior:].astype(np.float32), cosine[prior:].astype(np.float32)


def moments(rows):
    average = jnp.mean(rows, axis=-1, keepdims=True)
    centered = rows - average
    spread = jnp.mean(centered * centered, axis=-1, keepdims=True)
    return centered, lax.rsqrt(spread + EPS)


def norm_back(scaled, xhat, inverse):
    along = jnp.mean(scaled * xhat, axis=-1, keepdims=True)
    return (scaled - jnp.mean(scaled, axis=-1, keepdims=True) - xhat * along) * inverse


def gelu_pair(x):
    c = 0.7978845608028654
    square = x * x
    t = jnp.tanh(c * x * (1.0 + 0.044715 * square))
    half = 0.5 * (1.0 + t)
    slope = half + (0.5 * c) * x * (1.0 - t * t) * (1.0 + 0.134145 * square)
    return x * half, slope


def kernel(
    n,
    mem_fill,
    comp_fill,
    gain_attn,
    gain_ffn,
    content_bias,
    position_bias,
    comp_cot,
    segment,
    memory,
    compressed,
    w_qkv,
    w_rel,
    w_out,
    w_up,
    w_down,
    w_comp,
    cotangent,
    features,
    sine,
    cosine,
    layer_out,
    new_rows,
    input_grad,
    gain_attn_out,
    qkv_out,
    cbias_out,
    pbias_out,
    rel_out,
    outp_out,
    gain_ffn_out,
    up_out,
    down_out,
    comp_out,
    seg_v,
    mem_v,
    cmp_v,
    cot_v,
    wqkv,
    wrel,
    wout,
    wup,
    wdn,
    kf,
    qsin,
    qcos,
    vals,
    rot,
    pin,
    normed,
    probs,
    mix,
    shrink,
    mgrad,
    dseg,
    resid,
    rgrad,
    ccot,
    maskrow,
    grads,
    part,
    part2,
    core_in,
    x_in,
    total,
    small,
    small_in,
    tiny,
    tiny_in,
    first_in,
    later_in,
    in_sem,
    out_sem,
    first_send,
    first_recv,
    first_free,
    later_send,
    later_recv,
    later_free,
    core_send,
    core_recv,
    core_free,
    x_send,
    x_recv,
    x_free,
    back_send,
    back_recv,
    back_free,
    small_send,
    small_recv,
    tiny_send,
    tiny_recv,
):
    steps = n.bit_length() - 1
    width = seg_v.shape[1]
    rows = seg_v.shape[0]
    prior = 2 * rows
    head_size = content_bias.shape[1]
    scale = head_size ** (-0.5)
    piece = width // n
    new_count = comp_cot.shape[0]
    pad_count = ccot.shape[0]

    dp = lax.axis_index("dp")
    head = lax.axis_index("head")
    core = lax.rem(head, 2)
    other = 1 - core
    core_peer = (dp, head + 1 - 2 * core)
    x_peer = (dp, lax.rem(head + 2, 4))
    bits = [lax.rem(dp // (1 << s), 2) for s in range(steps)]
    dp_peers = [(dp + (1 - 2 * bits[s]) * (1 << s), head) for s in range(steps)]

    loads = {}

    def load(name, index, source, target):
        copy = pltpu.make_async_copy(source, target, in_sem.at[index])
        copy.start()
        loads[name] = copy

    def loaded(name):
        loads.pop(name).wait()

    load("memory", 0, memory, mem_v)
    for tap in range(3):
        load(
            f"w_comp{tap}",
            1 + tap,
            w_comp.at[pl.ds(tap * width, width)],
            wup.at[:, pl.ds(256 * tap, 256)],
        )
    load("compressed", 4, compressed, cmp_v)
    load("segment", 5, segment, seg_v)
    load("w_qkv", 6, w_qkv, wqkv)
    load("w_rel", 7, w_rel, wrel)
    load("sine", 8, sine, qsin)
    load("cosine", 9, cosine, qcos)
    load("features", 10, features, kf.at[:, pl.ds(head_size, width)])

    barrier = pltpu.get_barrier_semaphore()
    greeted = [core_peer, x_peer] + dp_peers
    for peer in greeted:
        pl.semaphore_signal(barrier, inc=1, device_id=peer, device_id_type=MESH)

    def remote(source, target, send, recv, peer):
        copy = pltpu.make_async_remote_copy(
            src_ref=source,
            dst_ref=target,
            send_sem=send,
            recv_sem=recv,
            device_id=peer,
            device_id_type=MESH,
        )
        copy.start()
        return copy

    low_first = list(range(steps))
    second_first = [1, 0] + low_first[2:]
    units = []
    for t in range(3):
        units.append((t, low_first, comp_out.at[pl.ds(t * piece, piece), :]))
    for t in range(3):
        units.append((3 + t, low_first, down_out.at[:, pl.ds(256 * t, 256)]))
    for t in range(3):
        units.append((7 + t, low_first, up_out.at[:, pl.ds(256 * t, 256)]))
    for t in range(3):
        units.append((t, low_first, qkv_out.at[:, pl.ds(256 * t, 256)]))
    units.append((10, low_first, up_out.at[:, pl.ds(768, 256)]))
    units.append((6, second_first, down_out.at[:, pl.ds(768, 256)]))
    units.append((12, second_first, rel_out.at[...]))
    units.append((11, second_first, outp_out.at[...]))
    COMP, DOWN, UP, QKV, REL, OUT = 0, (3, 4, 5, 13), (6, 7, 8, 12), 9, 14, 15
    RING = 13
    outs = {}
    sends = {}
    done = set()

    def place(order, j):
        found = 0
        for bit in order:
            found = 2 * found + ((j >> bit) & 1)
        return found

    def store_rows(unit, j, value, lanes=slice(None)):
        at, order, _ = units[unit]
        row = place(order, j) * piece
        grads[2 * at + row // 512, pl.ds(row % 512, piece), lanes] = value

    def store_unit(unit, value, lanes=slice(None)):
        for j in range(n):
            store_rows(unit, j, value[piece * j : piece * (j + 1)], lanes)

    def region(unit, step, mine):
        at, order, _ = units[unit]
        first = bits[order[0]]
        if step == 0:
            return 2 * at + (first if mine else 1 - first), 0, 512
        start = 0
        for s in range(1, step):
            start = start + bits[order[s]] * (width >> (s + 1))
        length = width >> (step + 1)
        mybit = bits[order[step]]
        start = start + (mybit if mine else 1 - mybit) * length
        return 2 * at + first, pl.multiple_of(start, length), length

    def slot_refs(unit, step):
        ring = slots(step)
        slot = unit % ring if unit < RING else ring + (unit == REL)
        if step == 0:
            return first_in.at[slot], first_send.at[slot], first_recv.at[slot], first_free.at[slot]
        index = (step - 1) * (LATER_SLOTS + 2) + slot
        length = width >> (step + 1)
        begin = 512 - (512 >> (step - 1))
        return (
            later_in.at[slot, pl.ds(begin, length), :],
            later_send.at[index],
            later_recv.at[index],
            later_free.at[index],
        )

    def slots(step):
        return LATER_SLOTS if step else FIRST_SLOTS

    def unit_send(unit, step):
        target, send, recv, free = slot_refs(unit, step)
        before = DOWN[3] if unit == OUT else unit - slots(step)
        if before >= 0 and (unit < RING or unit == OUT):
            assert (before, "done") in done or (before >= RING and (before, step) in done)
            pl.semaphore_wait(free, 1)
        at, start, length = region(unit, step, False)
        peer = dp_peers[units[unit][1][step]]
        sends[unit, step] = remote(grads.at[at, pl.ds(start, length), :], target, send, recv, peer)

    def unit_step(unit, step):
        if (unit, step) in done:
            return
        done.add((unit, step))
        target, _, _, free = slot_refs(unit, step)
        sends[unit, step].wait_recv()
        at, start, length = region(unit, step, True)
        chunk = min(64, length)

        def add(offset):
            here = pl.ds(pl.multiple_of(start + offset, chunk), chunk)
            grads[at, here, :] = grads[at, here, :] + target[pl.ds(offset, chunk), :]

        row_loop(length, chunk, add)
        if unit >= RING:
            sends.pop((unit, step)).wait_send()
        later = OUT if unit == DOWN[3] else unit + slots(step)
        if unit == DOWN[3] or later < RING:
            peer = dp_peers[units[later][1][step]]
            pl.semaphore_signal(free, inc=1, device_id=peer, device_id_type=MESH)
        if step + 1 < steps:
            unit_send(unit, step + 1)
        else:
            for s in range(steps):
                if (unit, s) in sends:
                    sends.pop((unit, s)).wait_send()
            copy = pltpu.make_async_copy(
                grads.at[at, pl.ds(start, length), :], units[unit][2], out_sem.at[unit]
            )
            copy.start()
            outs[unit] = copy
            done.add((unit, "done"))

    lags = [0, 1, 3] if steps == 3 else [0] * steps

    def tick(unit):
        for step in range(steps):
            if unit >= lags[step]:
                unit_step(unit - lags[step], step)

    def unit_upto(unit, last):
        for step in range(last + 1):
            unit_step(unit, step)

    moves = {}
    subs = 4
    sub_rows = rows // subs

    def span(sub):
        return pl.ds(sub * sub_rows, sub_rows)

    def sum_source(k):
        return part2 if k == 2 else part

    def sum_start(k, sub):
        if k >= 1 and sub == 0:
            pl.semaphore_wait(core_free, 1)
        ref = sum_source(k)
        moves[k, "core", sub] = remote(
            ref.at[pl.ds(2 * other, 2), span(sub), :],
            core_in.at[:, span(sub), :],
            core_send.at[sub],
            core_recv.at[sub],
            core_peer,
        )

    def sum_across(k, sub):
        ref = sum_source(k)
        moves[k, "core", sub].wait()
        for i in range(2):
            at = 2 * core + i
            ref[at, span(sub), :] = ref[at, span(sub), :] + core_in[i, span(sub), :]
        if sub == subs - 1 and k < 3:
            pl.semaphore_signal(core_free, inc=1, device_id=core_peer, device_id_type=MESH)
        if k >= 2 and sub == 0:
            pl.semaphore_wait(x_free.at[k % 2], 1)
        moves[k, "x", sub] = remote(
            ref.at[pl.ds(2 * core, 2), span(sub), :],
            x_in.at[k % 2, :, span(sub), :],
            x_send.at[k % 2, sub],
            x_recv.at[k % 2, sub],
            x_peer,
        )

    def sum_back(k, sub):
        ref = sum_source(k)
        moves[k, "x", sub].wait_recv()
        for i in range(2):
            total[2 * core + i, span(sub), :] = (
                ref[2 * core + i, span(sub), :] + x_in[k % 2, i, span(sub), :]
            )
        if sub == subs - 1 and k < 2:
            pl.semaphore_signal(x_free.at[k % 2], inc=1, device_id=x_peer, device_id_type=MESH)
        if k >= 1 and sub == 0:
            pl.semaphore_wait(back_free, 1)
        here = total.at[pl.ds(2 * core, 2), span(sub), :]
        moves[k, "back", sub] = remote(here, here, back_send.at[sub], back_recv.at[sub], core_peer)

    def sum_done(k, sub):
        moves[k, "back", sub].wait_recv()

    def sum_used(k):
        for sub in range(subs):
            moves[k, "x", sub].wait_send()
            moves[k, "back", sub].wait_send()
        if k < 3:
            pl.semaphore_signal(back_free, inc=1, device_id=core_peer, device_id_type=MESH)

    def total_rows(here):
        return jnp.concatenate([total[t, here, :] for t in range(4)], axis=1)

    ccot[...] = jnp.zeros_like(ccot)
    ccot[0:new_count, :] = comp_cot[...]
    loaded("memory")
    fill = mem_fill[0]
    compressed_rows = jnp.zeros((pad_count, 256), F32)
    row_at = lax.broadcasted_iota(jnp.int32, (pad_count, rows), 0)
    slot_at = lax.broadcasted_iota(jnp.int32, (pad_count, rows), 1)
    for tap in range(3):
        pick = (slot_at == 3 * row_at + tap) & (slot_at >= rows - fill) & (row_at < new_count)
        window = dot(jnp.where(pick, 1.0, 0.0).astype(BF), mem_v[...]).astype(BF)
        loaded(f"w_comp{tap}")
        compressed_rows = compressed_rows + dot(window, wup[:, pl.ds(256 * tap, 256)])
        tap_grad = dot(window, ccot[...], TN)
        for i in range(n):
            j, t = divmod(n * tap + i, 3)
            store_rows(COMP + t, j, tap_grad[piece * i : piece * (i + 1)])
    new_rows[...] = compressed_rows[0:new_count].astype(BF)
    pl.semaphore_wait(barrier, len(greeted))
    for t in range(3):
        unit_send(COMP + t, 0)
    load("w_up", 1, w_up, wup)

    lane = lax.broadcasted_iota(jnp.int32, (1, rows), 1)
    maskrow[0:1, 0:rows] = jnp.where(lane >= rows - comp_fill[0], 0.0, MASKED)
    maskrow[0:1, rows:prior] = jnp.where(lane >= rows - fill, 0.0, MASKED)

    def norm_into(source, base):
        def body(offset):
            centered, inverse = moments(source[pl.ds(offset, 64), :].astype(F32))
            normed[pl.ds(pl.multiple_of(base + offset, 64), 64), :] = (
                centered * inverse * gain_attn[...]
            ).astype(BF)

        row_loop(rows, 64, body)

    loaded("compressed")
    norm_into(cmp_v, 0)
    norm_into(mem_v, rows)
    loaded("segment")
    norm_into(seg_v, prior)

    load("w_out", 11, w_out, wout)
    load("cotangent", 12, cotangent, cot_v)
    load("w_down", 13, w_down, wdn)
    loaded("w_qkv")
    loaded("features")
    dh = head_size
    key_lane = (0, dh + width)
    pair_lane = (0, dh)
    place_lane = (dh, 0)
    query_lane = (0, width)
    for block in range(2):
        here = pl.ds(block * rows, rows)
        for h in range(2):
            both = dot(normed[here, :], wqkv[:, 3 * dh * h + dh : 3 * dh * (h + 1)])
            kf[here, key_lane[h] : key_lane[h] + dh] = both[:, 0:dh].astype(BF)
            vals[here, dh * h : dh * (h + 1)] = both[:, dh:].astype(BF)
    here = pl.ds(prior, rows)
    queries = [None, None]
    three = [dot(normed[here, :], wqkv[:, 256 * t : 256 * (t + 1)]) for t in range(3)]
    queries[0] = three[0][:, 0:dh]
    kf[here, key_lane[0] : key_lane[0] + dh] = three[0][:, dh:].astype(BF)
    vals[here, 0:dh] = three[1][:, 0:dh].astype(BF)
    queries[1] = three[1][:, dh:]
    kf[here, key_lane[1] : key_lane[1] + dh] = three[2][:, 0:dh].astype(BF)
    vals[here, dh : 2 * dh] = three[2][:, dh:].astype(BF)
    for h in range(2):
        rot[h, :, query_lane[h] : query_lane[h] + dh] = (
            queries[h] + content_bias[h : h + 1, :]
        ).astype(BF)
        pin[:, dh * h : dh * (h + 1)] = (queries[h] + position_bias[h : h + 1, :]).astype(BF)

    loaded("w_rel")
    loaded("sine")
    loaded("cosine")
    half = width // 2
    for h in range(2):
        for j in range(2):
            cols = slice(256 * j, 256 * (j + 1))
            weights = wrel[256 * j : 256 * (j + 1), dh * h : dh * (h + 1)]
            upper = dot(pin[:, dh * h : dh * (h + 1)], weights, NT)
            weights = wrel[half + 256 * j : half + 256 * (j + 1), dh * h : dh * (h + 1)]
            lower = dot(pin[:, dh * h : dh * (h + 1)], weights, NT)
            begin = place_lane[h] + 256 * j
            rot[h, :, begin : begin + 256] = (
                upper * qsin[:, cols] + lower * qcos[:, cols]
            ).astype(BF)
            rot[h, :, begin + half : begin + half + 256] = (
                lower * qsin[:, cols] - upper * qcos[:, cols]
            ).astype(BF)

    block_rows = rows // BLOCKS
    exponent_scale = scale * 1.4426950408889634
    probs[:, 0 : rows // 2, prior + 256 : prior + 512] = jnp.zeros((2, rows // 2, 256), BF)
    line = lax.broadcasted_iota(jnp.int32, (block_rows, 256), 0)
    column = lax.broadcasted_iota(jnp.int32, (block_rows, 256), 1)
    for block in range(BLOCKS):
        base = block * block_rows
        here = pl.ds(base, block_rows)
        tiles = 5 + base // 256
        for h in range(2):
            top = None
            for t in range(tiles):
                keys = slice(256 * t, 256 * (t + 1))
                s = dot(rot[h, here, :], kf[keys, pair_lane[h] : pair_lane[h] + dh + width], NT)
                s = s * exponent_scale
                if t < 4:
                    s = s + maskrow[0:1, keys]
                if t == tiles - 1:
                    s = jnp.where(column <= line + base % 256, s, MASKED)
                grads[6 + t, 256 * h : 256 * h + block_rows, :] = s
                wide = jnp.maximum(s[:, 0:128], s[:, 128:256])
                top = wide if top is None else jnp.maximum(top, wide)
            top = jnp.max(top, axis=-1, keepdims=True)
            whole = None
            for t in range(tiles):
                raised = jnp.exp2(grads[6 + t, 256 * h : 256 * h + block_rows, :] - top)
                probs[h, here, 256 * t : 256 * (t + 1)] = raised.astype(BF)
                wide = raised[:, 0:128] + raised[:, 128:256]
                whole = wide if whole is None else whole + wide
            inverse = 1.0 / jnp.sum(whole, axis=-1, keepdims=True)
            shrink[here, h : h + 1] = inverse
            if block and h == 0:
                for sub in waiting:
                    sum_across(0, sub)
            lanes = slice(dh * h, dh * (h + 1))
            mix[here, lanes] = (
                dot(probs[h, here, 0 : 256 * tiles], vals[0 : 256 * tiles, lanes]) * inverse
            ).astype(BF)
        if block == 0:
            loaded("w_out")
        for t in range(4):
            part[t, here, :] = dot(mix[here, :], wout[256 * t : 256 * (t + 1), :], NT)
        new_subs = range(block * subs // BLOCKS, (block + 1) * subs // BLOCKS)
        for sub in new_subs:
            sum_start(0, sub)
        waiting = list(new_subs)

    loaded("cotangent")
    loaded("w_down")
    for t in range(4):
        cols = pl.ds(256 * t, 256)
        rgrad[:, cols] = dot(cot_v[...], wdn[:, cols])
        if t == 1:
            for sub in waiting:
                sum_across(0, sub)
    tick(COMP)

    nf, act = mem_v, cmp_v
    for sub in range(subs):
        sum_back(0, sub)
        if sub == 2:
            tick(COMP + 1)
        sum_done(0, sub)

        def residual_rows(offset, sub=sub):
            here = pl.ds(pl.multiple_of(sub * sub_rows + offset, 64), 64)
            value = seg_v[here, :].astype(F32) + total_rows(here)
            resid[here, :] = value
            centered, inverse = moments(value)
            nf[here, :] = (centered * inverse * gain_ffn[...]).astype(BF)

        row_loop(sub_rows, 64, residual_rows)
    sum_used(0)

    loaded("w_up")
    hidden_lane = place_lane[0]
    for t in (0, 3, 1, 2):
        cols = slice(256 * t, 256 * (t + 1))
        value, slope = gelu_pair(dot(nf[...], wup[:, cols]))
        act[:, cols] = value.astype(BF)
        rot[0, :, hidden_lane + 256 * t : hidden_lane + 256 * (t + 1)] = (
            rgrad[:, cols] * slope
        ).astype(BF)
        store_unit(DOWN[t], dot(cot_v[...], act[:, cols], TN))
        unit_send(DOWN[t], 0)

    def hidden_grad():
        return rot[0, :, hidden_lane : hidden_lane + width]

    for which in (other, core):
        for i in range(2):
            lines = pl.ds(pl.multiple_of(512 * which + 256 * i, 256), 256)
            part[2 * which + i] = dot(hidden_grad(), wup[lines, :], NT)
        if which is other:
            for sub in range(subs):
                sum_start(1, sub)
    for sub in range(subs):
        sum_across(1, sub)
    for t in range(4):
        cols = slice(hidden_lane + 256 * t, hidden_lane + 256 * (t + 1))
        store_unit(UP[t], dot(nf[...], rot[0, :, cols], TN))
        if t == 0:
            tick(COMP + 2)
        if t < 2:
            unit_send(UP[t], 0)
    for t in range(4):
        part2[t] = dot(act[...], wdn[256 * t : 256 * (t + 1), :], NT)
    for sub in range(subs):
        sum_start(2, sub)

    agrad = mem_v
    small[...] = jnp.zeros_like(small)
    for sub in range(subs):
        sum_back(1, sub)
        if sub == 0:
            unit_step(DOWN[3], 0)
        if sub in (1, 3):
            tick(DOWN[sub // 2])
        if sub == 1:
            unit_upto(COMP, steps - 1)
            unit_send(UP[2], 0)
        sum_done(1, sub)

        def residual_back(offset, carry, sub=sub):
            here = pl.ds(pl.multiple_of(sub * sub_rows + offset * 64, 64), 64)
            grad = total_rows(here)
            centered, inverse = moments(resid[here, :])
            xhat = centered * inverse
            back = norm_back(grad * gain_ffn[...], xhat, inverse)
            value = cot_v[here, :].astype(F32) + back
            rgrad[here, :] = value
            agrad[here, :] = value.astype(BF)
            return carry + jnp.sum(grad * xhat, axis=0, keepdims=True)

        gain_part = lax.fori_loop(
            0, sub_rows // 64, residual_back, jnp.zeros((1, width), F32)
        )
        for j in range(width // 128):
            line = slice(8 + j, 9 + j)
            small[line, :] = small[line, :] + gain_part[:, 128 * j : 128 * (j + 1)]
    sum_used(1)
    for sub in range(subs):
        sum_across(2, sub)
    store_unit(OUT, dot(agrad[...], mix[...], TN))
    unit_send(OUT, 0)

    for h in range(2):
        lanes = slice(dh * h, dh * (h + 1))
        mgrad[:, lanes] = (dot(agrad[...], wout[:, lanes]) * shrink[:, h : h + 1]).astype(BF)
    for h in range(2):
        wup[:, 3 * dh * h : 3 * dh * h + dh] = jnp.zeros((prior, dh), BF)
    for h in range(2):
        lanes = slice(dh * h, dh * (h + 1))
        col = 3 * dh * h
        mg = mgrad[:, lanes]
        delta = jnp.sum(mg.astype(F32) * mix[:, lanes].astype(F32), axis=-1, keepdims=True)

        def key_tile(t, target, lines, ds_rows, ds_cols, h=h, lanes=lanes, col=col, mg=mg, delta=delta):
            keys = pl.ds(pl.multiple_of(t * 256, 256), 256)
            p = probs[h, :, keys]
            dp_tile = dot(mg, vals[keys, lanes], NT)
            ds = (p.astype(F32) * (dp_tile - delta)).astype(BF)
            wdn[ds_rows, ds_cols] = ds
            cq = rot[h, :, query_lane[h] : query_lane[h] + dh]
            target[lines, col + dh : col + 2 * dh] = (dot(ds, cq, TN) * scale).astype(BF)
            target[lines, col + 2 * dh : col + 3 * dh] = dot(p, mg, TN).astype(BF)

        def prior_tile(t, carry):
            at = pl.ds(pl.multiple_of(t * 256, 256), 256)
            key_tile(t, wup, at, slice(0, rows), at)
            return carry

        lax.fori_loop(0, 4, prior_tile, 0)
        for t in range(2):
            at = slice(256 * t, 256 * (t + 1))
            key_tile(4 + t, dseg, at, slice(rows, 2 * rows), at)

        def times_keys(cols):
            return (
                dot(wdn[0:rows, :], kf[0:prior, cols])
                + dot(wdn[rows : 2 * rows, 0:rows], kf[prior : prior + rows, cols])
            ) * scale

        for j in range(2):
            cols = slice(256 * j, 256 * (j + 1))
            upper = times_keys(slice(dh + 256 * j, dh + 256 * (j + 1)))
            lower = times_keys(slice(dh + half + 256 * j, dh + half + 256 * (j + 1)))
            begin = place_lane[h] + 256 * j
            rot[h, :, begin : begin + 256] = (
                upper * qsin[:, cols] - lower * qcos[:, cols]
            ).astype(BF)
            rot[h, :, begin + half : begin + half + 256] = (
                upper * qcos[:, cols] + lower * qsin[:, cols]
            ).astype(BF)
        content = times_keys(slice(key_lane[h], key_lane[h] + dh))
        position = dot(rot[h, :, place_lane[h] : place_lane[h] + width], wrel[:, lanes])
        dseg[:, col : col + dh] = (content + position).astype(BF)
        small[h : h + 1, :] = jnp.sum(content, axis=0, keepdims=True)
        small[2 + h : 3 + h, :] = jnp.sum(position, axis=0, keepdims=True)
        if h == 0:
            tick(DOWN[2])

    stage = cmp_v
    for which in (other, core):
        for i in range(2):
            lines = pl.ds(pl.multiple_of(512 * which + 256 * i, 256), 256)
            part[2 * which + i] = dot(dseg[...], wqkv[lines, :], NT)
        if which is other:
            for sub in range(subs):
                sum_start(3, sub)
    for sub in range(subs):
        sum_across(3, sub)

    def small_start(s):
        moves["small", s] = remote(
            small, small_in.at[s], small_send.at[s], small_recv.at[s], dp_peers[s]
        )

    def small_step(s):
        moves["small", s].wait()
        small[...] = small[...] + small_in[s]
        if s + 1 < steps:
            small_start(s + 1)

    small_start(0)

    tick(UP[0])

    def qkv_unit(t):
        outs.pop(COMP + t).wait()
        cols = slice(256 * t, 256 * (t + 1))
        store_unit(
            QKV + t,
            dot(normed[0:prior, :], wup[:, cols], TN) + dot(normed[prior:, :], dseg[:, cols], TN),
        )
        unit_send(QKV + t, 0)

    for h in range(2):
        lanes = slice(dh * h, dh * (h + 1))
        store_unit(
            REL,
            dot(rot[h, :, place_lane[h] : place_lane[h] + width], pin[:, lanes], TN),
            lanes,
        )
    unit_send(REL, 0)
    qkv_unit(0)
    qkv_unit(1)
    tick(UP[1])
    qkv_unit(2)
    unit_step(DOWN[3], 1)

    for sub in range(subs):
        sum_back(2, sub)
    for sub in range(subs):
        sum_done(2, sub)

        def output_rows(offset, sub=sub):
            here = pl.ds(pl.multiple_of(sub * sub_rows + offset, 64), 64)
            stage[here, :] = (resid[here, :] + total_rows(here)).astype(BF)

        row_loop(sub_rows, 64, output_rows)
    sum_used(2)
    out_copy = pltpu.make_async_copy(stage, layer_out, out_sem.at[16])
    out_copy.start()

    for sub in range(subs):
        sum_back(3, sub)
        if sub == 3:
            tick(UP[2])
            unit_send(UP[3], 0)
            unit_step(OUT, 0)
        sum_done(3, sub)

        def input_rows(offset, sub=sub):
            here = pl.ds(pl.multiple_of(sub * sub_rows + offset, 64), 64)
            centered, inverse = moments(seg_v[here, :].astype(F32))
            back = norm_back(total_rows(here) * gain_attn[...], centered * inverse, inverse)
            resid[here, :] = rgrad[here, :] + back

        row_loop(sub_rows, 64, input_rows)
    sum_used(3)
    grad_copy = pltpu.make_async_copy(resid, input_grad, out_sem.at[17])
    grad_copy.start()
    small_step(0)
    tick(QKV)
    unit_step(REL, 0)
    unit_upto(DOWN[3], steps - 1)
    small_step(1)
    tick(QKV + 1)
    for s in range(2, steps):
        small_step(s)

    line = lax.broadcasted_iota(jnp.int32, (piece, width), 0)
    column = lax.broadcasted_iota(jnp.int32, (piece, width), 1)
    mine = column == dp * piece + line

    def own_column(row):
        return jnp.sum(jnp.where(mine, row, 0.0), axis=-1, keepdims=True)

    def as_row(values):
        line = lax.broadcasted_iota(jnp.int32, (piece, 128), 0)
        column = lax.broadcasted_iota(jnp.int32, (piece, 128), 1)
        return jnp.sum(jnp.where(line == column, values, 0.0), axis=0, keepdims=True)

    gain_row = jnp.concatenate([small[8 + j : 9 + j, :] for j in range(width // 128)], axis=1)
    gain_ffn_out[...] = as_row(own_column(gain_row))[:, 0:piece]
    bias_piece = head_size // n
    line = lax.broadcasted_iota(jnp.int32, (bias_piece, head_size), 0)
    column = lax.broadcasted_iota(jnp.int32, (bias_piece, head_size), 1)
    for target, begin in ((cbias_out, 0), (pbias_out, 2)):
        for h in range(2):
            row = small[begin + h : begin + h + 1, :]
            values = jnp.sum(
                jnp.where(column == dp * bias_piece + line, row, 0.0), axis=-1, keepdims=True
            )
            across = jnp.sum(jnp.where(column == line, values, 0.0), axis=0, keepdims=True)
            target[h : h + 1, :] = across[:, 0:bias_piece]
    tick(QKV + 2)
    tick(UP[3])
    unit_upto(QKV + 1, steps - 1)
    unit_upto(UP[3], 1)
    unit_upto(QKV + 2, steps - 1)

    own = pl.ds(pl.multiple_of(dp * piece, piece), piece)
    gathered = jnp.zeros((piece, 1), F32)
    for t in range(3):
        at, start, length = region(QKV + t, steps - 1, True)
        product = grads[at, pl.ds(start, length), :] * wqkv[
            own, 256 * t : 256 * (t + 1)
        ].astype(F32)
        gathered = gathered + jnp.sum(product, axis=-1, keepdims=True)
    tiny[0:1, :] = as_row(gathered / own_column(gain_attn[...]))
    def tiny_start(s, peer):
        return remote(tiny, tiny_in.at[s], tiny_send.at[s], tiny_recv.at[s], peer)

    tiny_move = tiny_start(0, core_peer)
    unit_step(OUT, 1)
    tiny_move.wait()
    tiny[...] = tiny[...] + tiny_in[0]
    tiny_move = tiny_start(1, x_peer)
    unit_step(REL, 1)
    unit_upto(UP[3], steps - 1)
    tiny_move.wait()
    gain_attn_out[...] = (tiny[...] + tiny_in[1])[0:1, 0:piece]
    unit_upto(OUT, steps - 1)
    unit_upto(REL, steps - 1)

    assert not sends
    for copy in outs.values():
        copy.wait()
    out_copy.wait()
    grad_copy.wait()


def hand_on(count, *refs):
    sources, targets, rooms = refs[:count], refs[count : 2 * count], refs[2 * count : 3 * count]
    sem_in, sem_out = refs[3 * count :]
    arrivals, departures = [], []
    for i in range(count):
        parts = 4 if sources[i].shape[0] % 64 == 0 else 1
        size = sources[i].shape[0] // parts
        for k in range(parts):
            here = pl.ds(k * size, size)
            copy = pltpu.make_async_copy(sources[i].at[here], rooms[i].at[here], sem_in.at[i, k])
            copy.start()
            arrivals.append((copy, i, k, here))
    for copy, i, k, here in arrivals:
        copy.wait()
        copy = pltpu.make_async_copy(rooms[i].at[here], targets[i].at[here], sem_out.at[i, k])
        copy.start()
        departures.append(copy)
    for copy in departures:
        copy.wait()


def shards(
    n,
    segment,
    memory,
    compressed,
    mem_fill,
    comp_fill,
    gain_attn,
    w_qkv,
    content_bias,
    position_bias,
    w_rel,
    w_out,
    gain_ffn,
    w_up,
    w_down,
    w_comp,
    out_cotangent,
    comp_cotangent,
):
    rows, width = segment.shape[1:]
    keys = 3 * rows
    steps = n.bit_length() - 1
    piece = width // n
    head_size = content_bias.shape[0]
    new_count = comp_cotangent.shape[1]
    pad_count = -(-new_count // 16) * 16
    features, sine, cosine = tables(width, 2 * rows, keys)
    vm, anyw = pl.BlockSpec(memory_space=pltpu.VMEM), pl.BlockSpec(memory_space=pl.ANY)
    smem = pl.BlockSpec(memory_space=pltpu.SMEM)
    dma = pltpu.SemaphoreType.DMA
    plain = pltpu.SemaphoreType.REGULAR
    later_count = (LATER_SLOTS + 2) * max(steps - 1, 1)
    scratch = [
        pltpu.VMEM((rows, width), BF),
        pltpu.VMEM((rows, width), BF),
        pltpu.VMEM((rows, width), BF),
        pltpu.VMEM((rows, width), BF),
        pltpu.VMEM(w_qkv.shape, BF),
        pltpu.VMEM(w_rel.shape, BF),
        pltpu.VMEM(w_out.shape, BF),
        pltpu.VMEM(w_up.shape, BF),
        pltpu.VMEM(w_down.shape, BF),
        pltpu.VMEM((keys, width + 2 * head_size), BF),
        pltpu.VMEM((rows, width // 2), F32),
        pltpu.VMEM((rows, width // 2), F32),
        pltpu.VMEM((keys, 2 * head_size), BF),
        pltpu.VMEM((2, rows, width + head_size), BF),
        pltpu.VMEM((rows, 2 * head_size), BF),
        pltpu.VMEM((keys, width), BF),
        pltpu.VMEM((2, rows, keys), BF),
        pltpu.VMEM((rows, 2 * head_size), BF),
        pltpu.VMEM((rows, 2), F32),
        pltpu.VMEM((rows, 2 * head_size), BF),
        pltpu.VMEM((rows, 6 * head_size), BF),
        pltpu.VMEM((rows, width), F32),
        pltpu.VMEM((rows, width), F32),
        pltpu.VMEM((pad_count, 256), BF),
        pltpu.VMEM((8, 2 * rows), F32),
        pltpu.VMEM((26, 512, 256), F32),
        pltpu.VMEM((4, rows, 256), F32),
        pltpu.VMEM((4, rows, 256), F32),
        pltpu.VMEM((2, rows, 256), F32),
        pltpu.VMEM((2, 2, rows, 256), F32),
        pltpu.VMEM((4, rows, 256), F32),
        pltpu.VMEM((16, 128), F32),
        pltpu.VMEM((steps, 16, 128), F32),
        pltpu.VMEM((8, 128), F32),
        pltpu.VMEM((2, 8, 128), F32),
        pltpu.VMEM((FIRST_SLOTS + 2, 512, 256), F32),
        pltpu.VMEM((LATER_SLOTS + 2, 512, 256), F32),
        dma((16,)),
        dma((18,)),
        dma((FIRST_SLOTS + 2,)),
        dma((FIRST_SLOTS + 2,)),
        plain((FIRST_SLOTS + 2,)),
        dma((later_count,)),
        dma((later_count,)),
        plain((later_count,)),
        dma((4,)),
        dma((4,)),
        plain,
        dma((2, 4)),
        dma((2, 4)),
        plain((2,)),
        dma((4,)),
        dma((4,)),
        plain,
        dma((steps,)),
        dma((steps,)),
        dma((2,)),
        dma((2,)),
    ]
    shape = jax.ShapeDtypeStruct
    results = pl.pallas_call(
        functools.partial(kernel, n),
        out_shape=(
            shape((rows, width), BF),
            shape((new_count, 256), BF),
            shape((rows, width), F32),
            shape((1, piece), F32),
            shape((piece, w_qkv.shape[1]), F32),
            shape((2, head_size // n), F32),
            shape((2, head_size // n), F32),
            shape((piece, w_rel.shape[1]), F32),
            shape((piece, w_out.shape[1]), F32),
            shape((1, piece), F32),
            shape((piece, w_up.shape[1]), F32),
            shape((piece, w_down.shape[1]), F32),
            shape((3 * piece, w_comp.shape[1]), F32),
        ),
        in_specs=[smem] * 2 + [vm] * 5 + [anyw] * 13,
        out_specs=(anyw, vm, anyw, vm, anyw, vm, vm, anyw, anyw, vm, anyw, anyw, anyw),
        scratch_shapes=scratch,
        compiler_params=pltpu.CompilerParams(
            collective_id=0, has_side_effects=True, vmem_limit_bytes=127 * 2**19
        ),
    )(
        mem_fill,
        comp_fill,
        gain_attn.reshape(1, width),
        gain_ffn.reshape(1, width),
        content_bias.T,
        position_bias.T,
        comp_cotangent[0],
        segment[0],
        memory[0],
        compressed[0],
        w_qkv,
        w_rel,
        w_out,
        w_up,
        w_down,
        w_comp,
        out_cotangent[0],
        jnp.asarray(features, BF),
        jnp.asarray(sine),
        jnp.asarray(cosine),
    )
    count = len(results)
    results = pl.pallas_call(
        functools.partial(hand_on, count),
        out_shape=tuple(shape(r.shape, r.dtype) for r in results),
        in_specs=[anyw] * count,
        out_specs=(anyw,) * count,
        scratch_shapes=[pltpu.VMEM(r.shape, r.dtype) for r in results] + [dma((count, 4))] * 2,
        compiler_params=pltpu.CompilerParams(vmem_limit_bytes=63 * 2**20),
    )(*results)
    layer, new, grad, gattn, qkv, cbias, pbias, rel, outp, gffn, up, down, comp = results
    return (
        layer[None],
        new[None],
        grad[None],
        gattn.reshape(piece),
        qkv,
        cbias.T,
        pbias.T,
        rel,
        outp,
        gffn.reshape(piece),
        up,
        down,
        comp,
    )


def solution(mesh):
    stream = P("dp", None, None)
    split = P(None, "head")
    return jax.shard_map(
        functools.partial(shards, mesh.shape["dp"]),
        mesh=mesh,
        in_specs=(
            stream,
            stream,
            stream,
            P("dp"),
            P("dp"),
            P(),
            split,
            split,
            split,
            split,
            split,
            P(),
            split,
            split,
            split,
            stream,
            P("dp", None, "head"),
        ),
        out_specs=(
            stream,
            P("dp", None, "head"),
            stream,
            P("dp"),
            P("dp", "head"),
            P("dp", "head"),
            P("dp", "head"),
            P("dp", "head"),
            P("dp", "head"),
            P("dp"),
            P("dp", "head"),
            P("dp", "head"),
            P("dp", "head"),
        ),
        check_vma=False,
    )
```

```python
import functools

import jax
import jax.numpy as jnp
import numpy as np
from jax import lax
from jax.experimental import pallas as pl
from jax.experimental.pallas import tpu as pltpu
from jax.sharding import PartitionSpec as P

MESH = pl.DeviceIdType.MESH
BF = jnp.bfloat16
F32 = jnp.float32
EPS = 1e-05
MASKED = -1e30
NN = (((1,), (0,)), ((), ()))
NT = (((1,), (1,)), ((), ()))
TN = (((0,), (0,)), ((), ()))
FIRST_SLOTS = 8
BLOCKS = 4
LATER_SLOTS = 4


def dot(a, b, dims=NN):
    return lax.dot_general(a, b, dims, preferred_element_type=F32)


def row_loop(total, chunk, body, unroll=1):
    def step(index, carry):
        body(pl.multiple_of(index * chunk, chunk))
        return carry

    lax.fori_loop(0, total // chunk, step, 0, unroll=unroll)


def tables(width, prior, keys):
    half = width // 2
    frequency = np.exp(-np.log(10000.0) * np.arange(half) / half)
    angles = np.arange(keys)[:, None] * frequency[None, :]
    sine, cosine = np.sin(angles), np.cos(angles)
    features = np.concatenate([cosine, sine], axis=1).astype(np.float32)
    return features, sine[prior:].astype(np.float32), cosine[prior:].astype(np.float32)


def moments(rows):
    average = jnp.mean(rows, axis=-1, keepdims=True)
    centered = rows - average
    spread = jnp.mean(centered * centered, axis=-1, keepdims=True)
    return centered, lax.rsqrt(spread + EPS)


def norm_back(scaled, xhat, inverse):
    along = jnp.mean(scaled * xhat, axis=-1, keepdims=True)
    return (scaled - jnp.mean(scaled, axis=-1, keepdims=True) - xhat * along) * inverse


def gelu_pair(x):
    c = 0.7978845608028654
    square = x * x
    t = jnp.tanh(c * x * (1.0 + 0.044715 * square))
    half = 0.5 * (1.0 + t)
    slope = half + (0.5 * c) * x * (1.0 - t * t) * (1.0 + 0.134145 * square)
    return x * half, slope


def kernel(
    n,
    mem_fill,
    comp_fill,
    gain_attn,
    gain_ffn,
    content_bias,
    position_bias,
    comp_cot,
    segment,
    memory,
    compressed,
    w_qkv,
    w_rel,
    w_out,
    w_up,
    w_down,
    w_comp,
    cotangent,
    features,
    sine,
    cosine,
    layer_out,
    new_rows,
    input_grad,
    gain_attn_out,
    qkv_out,
    cbias_out,
    pbias_out,
    rel_out,
    outp_out,
    gain_ffn_out,
    up_out,
    down_out,
    comp_out,
    seg_v,
    mem_v,
    cmp_v,
    cot_v,
    wqkv,
    wrel,
    wout,
    wup,
    wdn,
    kf,
    qsin,
    qcos,
    vals,
    rot,
    pin,
    normed,
    probs,
    mix,
    shrink,
    mgrad,
    dseg,
    resid,
    rgrad,
    ccot,
    maskrow,
    grads,
    part,
    part2,
    core_in,
    x_in,
    total,
    small,
    small_in,
    tiny,
    tiny_in,
    first_in,
    later_in,
    in_sem,
    out_sem,
    first_send,
    first_recv,
    first_free,
    later_send,
    later_recv,
    later_free,
    core_send,
    core_recv,
    core_free,
    x_send,
    x_recv,
    x_free,
    back_send,
    back_recv,
    back_free,
    small_send,
    small_recv,
    tiny_send,
    tiny_recv,
):
    steps = n.bit_length() - 1
    width = seg_v.shape[1]
    rows = seg_v.shape[0]
    prior = 2 * rows
    head_size = content_bias.shape[1]
    scale = head_size ** (-0.5)
    piece = width // n
    new_count = comp_cot.shape[0]
    pad_count = ccot.shape[0]

    dp = lax.axis_index("dp")
    head = lax.axis_index("head")
    core = lax.rem(head, 2)
    other = 1 - core
    core_peer = (dp, head + 1 - 2 * core)
    x_peer = (dp, lax.rem(head + 2, 4))
    bits = [lax.rem(dp // (1 << s), 2) for s in range(steps)]
    dp_peers = [(dp + (1 - 2 * bits[s]) * (1 << s), head) for s in range(steps)]

    loads = {}

    def load(name, index, source, target):
        copy = pltpu.make_async_copy(source, target, in_sem.at[index])
        copy.start()
        loads[name] = copy

    def loaded(name):
        loads.pop(name).wait()

    load("memory", 0, memory, mem_v)
    for tap in range(3):
        load(
            f"w_comp{tap}",
            1 + tap,
            w_comp.at[pl.ds(tap * width, width)],
            wup.at[:, pl.ds(256 * tap, 256)],
        )
    load("compressed", 4, compressed, cmp_v)
    load("segment", 5, segment, seg_v)
    load("w_qkv", 6, w_qkv, wqkv)
    load("w_rel", 7, w_rel, wrel)
    load("sine", 8, sine, qsin)
    load("cosine", 9, cosine, qcos)
    load("features", 10, features, kf.at[:, pl.ds(head_size, width)])

    barrier = pltpu.get_barrier_semaphore()
    greeted = [core_peer, x_peer] + dp_peers
    for peer in greeted:
        pl.semaphore_signal(barrier, inc=1, device_id=peer, device_id_type=MESH)

    def remote(source, target, send, recv, peer):
        copy = pltpu.make_async_remote_copy(
            src_ref=source,
            dst_ref=target,
            send_sem=send,
            recv_sem=recv,
            device_id=peer,
            device_id_type=MESH,
        )
        copy.start()
        return copy

    low_first = list(range(steps))
    second_first = [1, 0] + low_first[2:]
    units = []
    for t in range(3):
        units.append((t, low_first, comp_out.at[pl.ds(t * piece, piece), :]))
    for t in range(2):
        units.append((3 + t, low_first, down_out.at[:, pl.ds(256 * t, 256)]))
    for t in range(3):
        units.append((7 + t, low_first, up_out.at[:, pl.ds(256 * t, 256)]))
    for t in range(3):
        units.append((t, low_first, qkv_out.at[:, pl.ds(256 * t, 256)]))
    units.append((12, low_first, rel_out.at[...]))
    units.append((10, low_first, up_out.at[:, pl.ds(768, 256)]))
    units.append((6, second_first, down_out.at[:, pl.ds(768, 256)]))
    units.append((5, second_first, down_out.at[:, pl.ds(512, 256)]))
    units.append((11, second_first, outp_out.at[...]))
    COMP, DOWN, UP, QKV, REL, OUT = 0, (3, 4, 14, 13), (5, 6, 7, 12), 8, 11, 15
    RING = 13
    outs = {}
    sends = {}
    done = set()

    def place(order, j):
        found = 0
        for bit in order:
            found = 2 * found + ((j >> bit) & 1)
        return found

    def store_rows(unit, j, value, lanes=slice(None)):
        at, order, _ = units[unit]
        row = place(order, j) * piece
        grads[2 * at + row // 512, pl.ds(row % 512, piece), lanes] = value

    def store_unit(unit, value, lanes=slice(None)):
        for j in range(n):
            store_rows(unit, j, value[piece * j : piece * (j + 1)], lanes)

    def region(unit, step, mine):
        at, order, _ = units[unit]
        first = bits[order[0]]
        if step == 0:
            return 2 * at + (first if mine else 1 - first), 0, 512
        start = 0
        for s in range(1, step):
            start = start + bits[order[s]] * (width >> (s + 1))
        length = width >> (step + 1)
        mybit = bits[order[step]]
        start = start + (mybit if mine else 1 - mybit) * length
        return 2 * at + first, pl.multiple_of(start, length), length

    def slot_refs(unit, step):
        ring = slots(step)
        slot = unit % ring if unit < RING else ring + (unit == DOWN[2])
        if step == 0:
            return first_in.at[slot], first_send.at[slot], first_recv.at[slot], first_free.at[slot]
        index = (step - 1) * (LATER_SLOTS + 2) + slot
        length = width >> (step + 1)
        begin = 512 - (512 >> (step - 1))
        return (
            later_in.at[slot, pl.ds(begin, length), :],
            later_send.at[index],
            later_recv.at[index],
            later_free.at[index],
        )

    def slots(step):
        return LATER_SLOTS if step else FIRST_SLOTS

    def unit_send(unit, step):
        target, send, recv, free = slot_refs(unit, step)
        before = DOWN[3] if unit == OUT else unit - slots(step)
        if before >= 0 and (unit < RING or unit == OUT):
            assert (before, "done") in done or (before >= RING and (before, step) in done)
            pl.semaphore_wait(free, 1)
        at, start, length = region(unit, step, False)
        peer = dp_peers[units[unit][1][step]]
        sends[unit, step] = remote(grads.at[at, pl.ds(start, length), :], target, send, recv, peer)

    def unit_step(unit, step):
        if (unit, step) in done:
            return
        done.add((unit, step))
        target, _, _, free = slot_refs(unit, step)
        sends[unit, step].wait_recv()
        at, start, length = region(unit, step, True)
        chunk = min(64, length)

        def add(offset):
            here = pl.ds(pl.multiple_of(start + offset, chunk), chunk)
            grads[at, here, :] = grads[at, here, :] + target[pl.ds(offset, chunk), :]

        row_loop(length, chunk, add)
        if unit >= RING:
            sends.pop((unit, step)).wait_send()
        later = OUT if unit == DOWN[3] else unit + slots(step)
        if unit == DOWN[3] or later < RING:
            peer = dp_peers[units[later][1][step]]
            pl.semaphore_signal(free, inc=1, device_id=peer, device_id_type=MESH)
        if step + 1 < steps:
            unit_send(unit, step + 1)
        else:
            for s in range(steps):
                if (unit, s) in sends:
                    sends.pop((unit, s)).wait_send()
            copy = pltpu.make_async_copy(
                grads.at[at, pl.ds(start, length), :], units[unit][2], out_sem.at[unit]
            )
            copy.start()
            outs[unit] = copy
            done.add((unit, "done"))

    lags = [0, 1, 3] if steps == 3 else [0] * steps

    def tick(unit):
        for step in range(steps):
            if unit >= lags[step]:
                unit_step(unit - lags[step], step)

    def unit_upto(unit, last):
        for step in range(last + 1):
            unit_step(unit, step)

    moves = {}
    subs = 4
    sub_rows = rows // subs

    def span(sub):
        return pl.ds(sub * sub_rows, sub_rows)

    def sum_source(k):
        return part2 if k == 2 else part

    def sum_start(k, sub):
        if k >= 1 and sub == 0:
            pl.semaphore_wait(core_free, 1)
        ref = sum_source(k)
        moves[k, "core", sub] = remote(
            ref.at[pl.ds(2 * other, 2), span(sub), :],
            core_in.at[:, span(sub), :],
            core_send.at[sub],
            core_recv.at[sub],
            core_peer,
        )

    def sum_across(k, sub):
        ref = sum_source(k)
        moves[k, "core", sub].wait()
        for i in range(2):
            at = 2 * core + i
            ref[at, span(sub), :] = ref[at, span(sub), :] + core_in[i, span(sub), :]
        if sub == subs - 1 and k < 3:
            pl.semaphore_signal(core_free, inc=1, device_id=core_peer, device_id_type=MESH)
        if k >= 2 and sub == 0:
            pl.semaphore_wait(x_free.at[k % 2], 1)
        moves[k, "x", sub] = remote(
            ref.at[pl.ds(2 * core, 2), span(sub), :],
            x_in.at[k % 2, :, span(sub), :],
            x_send.at[k % 2, sub],
            x_recv.at[k % 2, sub],
            x_peer,
        )

    def sum_back(k, sub):
        ref = sum_source(k)
        moves[k, "x", sub].wait_recv()
        for i in range(2):
            total[2 * core + i, span(sub), :] = (
                ref[2 * core + i, span(sub), :] + x_in[k % 2, i, span(sub), :]
            )
        if sub == subs - 1 and k < 2:
            pl.semaphore_signal(x_free.at[k % 2], inc=1, device_id=x_peer, device_id_type=MESH)
        if k >= 1 and sub == 0:
            pl.semaphore_wait(back_free, 1)
        here = total.at[pl.ds(2 * core, 2), span(sub), :]
        moves[k, "back", sub] = remote(here, here, back_send.at[sub], back_recv.at[sub], core_peer)

    def sum_done(k, sub):
        moves[k, "back", sub].wait_recv()

    def sum_used(k):
        for sub in range(subs):
            moves[k, "x", sub].wait_send()
            moves[k, "back", sub].wait_send()
        if k < 3:
            pl.semaphore_signal(back_free, inc=1, device_id=core_peer, device_id_type=MESH)

    def total_rows(here):
        return jnp.concatenate([total[t, here, :] for t in range(4)], axis=1)

    ccot[...] = jnp.zeros_like(ccot)
    ccot[0:new_count, :] = comp_cot[...]
    loaded("memory")
    fill = mem_fill[0]
    compressed_rows = jnp.zeros((pad_count, 256), F32)
    row_at = lax.broadcasted_iota(jnp.int32, (pad_count, rows), 0)
    slot_at = lax.broadcasted_iota(jnp.int32, (pad_count, rows), 1)
    for tap in range(3):
        pick = (slot_at == 3 * row_at + tap) & (slot_at >= rows - fill) & (row_at < new_count)
        window = dot(jnp.where(pick, 1.0, 0.0).astype(BF), mem_v[...]).astype(BF)
        loaded(f"w_comp{tap}")
        compressed_rows = compressed_rows + dot(window, wup[:, pl.ds(256 * tap, 256)])
        tap_grad = dot(window, ccot[...], TN)
        for i in range(n):
            j, t = divmod(n * tap + i, 3)
            store_rows(COMP + t, j, tap_grad[piece * i : piece * (i + 1)])
    new_rows[...] = compressed_rows[0:new_count].astype(BF)
    pl.semaphore_wait(barrier, len(greeted))
    for t in range(3):
        unit_send(COMP + t, 0)
    load("w_up", 1, w_up, wup)

    lane = lax.broadcasted_iota(jnp.int32, (1, rows), 1)
    maskrow[0:1, 0:rows] = jnp.where(lane >= rows - comp_fill[0], 0.0, MASKED)
    maskrow[0:1, rows:prior] = jnp.where(lane >= rows - fill, 0.0, MASKED)

    def norm_into(source, base):
        def body(offset):
            centered, inverse = moments(source[pl.ds(offset, 64), :].astype(F32))
            normed[pl.ds(pl.multiple_of(base + offset, 64), 64), :] = (
                centered * inverse * gain_attn[...]
            ).astype(BF)

        row_loop(rows, 64, body)

    loaded("compressed")
    norm_into(cmp_v, 0)
    norm_into(mem_v, rows)
    loaded("segment")
    norm_into(seg_v, prior)

    load("w_out", 11, w_out, wout)
    load("cotangent", 12, cotangent, cot_v)
    load("w_down", 13, w_down, wdn)
    loaded("w_qkv")
    loaded("features")
    dh = head_size
    key_lane = (0, dh + width)
    pair_lane = (0, dh)
    place_lane = (dh, 0)
    query_lane = (0, width)
    for block in range(2):
        here = pl.ds(block * rows, rows)
        for h in range(2):
            both = dot(normed[here, :], wqkv[:, 3 * dh * h + dh : 3 * dh * (h + 1)])
            kf[here, key_lane[h] : key_lane[h] + dh] = both[:, 0:dh].astype(BF)
            vals[here, dh * h : dh * (h + 1)] = both[:, dh:].astype(BF)
    here = pl.ds(prior, rows)
    queries = [None, None]
    three = [dot(normed[here, :], wqkv[:, 256 * t : 256 * (t + 1)]) for t in range(3)]
    queries[0] = three[0][:, 0:dh]
    kf[here, key_lane[0] : key_lane[0] + dh] = three[0][:, dh:].astype(BF)
    vals[here, 0:dh] = three[1][:, 0:dh].astype(BF)
    queries[1] = three[1][:, dh:]
    kf[here, key_lane[1] : key_lane[1] + dh] = three[2][:, 0:dh].astype(BF)
    vals[here, dh : 2 * dh] = three[2][:, dh:].astype(BF)
    for h in range(2):
        rot[h, :, query_lane[h] : query_lane[h] + dh] = (
            queries[h] + content_bias[h : h + 1, :]
        ).astype(BF)
        pin[:, dh * h : dh * (h + 1)] = (queries[h] + position_bias[h : h + 1, :]).astype(BF)

    loaded("w_rel")
    loaded("sine")
    loaded("cosine")
    half = width // 2
    for h in range(2):
        for j in range(2):
            cols = slice(256 * j, 256 * (j + 1))
            weights = wrel[256 * j : 256 * (j + 1), dh * h : dh * (h + 1)]
            upper = dot(pin[:, dh * h : dh * (h + 1)], weights, NT)
            weights = wrel[half + 256 * j : half + 256 * (j + 1), dh * h : dh * (h + 1)]
            lower = dot(pin[:, dh * h : dh * (h + 1)], weights, NT)
            begin = place_lane[h] + 256 * j
            rot[h, :, begin : begin + 256] = (
                upper * qsin[:, cols] + lower * qcos[:, cols]
            ).astype(BF)
            rot[h, :, begin + half : begin + half + 256] = (
                lower * qsin[:, cols] - upper * qcos[:, cols]
            ).astype(BF)

    block_rows = rows // BLOCKS
    exponent_scale = scale * 1.4426950408889634
    probs[:, 0 : rows // 2, prior + 256 : prior + 512] = jnp.zeros((2, rows // 2, 256), BF)
    line = lax.broadcasted_iota(jnp.int32, (block_rows, 256), 0)
    column = lax.broadcasted_iota(jnp.int32, (block_rows, 256), 1)
    for block in range(BLOCKS):
        base = block * block_rows
        here = pl.ds(base, block_rows)
        tiles = 5 + base // 256
        for h in range(2):
            top = None
            for t in range(tiles):
                keys = slice(256 * t, 256 * (t + 1))
                s = dot(rot[h, here, :], kf[keys, pair_lane[h] : pair_lane[h] + dh + width], NT)
                s = s * exponent_scale
                if t < 4:
                    s = s + maskrow[0:1, keys]
                if t == tiles - 1:
                    s = jnp.where(column <= line + base % 256, s, MASKED)
                grads[6 + t, 256 * h : 256 * h + block_rows, :] = s
                wide = jnp.maximum(s[:, 0:128], s[:, 128:256])
                top = wide if top is None else jnp.maximum(top, wide)
            top = jnp.max(top, axis=-1, keepdims=True)
            whole = None
            for t in range(tiles):
                raised = jnp.exp2(grads[6 + t, 256 * h : 256 * h + block_rows, :] - top)
                probs[h, here, 256 * t : 256 * (t + 1)] = raised.astype(BF)
                wide = raised[:, 0:128] + raised[:, 128:256]
                whole = wide if whole is None else whole + wide
            inverse = 1.0 / jnp.sum(whole, axis=-1, keepdims=True)
            shrink[here, h : h + 1] = inverse
            if block and h == 0:
                for sub in waiting:
                    sum_across(0, sub)
            lanes = slice(dh * h, dh * (h + 1))
            mix[here, lanes] = (
                dot(probs[h, here, 0 : 256 * tiles], vals[0 : 256 * tiles, lanes]) * inverse
            ).astype(BF)
        if block == 0:
            loaded("w_out")
        for t in range(4):
            part[t, here, :] = dot(mix[here, :], wout[256 * t : 256 * (t + 1), :], NT)
        new_subs = range(block * subs // BLOCKS, (block + 1) * subs // BLOCKS)
        for sub in new_subs:
            sum_start(0, sub)
        waiting = list(new_subs)
        if block == BLOCKS - 2:
            unit_step(COMP, 0)

    loaded("cotangent")
    loaded("w_down")
    for t in range(4):
        cols = pl.ds(256 * t, 256)
        rgrad[:, cols] = dot(cot_v[...], wdn[:, cols])
        if t == 1:
            for sub in waiting:
                sum_across(0, sub)

    nf, act = mem_v, cmp_v
    for sub in range(subs):
        sum_back(0, sub)
        if sub in (0, 2):
            unit_step(COMP + sub // 2, 1)
        if sub == 1:
            unit_step(COMP + 1, 0)
        sum_done(0, sub)

        def residual_rows(offset, sub=sub):
            here = pl.ds(pl.multiple_of(sub * sub_rows + offset, 64), 64)
            value = seg_v[here, :].astype(F32) + total_rows(here)
            resid[here, :] = value
            centered, inverse = moments(value)
            nf[here, :] = (centered * inverse * gain_ffn[...]).astype(BF)

        row_loop(sub_rows, 64, residual_rows)
    sum_used(0)

    loaded("w_up")
    hidden_lane = place_lane[0]
    for t in (0, 3, 2, 1):
        cols = slice(256 * t, 256 * (t + 1))
        value, slope = gelu_pair(dot(nf[...], wup[:, cols]))
        act[:, cols] = value.astype(BF)
        rot[0, :, hidden_lane + 256 * t : hidden_lane + 256 * (t + 1)] = (
            rgrad[:, cols] * slope
        ).astype(BF)
        store_unit(DOWN[t], dot(cot_v[...], act[:, cols], TN))
        unit_send(DOWN[t], 0)
        if t == 0:
            unit_step(COMP + 2, 0)

    def hidden_grad():
        return rot[0, :, hidden_lane : hidden_lane + width]

    for which in (other, core):
        for i in range(2):
            lines = pl.ds(pl.multiple_of(512 * which + 256 * i, 256), 256)
            part[2 * which + i] = dot(hidden_grad(), wup[lines, :], NT)
        if which is other:
            for sub in range(subs):
                sum_start(1, sub)
    for sub in range(subs):
        sum_across(1, sub)
    for t in range(4):
        cols = slice(hidden_lane + 256 * t, hidden_lane + 256 * (t + 1))
        store_unit(UP[t], dot(nf[...], rot[0, :, cols], TN))
        if t < 2:
            unit_send(UP[t], 0)
    for t in range(4):
        part2[t] = dot(act[...], wdn[256 * t : 256 * (t + 1), :], NT)
    for sub in range(subs):
        sum_start(2, sub)

    agrad = mem_v
    small[...] = jnp.zeros_like(small)
    for sub in range(subs):
        sum_back(1, sub)
        if sub == 0:
            unit_step(DOWN[3], 0)
        if sub in (1, 3):
            tick(DOWN[sub // 2])
        if sub == 3:
            unit_step(DOWN[2], 0)
        if sub == 1:
            for t in range(1 if max(lags) else 3):
                unit_upto(COMP + t, steps - 1)
            unit_send(UP[2], 0)
        sum_done(1, sub)

        def residual_back(offset, carry, sub=sub):
            here = pl.ds(pl.multiple_of(sub * sub_rows + offset * 64, 64), 64)
            grad = total_rows(here)
            centered, inverse = moments(resid[here, :])
            xhat = centered * inverse
            back = norm_back(grad * gain_ffn[...], xhat, inverse)
            value = cot_v[here, :].astype(F32) + back
            rgrad[here, :] = value
            agrad[here, :] = value.astype(BF)
            return carry + jnp.sum(grad * xhat, axis=0, keepdims=True)

        gain_part = lax.fori_loop(
            0, sub_rows // 64, residual_back, jnp.zeros((1, width), F32)
        )
        for j in range(width // 128):
            line = slice(8 + j, 9 + j)
            small[line, :] = small[line, :] + gain_part[:, 128 * j : 128 * (j + 1)]
    sum_used(1)
    for sub in range(subs):
        sum_across(2, sub)
    store_unit(OUT, dot(agrad[...], mix[...], TN))
    unit_send(OUT, 0)

    for h in range(2):
        lanes = slice(dh * h, dh * (h + 1))
        mgrad[:, lanes] = (dot(agrad[...], wout[:, lanes]) * shrink[:, h : h + 1]).astype(BF)
    for h in range(2):
        wup[:, 3 * dh * h : 3 * dh * h + dh] = jnp.zeros((prior, dh), BF)
    for h in range(2):
        lanes = slice(dh * h, dh * (h + 1))
        col = 3 * dh * h
        mg = mgrad[:, lanes]
        delta = jnp.sum(mg.astype(F32) * mix[:, lanes].astype(F32), axis=-1, keepdims=True)

        def key_tile(t, target, lines, ds_rows, ds_cols, h=h, lanes=lanes, col=col, mg=mg, delta=delta):
            keys = pl.ds(pl.multiple_of(t * 256, 256), 256)
            p = probs[h, :, keys]
            dp_tile = dot(mg, vals[keys, lanes], NT)
            ds = (p.astype(F32) * (dp_tile - delta)).astype(BF)
            wdn[ds_rows, ds_cols] = ds
            cq = rot[h, :, query_lane[h] : query_lane[h] + dh]
            target[lines, col + dh : col + 2 * dh] = (dot(ds, cq, TN) * scale).astype(BF)
            target[lines, col + 2 * dh : col + 3 * dh] = dot(p, mg, TN).astype(BF)

        def prior_tile(t, carry):
            at = pl.ds(pl.multiple_of(t * 256, 256), 256)
            key_tile(t, wup, at, slice(0, rows), at)
            return carry

        lax.fori_loop(0, 4, prior_tile, 0)
        for t in range(2):
            at = slice(256 * t, 256 * (t + 1))
            key_tile(4 + t, dseg, at, slice(rows, 2 * rows), at)

        def times_keys(cols):
            return (
                dot(wdn[0:rows, :], kf[0:prior, cols])
                + dot(wdn[rows : 2 * rows, 0:rows], kf[prior : prior + rows, cols])
            ) * scale

        for j in range(2):
            cols = slice(256 * j, 256 * (j + 1))
            upper = times_keys(slice(dh + 256 * j, dh + 256 * (j + 1)))
            lower = times_keys(slice(dh + half + 256 * j, dh + half + 256 * (j + 1)))
            begin = place_lane[h] + 256 * j
            rot[h, :, begin : begin + 256] = (
                upper * qsin[:, cols] - lower * qcos[:, cols]
            ).astype(BF)
            rot[h, :, begin + half : begin + half + 256] = (
                upper * qcos[:, cols] + lower * qsin[:, cols]
            ).astype(BF)
        content = times_keys(slice(key_lane[h], key_lane[h] + dh))
        position = dot(rot[h, :, place_lane[h] : place_lane[h] + width], wrel[:, lanes])
        dseg[:, col : col + dh] = (content + position).astype(BF)
        small[h : h + 1, :] = jnp.sum(content, axis=0, keepdims=True)
        small[2 + h : 3 + h, :] = jnp.sum(position, axis=0, keepdims=True)
        if h == 0:
            tick(UP[0])

    stage = cmp_v
    for which in (other, core):
        for i in range(2):
            lines = pl.ds(pl.multiple_of(512 * which + 256 * i, 256), 256)
            part[2 * which + i] = dot(dseg[...], wqkv[lines, :], NT)
        if which is other:
            for sub in range(subs):
                sum_start(3, sub)
    for sub in range(subs):
        sum_across(3, sub)

    def small_start(s):
        moves["small", s] = remote(
            small, small_in.at[s], small_send.at[s], small_recv.at[s], dp_peers[s]
        )

    def small_step(s):
        moves["small", s].wait()
        small[...] = small[...] + small_in[s]
        if s + 1 < steps:
            small_start(s + 1)

    small_start(0)

    tick(UP[1])

    def qkv_unit(t):
        outs.pop(COMP + t).wait()
        cols = slice(256 * t, 256 * (t + 1))
        store_unit(
            QKV + t,
            dot(normed[0:prior, :], wup[:, cols], TN) + dot(normed[prior:, :], dseg[:, cols], TN),
        )
        unit_send(QKV + t, 0)

    for h in range(2):
        lanes = slice(dh * h, dh * (h + 1))
        store_unit(
            REL,
            dot(rot[h, :, place_lane[h] : place_lane[h] + width], pin[:, lanes], TN),
            lanes,
        )
    qkv_unit(0)
    qkv_unit(1)
    qkv_unit(2)
    unit_step(DOWN[3], 1)

    for sub in range(subs):
        sum_back(2, sub)
    for sub in range(subs):
        sum_done(2, sub)

        def output_rows(offset, sub=sub):
            here = pl.ds(pl.multiple_of(sub * sub_rows + offset, 64), 64)
            stage[here, :] = (resid[here, :] + total_rows(here)).astype(BF)

        row_loop(sub_rows, 64, output_rows)
    sum_used(2)
    out_copy = pltpu.make_async_copy(stage, layer_out, out_sem.at[16])
    out_copy.start()

    for sub in range(subs):
        sum_back(3, sub)
        if sub == 1:
            tick(UP[2])
        if sub == 3:
            unit_step(DOWN[2], 1)
            unit_send(REL, 0)
            unit_send(UP[3], 0)
            unit_step(OUT, 0)
        sum_done(3, sub)

        def input_rows(offset, sub=sub):
            here = pl.ds(pl.multiple_of(sub * sub_rows + offset, 64), 64)
            centered, inverse = moments(seg_v[here, :].astype(F32))
            back = norm_back(total_rows(here) * gain_attn[...], centered * inverse, inverse)
            resid[here, :] = rgrad[here, :] + back

        row_loop(sub_rows, 64, input_rows)
    sum_used(3)
    grad_copy = pltpu.make_async_copy(resid, input_grad, out_sem.at[17])
    grad_copy.start()
    small_step(0)
    tick(QKV)
    unit_upto(DOWN[3], steps - 1)
    small_step(1)
    tick(QKV + 1)
    tick(QKV + 2)
    unit_upto(DOWN[2], steps - 1)
    for s in range(2, steps):
        small_step(s)

    line = lax.broadcasted_iota(jnp.int32, (piece, width), 0)
    column = lax.broadcasted_iota(jnp.int32, (piece, width), 1)
    mine = column == dp * piece + line

    def own_column(row):
        return jnp.sum(jnp.where(mine, row, 0.0), axis=-1, keepdims=True)

    def as_row(values):
        line = lax.broadcasted_iota(jnp.int32, (piece, 128), 0)
        column = lax.broadcasted_iota(jnp.int32, (piece, 128), 1)
        return jnp.sum(jnp.where(line == column, values, 0.0), axis=0, keepdims=True)

    gain_row = jnp.concatenate([small[8 + j : 9 + j, :] for j in range(width // 128)], axis=1)
    gain_ffn_out[...] = as_row(own_column(gain_row))[:, 0:piece]
    bias_piece = head_size // n
    line = lax.broadcasted_iota(jnp.int32, (bias_piece, head_size), 0)
    column = lax.broadcasted_iota(jnp.int32, (bias_piece, head_size), 1)
    for target, begin in ((cbias_out, 0), (pbias_out, 2)):
        for h in range(2):
            row = small[begin + h : begin + h + 1, :]
            values = jnp.sum(
                jnp.where(column == dp * bias_piece + line, row, 0.0), axis=-1, keepdims=True
            )
            across = jnp.sum(jnp.where(column == line, values, 0.0), axis=0, keepdims=True)
            target[h : h + 1, :] = across[:, 0:bias_piece]
    tick(REL)
    tick(UP[3])
    unit_step(OUT, 1)
    unit_upto(QKV + 1, steps - 1)
    unit_upto(UP[3], 1)
    unit_upto(QKV + 2, steps - 1)

    own = pl.ds(pl.multiple_of(dp * piece, piece), piece)
    gathered = jnp.zeros((piece, 1), F32)
    for t in range(3):
        at, start, length = region(QKV + t, steps - 1, True)
        product = grads[at, pl.ds(start, length), :] * wqkv[
            own, 256 * t : 256 * (t + 1)
        ].astype(F32)
        gathered = gathered + jnp.sum(product, axis=-1, keepdims=True)
    tiny[0:1, :] = as_row(gathered / own_column(gain_attn[...]))

    def tiny_start(s, peer):
        return remote(tiny, tiny_in.at[s], tiny_send.at[s], tiny_recv.at[s], peer)

    tiny_move = tiny_start(0, core_peer)
    unit_upto(OUT, steps - 1)
    tiny_move.wait()
    tiny[...] = tiny[...] + tiny_in[0]
    tiny_move = tiny_start(1, x_peer)
    unit_upto(UP[3], steps - 1)
    unit_upto(REL, steps - 1)
    tiny_move.wait()
    gain_attn_out[...] = (tiny[...] + tiny_in[1])[0:1, 0:piece]

    assert not sends
    for copy in outs.values():
        copy.wait()
    out_copy.wait()
    grad_copy.wait()


def hand_on(count, *refs):
    sources, targets, rooms = refs[:count], refs[count : 2 * count], refs[2 * count : 3 * count]
    sem_in, sem_out = refs[3 * count :]
    arrivals, departures = [], []
    for i in range(count):
        parts = 4 if sources[i].shape[0] % 64 == 0 else 1
        size = sources[i].shape[0] // parts
        for k in range(parts):
            here = pl.ds(k * size, size)
            copy = pltpu.make_async_copy(sources[i].at[here], rooms[i].at[here], sem_in.at[i, k])
            copy.start()
            arrivals.append((copy, i, k, here))
    for copy, i, k, here in arrivals:
        copy.wait()
        copy = pltpu.make_async_copy(rooms[i].at[here], targets[i].at[here], sem_out.at[i, k])
        copy.start()
        departures.append(copy)
    for copy in departures:
        copy.wait()


def shards(
    n,
    segment,
    memory,
    compressed,
    mem_fill,
    comp_fill,
    gain_attn,
    w_qkv,
    content_bias,
    position_bias,
    w_rel,
    w_out,
    gain_ffn,
    w_up,
    w_down,
    w_comp,
    out_cotangent,
    comp_cotangent,
):
    rows, width = segment.shape[1:]
    keys = 3 * rows
    steps = n.bit_length() - 1
    piece = width // n
    head_size = content_bias.shape[0]
    new_count = comp_cotangent.shape[1]
    pad_count = -(-new_count // 16) * 16
    features, sine, cosine = tables(width, 2 * rows, keys)
    vm, anyw = pl.BlockSpec(memory_space=pltpu.VMEM), pl.BlockSpec(memory_space=pl.ANY)
    smem = pl.BlockSpec(memory_space=pltpu.SMEM)
    dma = pltpu.SemaphoreType.DMA
    plain = pltpu.SemaphoreType.REGULAR
    later_count = (LATER_SLOTS + 2) * max(steps - 1, 1)
    scratch = [
        pltpu.VMEM((rows, width), BF),
        pltpu.VMEM((rows, width), BF),
        pltpu.VMEM((rows, width), BF),
        pltpu.VMEM((rows, width), BF),
        pltpu.VMEM(w_qkv.shape, BF),
        pltpu.VMEM(w_rel.shape, BF),
        pltpu.VMEM(w_out.shape, BF),
        pltpu.VMEM(w_up.shape, BF),
        pltpu.VMEM(w_down.shape, BF),
        pltpu.VMEM((keys, width + 2 * head_size), BF),
        pltpu.VMEM((rows, width // 2), F32),
        pltpu.VMEM((rows, width // 2), F32),
        pltpu.VMEM((keys, 2 * head_size), BF),
        pltpu.VMEM((2, rows, width + head_size), BF),
        pltpu.VMEM((rows, 2 * head_size), BF),
        pltpu.VMEM((keys, width), BF),
        pltpu.VMEM((2, rows, keys), BF),
        pltpu.VMEM((rows, 2 * head_size), BF),
        pltpu.VMEM((rows, 2), F32),
        pltpu.VMEM((rows, 2 * head_size), BF),
        pltpu.VMEM((rows, 6 * head_size), BF),
        pltpu.VMEM((rows, width), F32),
        pltpu.VMEM((rows, width), F32),
        pltpu.VMEM((pad_count, 256), BF),
        pltpu.VMEM((8, 2 * rows), F32),
        pltpu.VMEM((26, 512, 256), F32),
        pltpu.VMEM((4, rows, 256), F32),
        pltpu.VMEM((4, rows, 256), F32),
        pltpu.VMEM((2, rows, 256), F32),
        pltpu.VMEM((2, 2, rows, 256), F32),
        pltpu.VMEM((4, rows, 256), F32),
        pltpu.VMEM((16, 128), F32),
        pltpu.VMEM((steps, 16, 128), F32),
        pltpu.VMEM((8, 128), F32),
        pltpu.VMEM((2, 8, 128), F32),
        pltpu.VMEM((FIRST_SLOTS + 2, 512, 256), F32),
        pltpu.VMEM((LATER_SLOTS + 2, 512, 256), F32),
        dma((16,)),
        dma((18,)),
        dma((FIRST_SLOTS + 2,)),
        dma((FIRST_SLOTS + 2,)),
        plain((FIRST_SLOTS + 2,)),
        dma((later_count,)),
        dma((later_count,)),
        plain((later_count,)),
        dma((4,)),
        dma((4,)),
        plain,
        dma((2, 4)),
        dma((2, 4)),
        plain((2,)),
        dma((4,)),
        dma((4,)),
        plain,
        dma((steps,)),
        dma((steps,)),
        dma((2,)),
        dma((2,)),
    ]
    shape = jax.ShapeDtypeStruct
    results = pl.pallas_call(
        functools.partial(kernel, n),
        out_shape=(
            shape((rows, width), BF),
            shape((new_count, 256), BF),
            shape((rows, width), F32),
            shape((1, piece), F32),
            shape((piece, w_qkv.shape[1]), F32),
            shape((2, head_size // n), F32),
            shape((2, head_size // n), F32),
            shape((piece, w_rel.shape[1]), F32),
            shape((piece, w_out.shape[1]), F32),
            shape((1, piece), F32),
            shape((piece, w_up.shape[1]), F32),
            shape((piece, w_down.shape[1]), F32),
            shape((3 * piece, w_comp.shape[1]), F32),
        ),
        in_specs=[smem] * 2 + [vm] * 5 + [anyw] * 13,
        out_specs=(anyw, vm, anyw, vm, anyw, vm, vm, anyw, anyw, vm, anyw, anyw, anyw),
        scratch_shapes=scratch,
        compiler_params=pltpu.CompilerParams(
            collective_id=0, has_side_effects=True, vmem_limit_bytes=127 * 2**19
        ),
    )(
        mem_fill,
        comp_fill,
        gain_attn.reshape(1, width),
        gain_ffn.reshape(1, width),
        content_bias.T,
        position_bias.T,
        comp_cotangent[0],
        segment[0],
        memory[0],
        compressed[0],
        w_qkv,
        w_rel,
        w_out,
        w_up,
        w_down,
        w_comp,
        out_cotangent[0],
        jnp.asarray(features, BF),
        jnp.asarray(sine),
        jnp.asarray(cosine),
    )
    count = len(results)
    results = pl.pallas_call(
        functools.partial(hand_on, count),
        out_shape=tuple(shape(r.shape, r.dtype) for r in results),
        in_specs=[anyw] * count,
        out_specs=(anyw,) * count,
        scratch_shapes=[pltpu.VMEM(r.shape, r.dtype) for r in results] + [dma((count, 4))] * 2,
        compiler_params=pltpu.CompilerParams(vmem_limit_bytes=63 * 2**20),
    )(*results)
    layer, new, grad, gattn, qkv, cbias, pbias, rel, outp, gffn, up, down, comp = results
    return (
        layer[None],
        new[None],
        grad[None],
        gattn.reshape(piece),
        qkv,
        cbias.T,
        pbias.T,
        rel,
        outp,
        gffn.reshape(piece),
        up,
        down,
        comp,
    )


def solution(mesh):
    stream = P("dp", None, None)
    split = P(None, "head")
    return jax.shard_map(
        functools.partial(shards, mesh.shape["dp"]),
        mesh=mesh,
        in_specs=(
            stream,
            stream,
            stream,
            P("dp"),
            P("dp"),
            P(),
            split,
            split,
            split,
            split,
            split,
            P(),
            split,
            split,
            split,
            stream,
            P("dp", None, "head"),
        ),
        out_specs=(
            stream,
            P("dp", None, "head"),
            stream,
            P("dp"),
            P("dp", "head"),
            P("dp", "head"),
            P("dp", "head"),
            P("dp", "head"),
            P("dp", "head"),
            P("dp"),
            P("dp", "head"),
            P("dp", "head"),
            P("dp", "head"),
        ),
        check_vma=False,
    )
```

```python
import functools

import jax
import jax.numpy as jnp
import numpy as np
from jax import lax
from jax.experimental import pallas as pl
from jax.experimental.pallas import tpu as pltpu
from jax.sharding import PartitionSpec as P

MESH = pl.DeviceIdType.MESH
BF = jnp.bfloat16
F32 = jnp.float32
EPS = 1e-05
MASKED = -1e30
NN = (((1,), (0,)), ((), ()))
NT = (((1,), (1,)), ((), ()))
TN = (((0,), (0,)), ((), ()))
FIRST_SLOTS = 8
BLOCKS = 4
LATER_SLOTS = 4


def dot(a, b, dims=NN):
    return lax.dot_general(a, b, dims, preferred_element_type=F32)


def row_loop(total, chunk, body, unroll=1):
    def step(index, carry):
        body(pl.multiple_of(index * chunk, chunk))
        return carry

    lax.fori_loop(0, total // chunk, step, 0, unroll=unroll)


def tables(width, prior, keys):
    half = width // 2
    frequency = np.exp(-np.log(10000.0) * np.arange(half) / half)
    angles = np.arange(keys)[:, None] * frequency[None, :]
    sine, cosine = np.sin(angles), np.cos(angles)
    features = np.concatenate([cosine, sine], axis=1).astype(np.float32)
    return features, sine[prior:].astype(np.float32), cosine[prior:].astype(np.float32)


def moments(rows):
    average = jnp.mean(rows, axis=-1, keepdims=True)
    centered = rows - average
    spread = jnp.mean(centered * centered, axis=-1, keepdims=True)
    return centered, lax.rsqrt(spread + EPS)


def norm_back(scaled, xhat, inverse):
    along = jnp.mean(scaled * xhat, axis=-1, keepdims=True)
    return (scaled - jnp.mean(scaled, axis=-1, keepdims=True) - xhat * along) * inverse


def gelu_pair(x):
    c = 0.7978845608028654
    square = x * x
    t = jnp.tanh(c * x * (1.0 + 0.044715 * square))
    half = 0.5 * (1.0 + t)
    slope = half + (0.5 * c) * x * (1.0 - t * t) * (1.0 + 0.134145 * square)
    return x * half, slope


def kernel(
    n,
    mem_fill,
    comp_fill,
    gain_attn,
    gain_ffn,
    content_bias,
    position_bias,
    comp_cot,
    segment,
    memory,
    compressed,
    w_qkv,
    w_rel,
    w_out,
    w_up,
    w_down,
    w_comp,
    cotangent,
    features,
    sine,
    cosine,
    layer_out,
    new_rows,
    input_grad,
    gain_attn_out,
    qkv_out,
    cbias_out,
    pbias_out,
    rel_out,
    outp_out,
    gain_ffn_out,
    up_out,
    down_out,
    comp_out,
    seg_v,
    mem_v,
    cmp_v,
    cot_v,
    wqkv,
    wrel,
    wout,
    wup,
    wdn,
    kf,
    qsin,
    qcos,
    vals,
    rot,
    pin,
    normed,
    probs,
    mix,
    shrink,
    mgrad,
    dseg,
    resid,
    rgrad,
    ccot,
    maskrow,
    grads,
    part,
    part2,
    core_in,
    x_in,
    total,
    small,
    small_in,
    tiny,
    tiny_in,
    first_in,
    later_in,
    in_sem,
    out_sem,
    first_send,
    first_recv,
    first_free,
    later_send,
    later_recv,
    later_free,
    core_send,
    core_recv,
    core_free,
    x_send,
    x_recv,
    x_free,
    back_send,
    back_recv,
    back_free,
    small_send,
    small_recv,
    tiny_send,
    tiny_recv,
):
    steps = n.bit_length() - 1
    width = seg_v.shape[1]
    rows = seg_v.shape[0]
    prior = 2 * rows
    head_size = content_bias.shape[1]
    scale = head_size ** (-0.5)
    piece = width // n
    new_count = comp_cot.shape[0]
    pad_count = ccot.shape[0]

    dp = lax.axis_index("dp")
    head = lax.axis_index("head")
    core = lax.rem(head, 2)
    other = 1 - core
    core_peer = (dp, head + 1 - 2 * core)
    x_peer = (dp, lax.rem(head + 2, 4))
    bits = [lax.rem(dp // (1 << s), 2) for s in range(steps)]
    dp_peers = [(dp + (1 - 2 * bits[s]) * (1 << s), head) for s in range(steps)]

    loads = {}

    def load(name, index, source, target):
        copy = pltpu.make_async_copy(source, target, in_sem.at[index])
        copy.start()
        loads[name] = copy

    def loaded(name):
        loads.pop(name).wait()

    load("memory", 0, memory, mem_v)
    for tap in range(3):
        load(
            f"w_comp{tap}",
            1 + tap,
            w_comp.at[pl.ds(tap * width, width)],
            wup.at[:, pl.ds(256 * tap, 256)],
        )
    load("compressed", 4, compressed, cmp_v)
    load("segment", 5, segment, seg_v)
    load("w_qkv", 6, w_qkv, wqkv)
    load("w_rel", 7, w_rel, wrel)
    load("sine", 8, sine, qsin)
    load("cosine", 9, cosine, qcos)
    load("features", 10, features, kf.at[:, pl.ds(head_size, width)])

    barrier = pltpu.get_barrier_semaphore()
    greeted = [core_peer, x_peer] + dp_peers
    for peer in greeted:
        pl.semaphore_signal(barrier, inc=1, device_id=peer, device_id_type=MESH)

    def remote(source, target, send, recv, peer):
        copy = pltpu.make_async_remote_copy(
            src_ref=source,
            dst_ref=target,
            send_sem=send,
            recv_sem=recv,
            device_id=peer,
            device_id_type=MESH,
        )
        copy.start()
        return copy

    low_first = list(range(steps))
    second_first = [1, 0] + low_first[2:]
    units = []
    for t in range(3):
        units.append((t, low_first, comp_out.at[pl.ds(t * piece, piece), :]))
    for t in range(2):
        units.append((3 + t, low_first, down_out.at[:, pl.ds(256 * t, 256)]))
    for t in range(3):
        units.append((7 + t, low_first, up_out.at[:, pl.ds(256 * t, 256)]))
    for t in range(3):
        units.append((t, low_first, qkv_out.at[:, pl.ds(256 * t, 256)]))
    units.append((12, low_first, rel_out.at[...]))
    units.append((10, low_first, up_out.at[:, pl.ds(768, 256)]))
    units.append((6, second_first, down_out.at[:, pl.ds(768, 256)]))
    units.append((5, second_first, down_out.at[:, pl.ds(512, 256)]))
    units.append((11, second_first, outp_out.at[...]))
    COMP, DOWN, UP, QKV, REL, OUT = 0, (3, 4, 14, 13), (5, 6, 7, 12), 8, 11, 15
    RING = 13
    outs = {}
    sends = {}
    done = set()

    def place(order, j):
        found = 0
        for bit in order:
            found = 2 * found + ((j >> bit) & 1)
        return found

    def store_rows(unit, j, value, lanes=slice(None)):
        at, order, _ = units[unit]
        row = place(order, j) * piece
        grads[2 * at + row // 512, pl.ds(row % 512, piece), lanes] = value

    def store_unit(unit, value, lanes=slice(None)):
        for j in range(n):
            store_rows(unit, j, value[piece * j : piece * (j + 1)], lanes)

    def region(unit, step, mine):
        at, order, _ = units[unit]
        first = bits[order[0]]
        if step == 0:
            return 2 * at + (first if mine else 1 - first), 0, 512
        start = 0
        for s in range(1, step):
            start = start + bits[order[s]] * (width >> (s + 1))
        length = width >> (step + 1)
        mybit = bits[order[step]]
        start = start + (mybit if mine else 1 - mybit) * length
        return 2 * at + first, pl.multiple_of(start, length), length

    def slot_refs(unit, step):
        ring = slots(step)
        slot = unit % ring if unit < RING else ring + (unit == DOWN[2])
        if step == 0:
            return first_in.at[slot], first_send.at[slot], first_recv.at[slot], first_free.at[slot]
        index = (step - 1) * (LATER_SLOTS + 2) + slot
        length = width >> (step + 1)
        begin = 512 - (512 >> (step - 1))
        return (
            later_in.at[slot, pl.ds(begin, length), :],
            later_send.at[index],
            later_recv.at[index],
            later_free.at[index],
        )

    def slots(step):
        return LATER_SLOTS if step else FIRST_SLOTS

    def unit_send(unit, step):
        target, send, recv, free = slot_refs(unit, step)
        before = DOWN[3] if unit == OUT else unit - slots(step)
        if before >= 0 and (unit < RING or unit == OUT):
            assert (before, "done") in done or (before >= RING and (before, step) in done)
            pl.semaphore_wait(free, 1)
        at, start, length = region(unit, step, False)
        peer = dp_peers[units[unit][1][step]]
        sends[unit, step] = remote(grads.at[at, pl.ds(start, length), :], target, send, recv, peer)

    def unit_step(unit, step):
        if (unit, step) in done:
            return
        done.add((unit, step))
        target, _, _, free = slot_refs(unit, step)
        sends[unit, step].wait_recv()
        at, start, length = region(unit, step, True)
        chunk = min(64, length)

        def add(offset):
            here = pl.ds(pl.multiple_of(start + offset, chunk), chunk)
            grads[at, here, :] = grads[at, here, :] + target[pl.ds(offset, chunk), :]

        row_loop(length, chunk, add)
        if unit >= RING:
            sends.pop((unit, step)).wait_send()
        later = OUT if unit == DOWN[3] else unit + slots(step)
        if unit == DOWN[3] or later < RING:
            peer = dp_peers[units[later][1][step]]
            pl.semaphore_signal(free, inc=1, device_id=peer, device_id_type=MESH)
        if step + 1 < steps:
            unit_send(unit, step + 1)
        else:
            for s in range(steps):
                if (unit, s) in sends:
                    sends.pop((unit, s)).wait_send()
            copy = pltpu.make_async_copy(
                grads.at[at, pl.ds(start, length), :], units[unit][2], out_sem.at[unit]
            )
            copy.start()
            outs[unit] = copy
            done.add((unit, "done"))

    lags = [0, 1, 3] if steps == 3 else [0] * steps

    def tick(unit):
        for step in range(steps):
            if unit >= lags[step]:
                unit_step(unit - lags[step], step)

    def unit_upto(unit, last):
        for step in range(last + 1):
            unit_step(unit, step)

    moves = {}
    subs = 4
    sub_rows = rows // subs

    def span(sub):
        return pl.ds(sub * sub_rows, sub_rows)

    def sum_source(k):
        return part2 if k == 2 else part

    def sum_start(k, sub):
        if k >= 1 and sub == 0:
            pl.semaphore_wait(core_free, 1)
        ref = sum_source(k)
        moves[k, "core", sub] = remote(
            ref.at[pl.ds(2 * other, 2), span(sub), :],
            core_in.at[:, span(sub), :],
            core_send.at[sub],
            core_recv.at[sub],
            core_peer,
        )

    def sum_across(k, sub):
        ref = sum_source(k)
        moves[k, "core", sub].wait()
        for i in range(2):
            at = 2 * core + i
            ref[at, span(sub), :] = ref[at, span(sub), :] + core_in[i, span(sub), :]
        if sub == subs - 1 and k < 3:
            pl.semaphore_signal(core_free, inc=1, device_id=core_peer, device_id_type=MESH)
        if k >= 2 and sub == 0:
            pl.semaphore_wait(x_free.at[k % 2], 1)
        moves[k, "x", sub] = remote(
            ref.at[pl.ds(2 * core, 2), span(sub), :],
            x_in.at[k % 2, :, span(sub), :],
            x_send.at[k % 2, sub],
            x_recv.at[k % 2, sub],
            x_peer,
        )

    def sum_back(k, sub):
        ref = sum_source(k)
        moves[k, "x", sub].wait_recv()
        for i in range(2):
            total[2 * core + i, span(sub), :] = (
                ref[2 * core + i, span(sub), :] + x_in[k % 2, i, span(sub), :]
            )
        if sub == subs - 1 and k < 2:
            pl.semaphore_signal(x_free.at[k % 2], inc=1, device_id=x_peer, device_id_type=MESH)
        if k >= 1 and sub == 0:
            pl.semaphore_wait(back_free, 1)
        here = total.at[pl.ds(2 * core, 2), span(sub), :]
        moves[k, "back", sub] = remote(here, here, back_send.at[sub], back_recv.at[sub], core_peer)

    def sum_done(k, sub):
        moves[k, "back", sub].wait_recv()

    def sum_used(k):
        for sub in range(subs):
            moves[k, "x", sub].wait_send()
            moves[k, "back", sub].wait_send()
        if k < 3:
            pl.semaphore_signal(back_free, inc=1, device_id=core_peer, device_id_type=MESH)

    def total_rows(here):
        return jnp.concatenate([total[t, here, :] for t in range(4)], axis=1)

    ccot[...] = jnp.zeros_like(ccot)
    ccot[0:new_count, :] = comp_cot[...]
    loaded("memory")
    fill = mem_fill[0]
    row_at = lax.broadcasted_iota(jnp.int32, (pad_count, rows), 0)
    slot_at = lax.broadcasted_iota(jnp.int32, (pad_count, rows), 1)
    for tap in range(3):
        pick = (slot_at == 3 * row_at + tap) & (slot_at >= rows - fill) & (row_at < new_count)
        window = dot(jnp.where(pick, 1.0, 0.0).astype(BF), mem_v[...]).astype(BF)
        normed[pad_count * tap : pad_count * (tap + 1), :] = window
        tap_grad = dot(window, ccot[...], TN)
        for i in range(n):
            j, t = divmod(n * tap + i, 3)
            store_rows(COMP + t, j, tap_grad[piece * i : piece * (i + 1)])
    pl.semaphore_wait(barrier, len(greeted))
    for t in range(3):
        unit_send(COMP + t, 0)
    compressed_rows = jnp.zeros((pad_count, 256), F32)
    for tap in range(3):
        loaded(f"w_comp{tap}")
        window = normed[pad_count * tap : pad_count * (tap + 1), :]
        compressed_rows = compressed_rows + dot(window, wup[:, pl.ds(256 * tap, 256)])
    new_rows[...] = compressed_rows[0:new_count].astype(BF)
    load("w_up", 1, w_up, wup)

    lane = lax.broadcasted_iota(jnp.int32, (1, rows), 1)
    maskrow[0:1, 0:rows] = jnp.where(lane >= rows - comp_fill[0], 0.0, MASKED)
    maskrow[0:1, rows:prior] = jnp.where(lane >= rows - fill, 0.0, MASKED)

    def norm_into(source, base):
        def body(offset):
            centered, inverse = moments(source[pl.ds(offset, 64), :].astype(F32))
            normed[pl.ds(pl.multiple_of(base + offset, 64), 64), :] = (
                centered * inverse * gain_attn[...]
            ).astype(BF)

        row_loop(rows, 64, body)

    loaded("compressed")
    norm_into(cmp_v, 0)
    norm_into(mem_v, rows)
    loaded("segment")
    norm_into(seg_v, prior)

    load("w_out", 11, w_out, wout)
    load("cotangent", 12, cotangent, cot_v)
    load("w_down", 13, w_down, wdn)
    loaded("w_qkv")
    loaded("features")
    dh = head_size
    key_lane = (0, dh + width)
    pair_lane = (0, dh)
    place_lane = (dh, 0)
    query_lane = (0, width)
    for block in range(2):
        here = pl.ds(block * rows, rows)
        for h in range(2):
            both = dot(normed[here, :], wqkv[:, 3 * dh * h + dh : 3 * dh * (h + 1)])
            kf[here, key_lane[h] : key_lane[h] + dh] = both[:, 0:dh].astype(BF)
            vals[here, dh * h : dh * (h + 1)] = both[:, dh:].astype(BF)
    here = pl.ds(prior, rows)
    queries = [None, None]
    three = [dot(normed[here, :], wqkv[:, 256 * t : 256 * (t + 1)]) for t in range(3)]
    queries[0] = three[0][:, 0:dh]
    kf[here, key_lane[0] : key_lane[0] + dh] = three[0][:, dh:].astype(BF)
    vals[here, 0:dh] = three[1][:, 0:dh].astype(BF)
    queries[1] = three[1][:, dh:]
    kf[here, key_lane[1] : key_lane[1] + dh] = three[2][:, 0:dh].astype(BF)
    vals[here, dh : 2 * dh] = three[2][:, dh:].astype(BF)
    for h in range(2):
        rot[h, :, query_lane[h] : query_lane[h] + dh] = (
            queries[h] + content_bias[h : h + 1, :]
        ).astype(BF)
        pin[:, dh * h : dh * (h + 1)] = (queries[h] + position_bias[h : h + 1, :]).astype(BF)

    loaded("w_rel")
    loaded("sine")
    loaded("cosine")
    half = width // 2
    for h in range(2):
        for j in range(2):
            cols = slice(256 * j, 256 * (j + 1))
            weights = wrel[256 * j : 256 * (j + 1), dh * h : dh * (h + 1)]
            upper = dot(pin[:, dh * h : dh * (h + 1)], weights, NT)
            weights = wrel[half + 256 * j : half + 256 * (j + 1), dh * h : dh * (h + 1)]
            lower = dot(pin[:, dh * h : dh * (h + 1)], weights, NT)
            begin = place_lane[h] + 256 * j
            rot[h, :, begin : begin + 256] = (
                upper * qsin[:, cols] + lower * qcos[:, cols]
            ).astype(BF)
            rot[h, :, begin + half : begin + half + 256] = (
                lower * qsin[:, cols] - upper * qcos[:, cols]
            ).astype(BF)

    block_rows = rows // BLOCKS
    exponent_scale = scale * 1.4426950408889634
    probs[:, 0 : rows // 2, prior + 256 : prior + 512] = jnp.zeros((2, rows // 2, 256), BF)
    line = lax.broadcasted_iota(jnp.int32, (block_rows, 256), 0)
    column = lax.broadcasted_iota(jnp.int32, (block_rows, 256), 1)
    for block in range(BLOCKS):
        base = block * block_rows
        here = pl.ds(base, block_rows)
        tiles = 5 + base // 256
        for h in range(2):
            top = None
            for t in range(tiles):
                keys = slice(256 * t, 256 * (t + 1))
                s = dot(rot[h, here, :], kf[keys, pair_lane[h] : pair_lane[h] + dh + width], NT)
                s = s * exponent_scale
                if t < 4:
                    s = s + maskrow[0:1, keys]
                if t == tiles - 1:
                    s = jnp.where(column <= line + base % 256, s, MASKED)
                grads[6 + t, 256 * h : 256 * h + block_rows, :] = s
                wide = jnp.maximum(s[:, 0:128], s[:, 128:256])
                top = wide if top is None else jnp.maximum(top, wide)
            top = jnp.max(top, axis=-1, keepdims=True)
            whole = None
            for t in range(tiles):
                raised = jnp.exp2(grads[6 + t, 256 * h : 256 * h + block_rows, :] - top)
                probs[h, here, 256 * t : 256 * (t + 1)] = raised.astype(BF)
                wide = raised[:, 0:128] + raised[:, 128:256]
                whole = wide if whole is None else whole + wide
            inverse = 1.0 / jnp.sum(whole, axis=-1, keepdims=True)
            shrink[here, h : h + 1] = inverse
            if block and h == 0:
                for sub in waiting:
                    sum_across(0, sub)
            lanes = slice(dh * h, dh * (h + 1))
            mix[here, lanes] = (
                dot(probs[h, here, 0 : 256 * tiles], vals[0 : 256 * tiles, lanes]) * inverse
            ).astype(BF)
        if block == 0:
            loaded("w_out")
        for t in range(4):
            part[t, here, :] = dot(mix[here, :], wout[256 * t : 256 * (t + 1), :], NT)
        new_subs = range(block * subs // BLOCKS, (block + 1) * subs // BLOCKS)
        for sub in new_subs:
            sum_start(0, sub)
        waiting = list(new_subs)
        if block == BLOCKS - 2:
            unit_step(COMP, 0)

    loaded("cotangent")
    loaded("w_down")
    for t in range(4):
        cols = pl.ds(256 * t, 256)
        rgrad[:, cols] = dot(cot_v[...], wdn[:, cols])
        if t == 1:
            for sub in waiting:
                sum_across(0, sub)

    nf, act = mem_v, cmp_v
    for sub in range(subs):
        sum_back(0, sub)
        if sub in (0, 2):
            unit_step(COMP + sub // 2, 1)
        if sub == 1:
            unit_step(COMP + 1, 0)
        sum_done(0, sub)

        def residual_rows(offset, sub=sub):
            here = pl.ds(pl.multiple_of(sub * sub_rows + offset, 64), 64)
            value = seg_v[here, :].astype(F32) + total_rows(here)
            resid[here, :] = value
            centered, inverse = moments(value)
            nf[here, :] = (centered * inverse * gain_ffn[...]).astype(BF)

        row_loop(sub_rows, 64, residual_rows)
    sum_used(0)

    loaded("w_up")
    hidden_lane = place_lane[0]
    for t in (0, 3, 2, 1):
        cols = slice(256 * t, 256 * (t + 1))
        value, slope = gelu_pair(dot(nf[...], wup[:, cols]))
        act[:, cols] = value.astype(BF)
        rot[0, :, hidden_lane + 256 * t : hidden_lane + 256 * (t + 1)] = (
            rgrad[:, cols] * slope
        ).astype(BF)
        store_unit(DOWN[t], dot(cot_v[...], act[:, cols], TN))
        unit_send(DOWN[t], 0)
        if t == 0:
            unit_step(COMP + 2, 0)

    def hidden_grad():
        return rot[0, :, hidden_lane : hidden_lane + width]

    for which in (other, core):
        for i in range(2):
            lines = pl.ds(pl.multiple_of(512 * which + 256 * i, 256), 256)
            part[2 * which + i] = dot(hidden_grad(), wup[lines, :], NT)
        if which is other:
            for sub in range(subs):
                sum_start(1, sub)
    for sub in range(subs):
        sum_across(1, sub)
    for t in range(4):
        cols = slice(hidden_lane + 256 * t, hidden_lane + 256 * (t + 1))
        store_unit(UP[t], dot(nf[...], rot[0, :, cols], TN))
        if t < 2:
            unit_send(UP[t], 0)
    for t in range(4):
        part2[t] = dot(act[...], wdn[256 * t : 256 * (t + 1), :], NT)
    for sub in range(subs):
        sum_start(2, sub)

    agrad = mem_v
    small[...] = jnp.zeros_like(small)
    for sub in range(subs):
        sum_back(1, sub)
        if sub == 0:
            unit_step(DOWN[3], 0)
        if sub in (1, 3):
            tick(DOWN[sub // 2])
        if sub == 3:
            unit_step(DOWN[2], 0)
        if sub == 1:
            for t in range(1 if max(lags) else 3):
                unit_upto(COMP + t, steps - 1)
            unit_send(UP[2], 0)
        sum_done(1, sub)

        def residual_back(offset, carry, sub=sub):
            here = pl.ds(pl.multiple_of(sub * sub_rows + offset * 64, 64), 64)
            grad = total_rows(here)
            centered, inverse = moments(resid[here, :])
            xhat = centered * inverse
            back = norm_back(grad * gain_ffn[...], xhat, inverse)
            value = cot_v[here, :].astype(F32) + back
            rgrad[here, :] = value
            agrad[here, :] = value.astype(BF)
            return carry + jnp.sum(grad * xhat, axis=0, keepdims=True)

        gain_part = lax.fori_loop(
            0, sub_rows // 64, residual_back, jnp.zeros((1, width), F32)
        )
        for j in range(width // 128):
            line = slice(8 + j, 9 + j)
            small[line, :] = small[line, :] + gain_part[:, 128 * j : 128 * (j + 1)]
    sum_used(1)
    for sub in range(subs):
        sum_across(2, sub)
    store_unit(OUT, dot(agrad[...], mix[...], TN))
    unit_send(OUT, 0)

    for h in range(2):
        lanes = slice(dh * h, dh * (h + 1))
        mgrad[:, lanes] = (dot(agrad[...], wout[:, lanes]) * shrink[:, h : h + 1]).astype(BF)
    for h in range(2):
        wup[:, 3 * dh * h : 3 * dh * h + dh] = jnp.zeros((prior, dh), BF)
    for h in range(2):
        lanes = slice(dh * h, dh * (h + 1))
        col = 3 * dh * h
        mg = mgrad[:, lanes]
        delta = jnp.sum(mg.astype(F32) * mix[:, lanes].astype(F32), axis=-1, keepdims=True)

        def key_tile(t, target, lines, ds_rows, ds_cols, h=h, lanes=lanes, col=col, mg=mg, delta=delta):
            keys = pl.ds(pl.multiple_of(t * 256, 256), 256)
            p = probs[h, :, keys]
            dp_tile = dot(mg, vals[keys, lanes], NT)
            ds = (p.astype(F32) * (dp_tile - delta)).astype(BF)
            wdn[ds_rows, ds_cols] = ds
            cq = rot[h, :, query_lane[h] : query_lane[h] + dh]
            target[lines, col + dh : col + 2 * dh] = (dot(ds, cq, TN) * scale).astype(BF)
            target[lines, col + 2 * dh : col + 3 * dh] = dot(p, mg, TN).astype(BF)

        def prior_tile(t, carry):
            at = pl.ds(pl.multiple_of(t * 256, 256), 256)
            key_tile(t, wup, at, slice(0, rows), at)
            return carry

        lax.fori_loop(0, 4, prior_tile, 0)
        for t in range(2):
            at = slice(256 * t, 256 * (t + 1))
            key_tile(4 + t, dseg, at, slice(rows, 2 * rows), at)

        def times_keys(cols):
            return (
                dot(wdn[0:rows, :], kf[0:prior, cols])
                + dot(wdn[rows : 2 * rows, 0:rows], kf[prior : prior + rows, cols])
            ) * scale

        for j in range(2):
            cols = slice(256 * j, 256 * (j + 1))
            upper = times_keys(slice(dh + 256 * j, dh + 256 * (j + 1)))
            lower = times_keys(slice(dh + half + 256 * j, dh + half + 256 * (j + 1)))
            begin = place_lane[h] + 256 * j
            rot[h, :, begin : begin + 256] = (
                upper * qsin[:, cols] - lower * qcos[:, cols]
            ).astype(BF)
            rot[h, :, begin + half : begin + half + 256] = (
                upper * qcos[:, cols] + lower * qsin[:, cols]
            ).astype(BF)
        content = times_keys(slice(key_lane[h], key_lane[h] + dh))
        position = dot(rot[h, :, place_lane[h] : place_lane[h] + width], wrel[:, lanes])
        dseg[:, col : col + dh] = (content + position).astype(BF)
        small[h : h + 1, :] = jnp.sum(content, axis=0, keepdims=True)
        small[2 + h : 3 + h, :] = jnp.sum(position, axis=0, keepdims=True)
        if h == 0:
            tick(UP[0])

    stage = cmp_v
    for which in (other, core):
        for i in range(2):
            lines = pl.ds(pl.multiple_of(512 * which + 256 * i, 256), 256)
            part[2 * which + i] = dot(dseg[...], wqkv[lines, :], NT)
        if which is other:
            for sub in range(subs):
                sum_start(3, sub)
    for sub in range(subs):
        sum_across(3, sub)

    def small_start(s):
        moves["small", s] = remote(
            small, small_in.at[s], small_send.at[s], small_recv.at[s], dp_peers[s]
        )

    def small_step(s):
        moves["small", s].wait()
        small[...] = small[...] + small_in[s]
        if s + 1 < steps:
            small_start(s + 1)

    small_start(0)

    tick(UP[1])

    def qkv_unit(t):
        outs.pop(COMP + t).wait()
        cols = slice(256 * t, 256 * (t + 1))
        store_unit(
            QKV + t,
            dot(normed[0:prior, :], wup[:, cols], TN) + dot(normed[prior:, :], dseg[:, cols], TN),
        )
        unit_send(QKV + t, 0)

    for h in range(2):
        lanes = slice(dh * h, dh * (h + 1))
        store_unit(
            REL,
            dot(rot[h, :, place_lane[h] : place_lane[h] + width], pin[:, lanes], TN),
            lanes,
        )
    qkv_unit(0)
    qkv_unit(1)
    qkv_unit(2)
    unit_step(DOWN[3], 1)

    for sub in range(subs):
        sum_back(2, sub)
    for sub in range(subs):
        sum_done(2, sub)

        def output_rows(offset, sub=sub):
            here = pl.ds(pl.multiple_of(sub * sub_rows + offset, 64), 64)
            stage[here, :] = (resid[here, :] + total_rows(here)).astype(BF)

        row_loop(sub_rows, 64, output_rows)
    sum_used(2)
    out_copy = pltpu.make_async_copy(stage, layer_out, out_sem.at[16])
    out_copy.start()

    for sub in range(subs):
        sum_back(3, sub)
        if sub == 1:
            tick(UP[2])
        if sub == 3:
            unit_step(DOWN[2], 1)
            unit_send(REL, 0)
            unit_send(UP[3], 0)
            unit_step(OUT, 0)
        sum_done(3, sub)

        def input_rows(offset, sub=sub):
            here = pl.ds(pl.multiple_of(sub * sub_rows + offset, 64), 64)
            centered, inverse = moments(seg_v[here, :].astype(F32))
            back = norm_back(total_rows(here) * gain_attn[...], centered * inverse, inverse)
            resid[here, :] = rgrad[here, :] + back

        row_loop(sub_rows, 64, input_rows)
    sum_used(3)
    grad_copy = pltpu.make_async_copy(resid, input_grad, out_sem.at[17])
    grad_copy.start()
    small_step(0)
    tick(QKV)
    unit_upto(DOWN[3], steps - 1)
    small_step(1)
    tick(QKV + 1)
    tick(QKV + 2)
    unit_upto(DOWN[2], steps - 1)
    for s in range(2, steps):
        small_step(s)

    line = lax.broadcasted_iota(jnp.int32, (piece, width), 0)
    column = lax.broadcasted_iota(jnp.int32, (piece, width), 1)
    mine = column == dp * piece + line

    def own_column(row):
        return jnp.sum(jnp.where(mine, row, 0.0), axis=-1, keepdims=True)

    def as_row(values):
        line = lax.broadcasted_iota(jnp.int32, (piece, 128), 0)
        column = lax.broadcasted_iota(jnp.int32, (piece, 128), 1)
        return jnp.sum(jnp.where(line == column, values, 0.0), axis=0, keepdims=True)

    gain_row = jnp.concatenate([small[8 + j : 9 + j, :] for j in range(width // 128)], axis=1)
    gain_ffn_out[...] = as_row(own_column(gain_row))[:, 0:piece]
    bias_piece = head_size // n
    line = lax.broadcasted_iota(jnp.int32, (bias_piece, head_size), 0)
    column = lax.broadcasted_iota(jnp.int32, (bias_piece, head_size), 1)
    for target, begin in ((cbias_out, 0), (pbias_out, 2)):
        for h in range(2):
            row = small[begin + h : begin + h + 1, :]
            values = jnp.sum(
                jnp.where(column == dp * bias_piece + line, row, 0.0), axis=-1, keepdims=True
            )
            across = jnp.sum(jnp.where(column == line, values, 0.0), axis=0, keepdims=True)
            target[h : h + 1, :] = across[:, 0:bias_piece]
    tick(REL)
    tick(UP[3])
    unit_step(OUT, 1)
    unit_upto(QKV + 1, steps - 1)
    unit_upto(UP[3], 1)
    unit_upto(QKV + 2, steps - 1)

    own = pl.ds(pl.multiple_of(dp * piece, piece), piece)
    gathered = jnp.zeros((piece, 1), F32)
    for t in range(3):
        at, start, length = region(QKV + t, steps - 1, True)
        product = grads[at, pl.ds(start, length), :] * wqkv[
            own, 256 * t : 256 * (t + 1)
        ].astype(F32)
        gathered = gathered + jnp.sum(product, axis=-1, keepdims=True)
    tiny[0:1, :] = as_row(gathered / own_column(gain_attn[...]))

    def tiny_start(s, peer):
        return remote(tiny, tiny_in.at[s], tiny_send.at[s], tiny_recv.at[s], peer)

    tiny_move = tiny_start(0, core_peer)
    unit_upto(OUT, steps - 1)
    tiny_move.wait()
    tiny[...] = tiny[...] + tiny_in[0]
    tiny_move = tiny_start(1, x_peer)
    unit_upto(UP[3], steps - 1)
    unit_upto(REL, steps - 1)
    tiny_move.wait()
    gain_attn_out[...] = (tiny[...] + tiny_in[1])[0:1, 0:piece]

    assert not sends
    for copy in outs.values():
        copy.wait()
    out_copy.wait()
    grad_copy.wait()


def hand_on(count, *refs):
    sources, targets, rooms = refs[:count], refs[count : 2 * count], refs[2 * count : 3 * count]
    sem_in, sem_out = refs[3 * count :]
    arrivals, departures = [], []
    for i in range(count):
        parts = 4 if sources[i].shape[0] % 64 == 0 else 1
        size = sources[i].shape[0] // parts
        for k in range(parts):
            here = pl.ds(k * size, size)
            copy = pltpu.make_async_copy(sources[i].at[here], rooms[i].at[here], sem_in.at[i, k])
            copy.start()
            arrivals.append((copy, i, k, here))
    for copy, i, k, here in arrivals:
        copy.wait()
        copy = pltpu.make_async_copy(rooms[i].at[here], targets[i].at[here], sem_out.at[i, k])
        copy.start()
        departures.append(copy)
    for copy in departures:
        copy.wait()


def shards(
    n,
    segment,
    memory,
    compressed,
    mem_fill,
    comp_fill,
    gain_attn,
    w_qkv,
    content_bias,
    position_bias,
    w_rel,
    w_out,
    gain_ffn,
    w_up,
    w_down,
    w_comp,
    out_cotangent,
    comp_cotangent,
):
    rows, width = segment.shape[1:]
    keys = 3 * rows
    steps = n.bit_length() - 1
    piece = width // n
    head_size = content_bias.shape[0]
    new_count = comp_cotangent.shape[1]
    pad_count = -(-new_count // 16) * 16
    features, sine, cosine = tables(width, 2 * rows, keys)
    vm, anyw = pl.BlockSpec(memory_space=pltpu.VMEM), pl.BlockSpec(memory_space=pl.ANY)
    smem = pl.BlockSpec(memory_space=pltpu.SMEM)
    dma = pltpu.SemaphoreType.DMA
    plain = pltpu.SemaphoreType.REGULAR
    later_count = (LATER_SLOTS + 2) * max(steps - 1, 1)
    scratch = [
        pltpu.VMEM((rows, width), BF),
        pltpu.VMEM((rows, width), BF),
        pltpu.VMEM((rows, width), BF),
        pltpu.VMEM((rows, width), BF),
        pltpu.VMEM(w_qkv.shape, BF),
        pltpu.VMEM(w_rel.shape, BF),
        pltpu.VMEM(w_out.shape, BF),
        pltpu.VMEM(w_up.shape, BF),
        pltpu.VMEM(w_down.shape, BF),
        pltpu.VMEM((keys, width + 2 * head_size), BF),
        pltpu.VMEM((rows, width // 2), F32),
        pltpu.VMEM((rows, width // 2), F32),
        pltpu.VMEM((keys, 2 * head_size), BF),
        pltpu.VMEM((2, rows, width + head_size), BF),
        pltpu.VMEM((rows, 2 * head_size), BF),
        pltpu.VMEM((keys, width), BF),
        pltpu.VMEM((2, rows, keys), BF),
        pltpu.VMEM((rows, 2 * head_size), BF),
        pltpu.VMEM((rows, 2), F32),
        pltpu.VMEM((rows, 2 * head_size), BF),
        pltpu.VMEM((rows, 6 * head_size), BF),
        pltpu.VMEM((rows, width), F32),
        pltpu.VMEM((rows, width), F32),
        pltpu.VMEM((pad_count, 256), BF),
        pltpu.VMEM((8, 2 * rows), F32),
        pltpu.VMEM((26, 512, 256), F32),
        pltpu.VMEM((4, rows, 256), F32),
        pltpu.VMEM((4, rows, 256), F32),
        pltpu.VMEM((2, rows, 256), F32),
        pltpu.VMEM((2, 2, rows, 256), F32),
        pltpu.VMEM((4, rows, 256), F32),
        pltpu.VMEM((16, 128), F32),
        pltpu.VMEM((steps, 16, 128), F32),
        pltpu.VMEM((8, 128), F32),
        pltpu.VMEM((2, 8, 128), F32),
        pltpu.VMEM((FIRST_SLOTS + 2, 512, 256), F32),
        pltpu.VMEM((LATER_SLOTS + 2, 512 - (512 >> (steps - 1)), 256), F32),
        dma((16,)),
        dma((18,)),
        dma((FIRST_SLOTS + 2,)),
        dma((FIRST_SLOTS + 2,)),
        plain((FIRST_SLOTS + 2,)),
        dma((later_count,)),
        dma((later_count,)),
        plain((later_count,)),
        dma((4,)),
        dma((4,)),
        plain,
        dma((2, 4)),
        dma((2, 4)),
        plain((2,)),
        dma((4,)),
        dma((4,)),
        plain,
        dma((steps,)),
        dma((steps,)),
        dma((2,)),
        dma((2,)),
    ]
    shape = jax.ShapeDtypeStruct
    results = pl.pallas_call(
        functools.partial(kernel, n),
        out_shape=(
            shape((rows, width), BF),
            shape((new_count, 256), BF),
            shape((rows, width), F32),
            shape((1, piece), F32),
            shape((piece, w_qkv.shape[1]), F32),
            shape((2, head_size // n), F32),
            shape((2, head_size // n), F32),
            shape((piece, w_rel.shape[1]), F32),
            shape((piece, w_out.shape[1]), F32),
            shape((1, piece), F32),
            shape((piece, w_up.shape[1]), F32),
            shape((piece, w_down.shape[1]), F32),
            shape((3 * piece, w_comp.shape[1]), F32),
        ),
        in_specs=[smem] * 2 + [vm] * 5 + [anyw] * 13,
        out_specs=(anyw, vm, anyw, vm, anyw, vm, vm, anyw, anyw, vm, anyw, anyw, anyw),
        scratch_shapes=scratch,
        compiler_params=pltpu.CompilerParams(
            collective_id=0, has_side_effects=True, vmem_limit_bytes=127 * 2**19
        ),
    )(
        mem_fill,
        comp_fill,
        gain_attn.reshape(1, width),
        gain_ffn.reshape(1, width),
        content_bias.T,
        position_bias.T,
        comp_cotangent[0],
        segment[0],
        memory[0],
        compressed[0],
        w_qkv,
        w_rel,
        w_out,
        w_up,
        w_down,
        w_comp,
        out_cotangent[0],
        jnp.asarray(features, BF),
        jnp.asarray(sine),
        jnp.asarray(cosine),
    )
    count = len(results)
    results = pl.pallas_call(
        functools.partial(hand_on, count),
        out_shape=tuple(shape(r.shape, r.dtype) for r in results),
        in_specs=[anyw] * count,
        out_specs=(anyw,) * count,
        scratch_shapes=[pltpu.VMEM(r.shape, r.dtype) for r in results] + [dma((count, 4))] * 2,
        compiler_params=pltpu.CompilerParams(vmem_limit_bytes=63 * 2**20),
    )(*results)
    layer, new, grad, gattn, qkv, cbias, pbias, rel, outp, gffn, up, down, comp = results
    return (
        layer[None],
        new[None],
        grad[None],
        gattn.reshape(piece),
        qkv,
        cbias.T,
        pbias.T,
        rel,
        outp,
        gffn.reshape(piece),
        up,
        down,
        comp,
    )


def solution(mesh):
    stream = P("dp", None, None)
    split = P(None, "head")
    return jax.shard_map(
        functools.partial(shards, mesh.shape["dp"]),
        mesh=mesh,
        in_specs=(
            stream,
            stream,
            stream,
            P("dp"),
            P("dp"),
            P(),
            split,
            split,
            split,
            split,
            split,
            P(),
            split,
            split,
            split,
            stream,
            P("dp", None, "head"),
        ),
        out_specs=(
            stream,
            P("dp", None, "head"),
            stream,
            P("dp"),
            P("dp", "head"),
            P("dp", "head"),
            P("dp", "head"),
            P("dp", "head"),
            P("dp", "head"),
            P("dp"),
            P("dp", "head"),
            P("dp", "head"),
            P("dp", "head"),
        ),
        check_vma=False,
    )
```
